32 devices in a mesh: head: 4 (over y, core), inner: 4 (over z), outer: 2 (over x).
Axes of the slice: x: 2, y: 2, z: 4, core: 2. Of those that a mesh axis runs over, the one named last changes fastest.
Arguments:
- activations: bfloat16 [1024, 8192], P(('inner', 'outer')), may hold values from -6 to 6
- key_matrix: bfloat16 [8192, 512], P('inner'), may hold values from -0.0625 to 0.0625
- value_matrix: bfloat16 [8192, 512], P('inner'), may hold values from -0.0625 to 0.0625
- queries: bfloat16 [1024, 4096], P(('inner', 'outer'), 'head'), may hold values from -160 to 160
- block_order: int32 [16], replicated, may hold values from 0 to 15, each once
Outputs:
- attended: bfloat16 [8, 4, 32, 4096], P(('inner', 'outer'), 'head')
The draws below stay inside these ranges and needn't reach their ends.
Inputs may be any that keep to these rules, and one draw needn't show every extreme that they name: `block_order`: every block number appears once.
All inputs are finite; a program needn't handle non-finite values.
Results may differ from the reference program's by a relative error of at most 0.011.
Values may be sent and summed in bfloat16 or wider, within the bound.
No kernel may reach another device: no remote copies, remote signals or barrier semaphores. Data moves between devices by JAX's collectives and lax.ppermute only.
A program may use at most 64 MiB of HBM per device.

```python
import math
import jax
import jax.numpy as jnp
from jax import lax

MODEL_WIDTH = 8192
QUERY_HEADS = 32
KEY_VALUE_HEADS = 4
HEAD_WIDTH = 128
TOK = 128
SEQ = 1024
CYCLE = 8
NBLK = 16
SUB = 32
N_HEAD = 4


def draw_queries(key, part):
    first_key = jax.random.fold_in(key, 0)
    return jnp.clip(2.5 * jax.random.normal(first_key, (SEQ, QUERY_HEADS * HEAD_WIDTH), jnp.float32), -15.0, 15.0).astype(jnp.bfloat16)


def block_levels(key, dims, cuts, least, high):
    level, own = 1.0, jax.random.fold_in(key, 6)
    for position, shards_of in cuts:
        draws = jnp.exp(jax.random.uniform(jax.random.fold_in(own, position), (shards_of,), jnp.float32, least / len(cuts), high / len(cuts)))
        level = level * jnp.repeat(draws, dims[position] // shards_of).reshape([-1 if axis == position else 1 for axis in range(len(dims))])
    return level


def scatter_about(rng, dims, scale, bound, cuts=(), held_as=jnp.bfloat16):
    loudness = block_levels(rng, dims, cuts, -0.22, 0.18) if cuts else 1.0
    drawn = jax.random.normal(rng, dims, jnp.float32) * scale * loudness
    return jnp.minimum(jnp.maximum(drawn, -bound), bound).astype(held_as)


def setup_inputs(seed: int = 0) -> dict:
    key_of = jax.random.split(jax.random.key(seed), 6)
    activations = scatter_about(key_of[0], (SEQ, MODEL_WIDTH), 1.0, 6.0, ((0, 8),))
    key_matrix = scatter_about(key_of[1], (MODEL_WIDTH, KEY_VALUE_HEADS * HEAD_WIDTH), MODEL_WIDTH ** -0.5, 0.0625, ((0, 4),))
    value_matrix = scatter_about(key_of[2], (MODEL_WIDTH, KEY_VALUE_HEADS * HEAD_WIDTH), MODEL_WIDTH ** -0.5, 0.0625, ((0, 4),))
    queries = draw_queries(jax.random.fold_in(key_of[5], 71), 0)
    block_order = jax.random.permutation(key_of[4], NBLK).astype(jnp.int32)
    return {"activations": activations, "key_matrix": key_matrix, "value_matrix": value_matrix, "queries": queries, "block_order": block_order}


def reference(activations, key_matrix, value_matrix, queries, block_order):
    keys = jnp.dot(activations, key_matrix, preferred_element_type=jnp.float32).astype(jnp.bfloat16)
    values = jnp.dot(activations, value_matrix, preferred_element_type=jnp.float32).astype(jnp.bfloat16)
    block_size = TOK // 2
    positions = (block_order[:, None] * block_size + jnp.arange(block_size, dtype=jnp.int32)[None, :]).reshape(SEQ)
    allowed = positions[None, :] <= positions[:, None]
    heads_per_group = QUERY_HEADS // KEY_VALUE_HEADS
    score_scale = 1.0 / math.sqrt(HEAD_WIDTH)

    def one_head(head):
        query_rows = lax.dynamic_slice_in_dim(queries, (head * HEAD_WIDTH).astype(jnp.int32), HEAD_WIDTH, 1)
        kv_head = (head // heads_per_group).astype(jnp.int32)
        key_rows = lax.dynamic_slice_in_dim(keys, kv_head * HEAD_WIDTH, HEAD_WIDTH, 1)
        value_rows = lax.dynamic_slice_in_dim(values, kv_head * HEAD_WIDTH, HEAD_WIDTH, 1)
        scores = jnp.dot(query_rows, key_rows.T, preferred_element_type=jnp.float32) * score_scale
        row_max = lax.optimization_barrier(jnp.max(jnp.where(allowed, scores, -1e+30), axis=1, keepdims=True))
        unnormed = jnp.where(allowed, jnp.exp(scores - row_max), 0.0)
        totals = lax.optimization_barrier(jnp.sum(unnormed, axis=1))
        mixed = jnp.dot(unnormed.astype(jnp.bfloat16), value_rows, preferred_element_type=jnp.float32)
        return mixed / totals[:, None]
    heads_out = lax.map(one_head, jnp.arange(QUERY_HEADS, dtype=jnp.int32))
    attended = jnp.transpose(heads_out, (1, 0, 2)).reshape(SEQ, QUERY_HEADS * HEAD_WIDTH).astype(jnp.bfloat16)
    return attended.reshape(CYCLE, N_HEAD, SUB, QUERY_HEADS * HEAD_WIDTH)
```

```python
import functools
import math

import jax
import jax.numpy as jnp
from jax import lax
from jax.experimental import pallas as pl
from jax.experimental.pallas import tpu as pltpu
from jax.sharding import PartitionSpec as P

QUERY_HEADS = 32
KEY_VALUE_HEADS = 4
HEAD_WIDTH = 128
VMEM = pl.BlockSpec(memory_space=pltpu.VMEM)
SMEM = pl.BlockSpec(memory_space=pltpu.SMEM)
LIMIT = 40 * 1024 * 1024


def swap(piece, axis, offset):
    return lax.ppermute(piece, axis, [(i, i ^ offset) for i in range(lax.axis_size(axis))])


def swap_all(pieces, axis):
    got = {k: swap(pieces[k], axis, k) for k in reversed(range(1, len(pieces)))}
    return [pieces[0]] + [got[k] for k in range(1, len(pieces))]


def project_kernel(count, *refs):
    pieces, (key_matrix, value_matrix), outs = refs[:count], refs[count : count + 2], refs[count + 2 :]
    rows = pieces[0][...] if count == 1 else jnp.concatenate([piece[...] for piece in pieces], axis=0)
    width = key_matrix.shape[1]
    each = outs[0].shape[0]
    for half, matrix in enumerate((key_matrix, value_matrix)):
        product = jnp.dot(rows, matrix[...], preferred_element_type=jnp.float32)
        for k, out in enumerate(outs):
            out[:, half * width : (half + 1) * width] = product[k * each : (k + 1) * each]


def project(pieces, key_matrix, value_matrix):
    rows, width = pieces[0].shape[0], 2 * key_matrix.shape[1]
    given = pieces if rows % 16 == 0 else [jnp.concatenate(pieces, axis=0)]
    return pl.pallas_call(
        functools.partial(project_kernel, len(given)),
        out_shape=[jax.ShapeDtypeStruct((rows, width), jnp.float32)] * len(pieces),
        in_specs=[VMEM] * (len(given) + 2),
        out_specs=[VMEM] * len(pieces),
        compiler_params=pltpu.CompilerParams(vmem_limit_bytes=LIMIT),
        name="project",
    )(*given, key_matrix, value_matrix)


def total_kernel(count, heads_of, *refs):
    parts, outs = refs[:count], refs[count:]
    for k, out in enumerate(outs):
        for half in range(2):
            first = pl.multiple_of((half * KEY_VALUE_HEADS + heads_of[k]) * HEAD_WIDTH, HEAD_WIDTH)
            columns = pl.ds(first, HEAD_WIDTH)
            whole = parts[0][:, columns]
            for part in parts[1:]:
                whole = whole + part[:, columns]
            out[:, half * HEAD_WIDTH : (half + 1) * HEAD_WIDTH] = whole.astype(out.dtype)


def total(parts, heads_of, receivers):
    rows = parts[0].shape[0]

    def body(heads_ref, *refs):
        total_kernel(len(parts), heads_ref, *refs)

    return pl.pallas_call(
        body,
        out_shape=[jax.ShapeDtypeStruct((rows, 2 * HEAD_WIDTH), jnp.bfloat16)] * receivers,
        in_specs=[SMEM] + [VMEM] * len(parts),
        out_specs=[VMEM] * receivers,
        compiler_params=pltpu.CompilerParams(vmem_limit_bytes=LIMIT),
        name="total",
    )(heads_of, *parts)


def attend_kernel(count, head_index, queries, query_pos, key_pos, *refs):
    blocks, outs, (keys, values) = refs[:count], refs[count:-2], refs[-2:]
    tokens = blocks[0].shape[0]
    for b, block in enumerate(blocks):
        keys[b * tokens : (b + 1) * tokens, :] = block[:, :HEAD_WIDTH]
        values[b * tokens : (b + 1) * tokens, :] = block[:, HEAD_WIDTH:]
    sub = outs[0].shape[0]
    per_device = queries.shape[1] // HEAD_WIDTH
    length = keys.shape[0]
    factor = math.log2(math.e) / math.sqrt(HEAD_WIDTH)
    for k, out in enumerate(outs):
        first = pl.multiple_of((head_index[0] ^ k) * sub, sub)
        rows = queries[pl.ds(first, sub), :]
        stacked = jnp.concatenate([rows[:, i * HEAD_WIDTH : (i + 1) * HEAD_WIDTH] for i in range(per_device)], axis=0)
        scores = lax.dot_general(stacked, keys[...], (((1,), (1,)), ((), ())), preferred_element_type=jnp.float32)
        allowed = key_pos[...] <= query_pos[pl.ds(first, sub), :]
        scores = jnp.where(allowed[None], scores.reshape(per_device, sub, length), -1e30)
        largest = jnp.max(scores, axis=2, keepdims=True)
        unnormed = jnp.exp2((scores - largest) * factor)
        totals = jnp.sum(unnormed, axis=2, keepdims=True)
        weights = unnormed.astype(jnp.bfloat16).reshape(per_device * sub, length)
        mixed = jnp.dot(weights, values[...], preferred_element_type=jnp.float32)
        mixed = mixed.reshape(per_device, sub, HEAD_WIDTH) / totals
        for i in range(per_device):
            out[:, i * HEAD_WIDTH : (i + 1) * HEAD_WIDTH] = mixed[i].astype(out.dtype)


def attend(head_index, queries, query_pos, key_pos, blocks, receivers):
    tokens, width = queries.shape
    length = tokens * len(blocks)
    return pl.pallas_call(
        functools.partial(attend_kernel, len(blocks)),
        out_shape=[jax.ShapeDtypeStruct((tokens // receivers, width), jnp.bfloat16)] * receivers,
        in_specs=[SMEM] + [VMEM] * (3 + len(blocks)),
        out_specs=[VMEM] * receivers,
        scratch_shapes=[pltpu.VMEM((length, HEAD_WIDTH), jnp.bfloat16)] * 2,
        compiler_params=pltpu.CompilerParams(vmem_limit_bytes=LIMIT),
        name="attend",
    )(head_index, queries, query_pos, key_pos, *blocks)


def join_kernel(count, head_index, *refs):
    pieces, out = refs[:count], refs[count]
    width = pieces[0].shape[1]
    for k, piece in enumerate(pieces):
        out[0, 0, :, pl.ds(pl.multiple_of((head_index[0] ^ k) * width, width), width)] = piece[...]


def join(head_index, pieces):
    rows, width = pieces[0].shape
    return pl.pallas_call(
        functools.partial(join_kernel, len(pieces)),
        out_shape=jax.ShapeDtypeStruct((1, 1, rows, width * len(pieces)), jnp.bfloat16),
        in_specs=[SMEM] + [VMEM] * len(pieces),
        out_specs=VMEM,
        name="join",
    )(head_index, *pieces)


def body(activations, key_matrix, value_matrix, queries, block_order):
    heads, inner, outer = (lax.axis_size(name) for name in ("head", "inner", "outer"))
    head, z, x = (lax.axis_index(name) for name in ("head", "inner", "outer"))
    tokens = activations.shape[0]
    sub = tokens // heads
    depth = key_matrix.shape[0]
    sharing = heads // KEY_VALUE_HEADS
    head_index = jnp.reshape(head, (1,))

    pieces = [
        lax.dynamic_slice(activations, (head * sub, (z ^ k) * depth), (sub, depth)) for k in range(inner)
    ]
    partial = project(swap_all(pieces, "inner"), key_matrix, value_matrix)
    heads_of = (head ^ jnp.arange(heads, dtype=jnp.int32)) // sharing
    parts = swap_all(partial, "inner")
    shares = total(parts, heads_of, heads)
    own = jnp.concatenate(swap_all(shares, "head"), axis=0)

    nearby = swap_all([own] * inner, "inner")
    blocks, cycle = [], []
    for j in range(outer):
        for k in range(inner):
            blocks.append(nearby[k] if j == 0 else swap(nearby[k], "outer", j))
            cycle.append((z ^ k) * outer + (x ^ j))

    block_size = tokens // 2
    row = jnp.arange(tokens, dtype=jnp.int32)
    order = block_order.reshape(-1, 2)

    def positions(shard):
        return (lax.dynamic_index_in_dim(order, shard, 0, False)[:, None] * block_size + row[None, :block_size]).reshape(
            tokens
        )

    query_pos = positions(z * outer + x)
    shards = jnp.stack(cycle)
    rows_of = ((head ^ jnp.arange(heads, dtype=jnp.int32))[:, None] * sub + row[None, :sub]).reshape(tokens)
    one_hot = shards[:, None] == jnp.arange(order.shape[0], dtype=jnp.int32)[None, :]
    firsts = jnp.sum(jnp.where(one_hot[:, :, None], order[None], 0), axis=1)
    block_of = jnp.where(rows_of[None, :] < block_size, firsts[:, :1], firsts[:, 1:])
    key_pos = (block_of * block_size + rows_of[None, :] % block_size).reshape(1, -1)

    attended = attend(head_index, queries, query_pos[:, None], key_pos, blocks, heads)
    return join(head_index, swap_all(attended, "head"))


def solution(mesh):
    placed = (
        P(("inner", "outer"), None),
        P("inner", None),
        P("inner", None),
        P(("inner", "outer"), "head"),
        P(),
    )
    return jax.shard_map(
        body,
        mesh=mesh,
        in_specs=placed,
        out_specs=P(("inner", "outer"), "head", None, None),
        check_vma=False,
    )
```

```python
import functools
import math

import jax
import jax.numpy as jnp
from jax import lax
from jax.experimental import pallas as pl
from jax.experimental.pallas import tpu as pltpu
from jax.sharding import PartitionSpec as P

QUERY_HEADS = 32
KEY_VALUE_HEADS = 4
HEAD_WIDTH = 128
VMEM = pl.BlockSpec(memory_space=pltpu.VMEM)
SMEM = pl.BlockSpec(memory_space=pltpu.SMEM)
HBM = pl.BlockSpec(memory_space=pltpu.HBM)
LIMIT = 16 * 1024 * 1024


def params():
    return pltpu.CompilerParams(vmem_limit_bytes=LIMIT)


def swap(piece, axis, offset):
    return lax.ppermute(piece, axis, [(i, i ^ offset) for i in range(lax.axis_size(axis))])


def swap_all(pieces, axis):
    got = {k: swap(pieces[k], axis, k) for k in reversed(range(1, len(pieces)))}
    return [pieces[0]] + [got[k] for k in range(1, len(pieces))]


def copies(pairs, sems):
    started = [pltpu.make_async_copy(source, target, sems.at[i]) for i, (source, target) in enumerate(pairs)]
    for copy in started:
        copy.start()
    for copy in started:
        copy.wait()


def load_kernel(*refs):
    half = len(refs) // 2
    copies(list(zip(refs[:half], refs[half : 2 * half])), refs[-1])


def load(*arrays):
    return pl.pallas_call(
        load_kernel,
        out_shape=[jax.ShapeDtypeStruct(a.shape, a.dtype) for a in arrays],
        in_specs=[HBM] * len(arrays),
        out_specs=[VMEM] * len(arrays),
        scratch_shapes=[pltpu.SemaphoreType.DMA((len(arrays),))],
        compiler_params=params(),
        cost_estimate=pl.CostEstimate(flops=0, bytes_accessed=2 * sum(a.size * 2 for a in arrays), transcendentals=0),
        name="load",
    )(*arrays)


def project_kernel(count, *refs):
    pieces, (key_matrix, value_matrix), outs = refs[:count], refs[count : count + 2], refs[count + 2 :]
    rows = pieces[0][...] if count == 1 else jnp.concatenate([piece[...] for piece in pieces], axis=0)
    width = key_matrix.shape[1]
    each = outs[0].shape[0]
    for half, matrix in enumerate((key_matrix, value_matrix)):
        product = jnp.dot(rows, matrix[...], preferred_element_type=jnp.float32)
        for k, out in enumerate(outs):
            out[:, half * width : (half + 1) * width] = product[k * each : (k + 1) * each]


def project(pieces, key_matrix, value_matrix):
    rows, width = pieces[0].shape[0], 2 * key_matrix.shape[1]
    given = pieces if rows % 16 == 0 else [jnp.concatenate(pieces, axis=0)]
    return pl.pallas_call(
        functools.partial(project_kernel, len(given)),
        out_shape=[jax.ShapeDtypeStruct((rows, width), jnp.float32)] * len(pieces),
        in_specs=[VMEM] * (len(given) + 2),
        out_specs=[VMEM] * len(pieces),
        compiler_params=params(),
        name="project",
    )(*given, key_matrix, value_matrix)


def total_kernel(count, heads_of, *refs):
    parts, outs = refs[:count], refs[count:]
    for k, out in enumerate(outs):
        for half in range(2):
            first = pl.multiple_of((half * KEY_VALUE_HEADS + heads_of[k]) * HEAD_WIDTH, HEAD_WIDTH)
            columns = pl.ds(first, HEAD_WIDTH)
            whole = parts[0][:, columns]
            for part in parts[1:]:
                whole = whole + part[:, columns]
            out[:, half * HEAD_WIDTH : (half + 1) * HEAD_WIDTH] = whole.astype(out.dtype)


def total(parts, heads_of, receivers):
    rows = parts[0].shape[0]

    def body(heads_ref, *refs):
        total_kernel(len(parts), heads_ref, *refs)

    return pl.pallas_call(
        body,
        out_shape=[jax.ShapeDtypeStruct((rows, 2 * HEAD_WIDTH), jnp.bfloat16)] * receivers,
        in_specs=[SMEM] + [VMEM] * len(parts),
        out_specs=[VMEM] * receivers,
        compiler_params=params(),
        name="total",
    )(heads_of, *parts)


def stack_kernel(count, *refs):
    blocks, (keys, values) = refs[:count], refs[count:]
    tokens = blocks[0].shape[0]
    for b, block in enumerate(blocks):
        keys[b * tokens : (b + 1) * tokens, :] = block[:, :HEAD_WIDTH]
        values[b * tokens : (b + 1) * tokens, :] = block[:, HEAD_WIDTH:]


def attend_kernel(count, offsets, head_index, queries, query_pos, key_pos, *refs):
    if count:
        outs, (keys, values) = refs[count:-2], refs[-2:]
        stack_kernel(count, *refs[:count], keys, values)
    else:
        (keys, values), outs = refs[:2], refs[2:]
    sub = outs[0].shape[0]
    per_device = queries.shape[1] // HEAD_WIDTH
    length = keys.shape[0]
    factor = math.log2(math.e) / math.sqrt(HEAD_WIDTH)
    for k, out in zip(offsets, outs):
        first = pl.multiple_of((head_index[0] ^ k) * sub, sub)
        rows = queries[pl.ds(first, sub), :]
        stacked = jnp.concatenate([rows[:, i * HEAD_WIDTH : (i + 1) * HEAD_WIDTH] for i in range(per_device)], axis=0)
        scores = lax.dot_general(stacked, keys[...], (((1,), (1,)), ((), ())), preferred_element_type=jnp.float32)
        allowed = key_pos[...] <= query_pos[pl.ds(first, sub), :]
        scores = jnp.where(allowed[None], scores.reshape(per_device, sub, length), -1e30)
        largest = jnp.max(scores, axis=2, keepdims=True)
        unnormed = jnp.exp2((scores - largest) * factor)
        totals = jnp.sum(unnormed, axis=2, keepdims=True)
        weights = unnormed.astype(jnp.bfloat16).reshape(per_device * sub, length)
        mixed = jnp.dot(weights, values[...], preferred_element_type=jnp.float32)
        mixed = mixed.reshape(per_device, sub, HEAD_WIDTH) / totals
        for i in range(per_device):
            out[:, i * HEAD_WIDTH : (i + 1) * HEAD_WIDTH] = mixed[i].astype(out.dtype)


def attend(offsets, receivers, head_index, queries, query_pos, key_pos, blocks, stacked=()):
    tokens, width = queries.shape
    length = key_pos.shape[1]
    count = 0 if stacked else len(blocks)
    given = stacked or blocks
    piece = jax.ShapeDtypeStruct((tokens // receivers, width), jnp.bfloat16)
    held = [] if stacked else [jax.ShapeDtypeStruct((length, HEAD_WIDTH), jnp.bfloat16)] * 2
    rows = tokens * len(offsets) // receivers
    work = rows * length * width
    return pl.pallas_call(
        functools.partial(attend_kernel, count, offsets),
        out_shape=[piece] * len(offsets) + held,
        in_specs=[SMEM] + [VMEM] * (3 + len(given)),
        out_specs=[VMEM] * (len(offsets) + len(held)),
        compiler_params=params(),
        cost_estimate=pl.CostEstimate(
            flops=16 * work, bytes_accessed=4 * length * HEAD_WIDTH, transcendentals=work // HEAD_WIDTH
        ),
        name="attend",
    )(head_index, queries, query_pos, key_pos, *given)


def join_kernel(count, head_index, *refs):
    pieces, (out, sems) = refs[:count], refs[count:]
    width = pieces[0].shape[1]
    copies(
        [
            (piece, out.at[0, 0, :, pl.ds(pl.multiple_of((head_index[0] ^ k) * width, width), width)])
            for k, piece in enumerate(pieces)
        ],
        sems,
    )


def join(head_index, pieces):
    rows, width = pieces[0].shape
    return pl.pallas_call(
        functools.partial(join_kernel, len(pieces)),
        out_shape=jax.ShapeDtypeStruct((1, 1, rows, width * len(pieces)), jnp.bfloat16),
        in_specs=[SMEM] + [VMEM] * len(pieces),
        out_specs=HBM,
        scratch_shapes=[pltpu.SemaphoreType.DMA((len(pieces),))],
        compiler_params=params(),
        name="join",
    )(head_index, *pieces)


def body(activations, key_matrix, value_matrix, queries, block_order):
    heads, inner, outer = (lax.axis_size(name) for name in ("head", "inner", "outer"))
    head, z, x = (lax.axis_index(name) for name in ("head", "inner", "outer"))
    tokens = activations.shape[0]
    sub = tokens // heads
    depth = key_matrix.shape[0]
    sharing = heads // KEY_VALUE_HEADS
    head_index = jnp.reshape(head, (1,))

    pieces = [
        lax.dynamic_slice(activations, (head * sub, (z ^ k) * depth), (sub, depth)) for k in range(inner)
    ]
    pieces[0], matrices = lax.optimization_barrier((pieces[0], (key_matrix, value_matrix)))
    partial = project(swap_all(pieces, "inner"), *load(*matrices))
    heads_of = (head ^ jnp.arange(heads, dtype=jnp.int32)) // sharing
    parts = swap_all(partial, "inner")
    shares = total(parts, heads_of, heads)
    own = jnp.concatenate(swap_all(shares, "head"), axis=0)

    nearby = swap_all([own] * inner, "inner")
    blocks, cycle = [], []
    for j in range(outer):
        for k in range(inner):
            blocks.append(nearby[k] if j == 0 else swap(nearby[k], "outer", j))
            cycle.append((z ^ k) * outer + (x ^ j))

    block_size = tokens // 2
    row = jnp.arange(tokens, dtype=jnp.int32)
    order = block_order.reshape(-1, 2)

    def positions(shard):
        return (lax.dynamic_index_in_dim(order, shard, 0, False)[:, None] * block_size + row[None, :block_size]).reshape(
            tokens
        )

    query_pos = positions(z * outer + x)
    shards = jnp.stack(cycle)
    rows_of = ((head ^ jnp.arange(heads, dtype=jnp.int32))[:, None] * sub + row[None, :sub]).reshape(tokens)
    one_hot = shards[:, None] == jnp.arange(order.shape[0], dtype=jnp.int32)[None, :]
    firsts = jnp.sum(jnp.where(one_hot[:, :, None], order[None], 0), axis=1)
    block_of = jnp.where(rows_of[None, :] < block_size, firsts[:, :1], firsts[:, 1:])
    key_pos = (block_of * block_size + rows_of[None, :] % block_size).reshape(1, -1)

    place = head_index, queries, query_pos[:, None], key_pos, blocks
    *leaving, keys, values = attend(range(1, heads), heads, *place)
    own_rows = attend(range(1), heads, *place, stacked=(keys, values))
    return join(head_index, swap_all([*own_rows, *leaving], "head"))


def solution(mesh):
    placed = (
        P(("inner", "outer"), None),
        P("inner", None),
        P("inner", None),
        P(("inner", "outer"), "head"),
        P(),
    )
    return jax.shard_map(
        body,
        mesh=mesh,
        in_specs=placed,
        out_specs=P(("inner", "outer"), "head", None, None),
        check_vma=False,
    )
```

```python
import functools
import math

import jax
import jax.numpy as jnp
from jax import lax
from jax.experimental import pallas as pl
from jax.experimental.pallas import tpu as pltpu
from jax.sharding import PartitionSpec as P

QUERY_HEADS = 32
KEY_VALUE_HEADS = 4
HEAD_WIDTH = 128
VMEM = pl.BlockSpec(memory_space=pltpu.VMEM)
SMEM = pl.BlockSpec(memory_space=pltpu.SMEM)
HBM = pl.BlockSpec(memory_space=pltpu.HBM)
LIMIT = 16 * 1024 * 1024


def params():
    return pltpu.CompilerParams(vmem_limit_bytes=LIMIT)


def swap(piece, axis, offset):
    return lax.ppermute(piece, axis, [(i, i ^ offset) for i in range(lax.axis_size(axis))])


def swap_both(piece, along, offset, across, other):
    first, second = lax.axis_size(along), lax.axis_size(across)
    order = [(i * second + j, (i ^ offset) * second + (j ^ other)) for i in range(first) for j in range(second)]
    return lax.ppermute(piece, (along, across), order)


def swap_all(pieces, axis):
    got = {k: swap(pieces[k], axis, k) for k in reversed(range(1, len(pieces)))}
    return [pieces[0]] + [got[k] for k in range(1, len(pieces))]


def copies(pairs, sems):
    started = [pltpu.make_async_copy(source, target, sems.at[i]) for i, (source, target) in enumerate(pairs)]
    for copy in started:
        copy.start()
    for copy in started:
        copy.wait()


def load_kernel(*refs):
    half = len(refs) // 2
    copies(list(zip(refs[:half], refs[half : 2 * half])), refs[-1])


def load(*arrays):
    return pl.pallas_call(
        load_kernel,
        out_shape=[jax.ShapeDtypeStruct(a.shape, a.dtype) for a in arrays],
        in_specs=[HBM] * len(arrays),
        out_specs=[VMEM] * len(arrays),
        scratch_shapes=[pltpu.SemaphoreType.DMA((len(arrays),))],
        compiler_params=params(),
        cost_estimate=pl.CostEstimate(flops=0, bytes_accessed=2 * sum(a.size * 2 for a in arrays), transcendentals=0),
        name="load",
    )(*arrays)


def project_kernel(count, pair_heads, *refs):
    pieces, (key_matrix, value_matrix) = refs[:count], refs[count : count + 2]
    outs, (keys, values) = refs[count + 2 : -2], refs[-2:]
    rows = pieces[0][...] if count == 1 else jnp.concatenate([piece[...] for piece in pieces], axis=0)
    keys[...] = jnp.dot(rows, key_matrix[...], preferred_element_type=jnp.float32)
    values[...] = jnp.dot(rows, value_matrix[...], preferred_element_type=jnp.float32)
    pairs = pair_heads.shape[0] // 2
    sub = outs[0].shape[0]
    for i, out in enumerate(outs):
        k, f = i // pairs, i % pairs
        for member in range(2):
            columns = pl.ds(pl.multiple_of(pair_heads[2 * f + member] * HEAD_WIDTH, HEAD_WIDTH), HEAD_WIDTH)
            for half, product in enumerate((keys, values)):
                first = (2 * member + half) * HEAD_WIDTH
                out[:, first : first + HEAD_WIDTH] = product[k * sub : (k + 1) * sub, columns]


def project(pair_heads, pieces, key_matrix, value_matrix):
    sub, pairs = pieces[0].shape[0], pair_heads.shape[0] // 2
    given = pieces if sub % 16 == 0 else [jnp.concatenate(pieces, axis=0)]
    rows, width = len(pieces) * sub, key_matrix.shape[1]
    outs = pl.pallas_call(
        functools.partial(project_kernel, len(given)),
        out_shape=[jax.ShapeDtypeStruct((sub, 4 * HEAD_WIDTH), jnp.float32)] * (len(pieces) * pairs),
        in_specs=[SMEM] + [VMEM] * (len(given) + 2),
        out_specs=[VMEM] * (len(pieces) * pairs),
        scratch_shapes=[pltpu.VMEM((rows, width), jnp.float32)] * 2,
        compiler_params=params(),
        cost_estimate=pl.CostEstimate(
            flops=4 * rows * key_matrix.size, bytes_accessed=4 * key_matrix.size, transcendentals=0
        ),
        name="project",
    )(pair_heads, *given, key_matrix, value_matrix)
    return [outs[k * pairs : (k + 1) * pairs] for k in range(len(pieces))]


def total_kernel(count, member, *refs):
    parts, outs = refs[:-2], refs[-2:]
    width = 2 * HEAD_WIDTH
    for i, out in enumerate(outs):
        columns = pl.ds(pl.multiple_of((member[0] ^ i) * width, width), width)
        sums = []
        for f in range(len(parts) // count):
            whole = parts[f * count][:, columns]
            for part in parts[f * count + 1 : (f + 1) * count]:
                whole = whole + part[:, columns]
            sums.append(whole)
        out[...] = jnp.concatenate(sums, axis=0).astype(out.dtype)


def total(member, parts):
    count = len(parts[0])
    rows = parts[0][0].shape[0] * len(parts)
    given = [part for row in parts for part in row]
    return pl.pallas_call(
        functools.partial(total_kernel, count),
        out_shape=[jax.ShapeDtypeStruct((rows, 2 * HEAD_WIDTH), jnp.bfloat16)] * 2,
        in_specs=[SMEM] + [VMEM] * len(given),
        out_specs=[VMEM] * 2,
        compiler_params=params(),
        name="total",
    )(member, *given)


def stack_kernel(count, *refs):
    blocks, (keys, values) = refs[:count], refs[count:]
    tokens = blocks[0].shape[0]
    for b, block in enumerate(blocks):
        keys[b * tokens : (b + 1) * tokens, :] = block[:, :HEAD_WIDTH]
        values[b * tokens : (b + 1) * tokens, :] = block[:, HEAD_WIDTH:]


def attend_kernel(count, offsets, head_index, queries, query_pos, key_pos, *refs):
    if count:
        outs, (keys, values) = refs[count:-2], refs[-2:]
        stack_kernel(count, *refs[:count], keys, values)
    else:
        (keys, values), outs = refs[:2], refs[2:]
    sub = outs[0].shape[0]
    per_device = queries.shape[1] // HEAD_WIDTH
    length = keys.shape[0]
    factor = math.log2(math.e) / math.sqrt(HEAD_WIDTH)
    for k, out in zip(offsets, outs):
        first = pl.multiple_of((head_index[0] ^ k) * sub, sub)
        rows = queries[pl.ds(first, sub), :]
        stacked = jnp.concatenate([rows[:, i * HEAD_WIDTH : (i + 1) * HEAD_WIDTH] for i in range(per_device)], axis=0)
        scores = lax.dot_general(stacked, keys[...], (((1,), (1,)), ((), ())), preferred_element_type=jnp.float32)
        allowed = key_pos[...] <= query_pos[pl.ds(first, sub), :]
        scores = jnp.where(allowed[None], scores.reshape(per_device, sub, length), -1e30)
        largest = jnp.max(scores, axis=2, keepdims=True)
        unnormed = jnp.exp2((scores - largest) * factor)
        totals = jnp.sum(unnormed, axis=2, keepdims=True)
        weights = unnormed.astype(jnp.bfloat16).reshape(per_device * sub, length)
        mixed = jnp.dot(weights, values[...], preferred_element_type=jnp.float32)
        mixed = mixed.reshape(per_device, sub, HEAD_WIDTH) / totals
        for i in range(per_device):
            out[:, i * HEAD_WIDTH : (i + 1) * HEAD_WIDTH] = mixed[i].astype(out.dtype)


def attend(offsets, receivers, head_index, queries, query_pos, key_pos, blocks, stacked=()):
    tokens, width = queries.shape
    length = key_pos.shape[1]
    count = 0 if stacked else len(blocks)
    given = stacked or blocks
    piece = jax.ShapeDtypeStruct((tokens // receivers, width), jnp.bfloat16)
    held = [] if stacked else [jax.ShapeDtypeStruct((length, HEAD_WIDTH), jnp.bfloat16)] * 2
    rows = tokens * len(offsets) // receivers
    work = rows * length * width
    return pl.pallas_call(
        functools.partial(attend_kernel, count, offsets),
        out_shape=[piece] * len(offsets) + held,
        in_specs=[SMEM] + [VMEM] * (3 + len(given)),
        out_specs=[VMEM] * (len(offsets) + len(held)),
        compiler_params=params(),
        cost_estimate=pl.CostEstimate(
            flops=16 * work, bytes_accessed=4 * length * HEAD_WIDTH, transcendentals=work // HEAD_WIDTH
        ),
        name="attend",
    )(head_index, queries, query_pos, key_pos, *given)


def join_kernel(count, head_index, *refs):
    pieces, (out, sems) = refs[:count], refs[count:]
    width = pieces[0].shape[1]
    copies(
        [
            (piece, out.at[0, 0, :, pl.ds(pl.multiple_of((head_index[0] ^ k) * width, width), width)])
            for k, piece in enumerate(pieces)
        ],
        sems,
    )


def join(head_index, pieces):
    rows, width = pieces[0].shape
    return pl.pallas_call(
        functools.partial(join_kernel, len(pieces)),
        out_shape=jax.ShapeDtypeStruct((1, 1, rows, width * len(pieces)), jnp.bfloat16),
        in_specs=[SMEM] + [VMEM] * len(pieces),
        out_specs=HBM,
        scratch_shapes=[pltpu.SemaphoreType.DMA((len(pieces),))],
        compiler_params=params(),
        name="join",
    )(head_index, *pieces)


def body(activations, key_matrix, value_matrix, queries, block_order):
    heads, inner, outer = (lax.axis_size(name) for name in ("head", "inner", "outer"))
    head, z, x = (lax.axis_index(name) for name in ("head", "inner", "outer"))
    tokens = activations.shape[0]
    sub = tokens // heads
    depth = key_matrix.shape[0]
    sharing = heads // KEY_VALUE_HEADS
    head_index = jnp.reshape(head, (1,))

    pieces = [
        lax.dynamic_slice(activations, (head * sub, (z ^ k) * depth), (sub, depth)) for k in range(inner)
    ]
    pieces[0], matrices = lax.optimization_barrier((pieces[0], (key_matrix, value_matrix)))
    matrices = load(*matrices)
    arrived = swap_all(pieces, "inner")
    member = head % 2
    pair_heads = (head - member + jnp.arange(2, dtype=jnp.int32)[None, :]) ^ (2 * jnp.arange(heads // 2, dtype=jnp.int32))[:, None]
    pair_heads = (pair_heads // sharing).reshape(-1)
    half = inner // 2
    partial = project(pair_heads, arrived[:half], *matrices) + project(pair_heads, arrived[half:], *matrices)
    parts = [
        [partial[k][f] if k == f == 0 else swap_both(partial[k][f], "head", 2 * f, "inner", k) for k in range(inner)]
        for f in range(heads // 2)
    ]
    mine, others = total(jnp.reshape(member, (1,)), parts)
    own = jnp.concatenate([mine, swap(others, "head", 1)], axis=0)

    nearby = swap_all([own] * inner, "inner")
    blocks, cycle = [], []
    for j in range(outer):
        for k in range(inner):
            blocks.append(nearby[k] if j == 0 else swap(nearby[k], "outer", j))
            cycle.append((z ^ k) * outer + (x ^ j))

    block_size = tokens // 2
    row = jnp.arange(tokens, dtype=jnp.int32)
    order = block_order.reshape(-1, 2)

    def positions(shard):
        return (lax.dynamic_index_in_dim(order, shard, 0, False)[:, None] * block_size + row[None, :block_size]).reshape(
            tokens
        )

    query_pos = positions(z * outer + x)
    shards = jnp.stack(cycle)
    distance = jnp.arange(heads, dtype=jnp.int32).reshape(heads // 2, 2).T.reshape(heads)
    rows_of = ((head ^ distance)[:, None] * sub + row[None, :sub]).reshape(tokens)
    one_hot = shards[:, None] == jnp.arange(order.shape[0], dtype=jnp.int32)[None, :]
    firsts = jnp.sum(jnp.where(one_hot[:, :, None], order[None], 0), axis=1)
    block_of = jnp.where(rows_of[None, :] < block_size, firsts[:, :1], firsts[:, 1:])
    key_pos = (block_of * block_size + rows_of[None, :] % block_size).reshape(1, -1)

    place = head_index, queries, query_pos[:, None], key_pos, blocks
    *leaving, keys, values = attend(range(1, heads), heads, *place)
    own_rows = attend(range(1), heads, *place, stacked=(keys, values))
    return join(head_index, swap_all([*own_rows, *leaving], "head"))


def solution(mesh):
    placed = (
        P(("inner", "outer"), None),
        P("inner", None),
        P("inner", None),
        P(("inner", "outer"), "head"),
        P(),
    )
    return jax.shard_map(
        body,
        mesh=mesh,
        in_specs=placed,
        out_specs=P(("inner", "outer"), "head", None, None),
        check_vma=False,
    )
```

```python
import functools
import math

import jax
import jax.numpy as jnp
from jax import lax
from jax.experimental import pallas as pl
from jax.experimental.pallas import tpu as pltpu
from jax.sharding import PartitionSpec as P

QUERY_HEADS = 32
KEY_VALUE_HEADS = 4
HEAD_WIDTH = 128
VMEM = pl.BlockSpec(memory_space=pltpu.VMEM)
SMEM = pl.BlockSpec(memory_space=pltpu.SMEM)
HBM = pl.BlockSpec(memory_space=pltpu.HBM)
LIMIT = 16 * 1024 * 1024


def params():
    return pltpu.CompilerParams(vmem_limit_bytes=LIMIT)


def swap(piece, axis, offset):
    return lax.ppermute(piece, axis, [(i, i ^ offset) for i in range(lax.axis_size(axis))])


def swap_all(pieces, axis):
    got = {k: swap(pieces[k], axis, k) for k in reversed(range(1, len(pieces)))}
    return [pieces[0]] + [got[k] for k in range(1, len(pieces))]


def copies(pairs, sems):
    started = [pltpu.make_async_copy(source, target, sems.at[i]) for i, (source, target) in enumerate(pairs)]
    for copy in started:
        copy.start()
    for copy in started:
        copy.wait()


def load_kernel(*refs):
    half = len(refs) // 2
    copies(list(zip(refs[:half], refs[half : 2 * half])), refs[-1])


def load(*arrays):
    return pl.pallas_call(
        load_kernel,
        out_shape=[jax.ShapeDtypeStruct(a.shape, a.dtype) for a in arrays],
        in_specs=[HBM] * len(arrays),
        out_specs=[VMEM] * len(arrays),
        scratch_shapes=[pltpu.SemaphoreType.DMA((len(arrays),))],
        compiler_params=params(),
        cost_estimate=pl.CostEstimate(flops=0, bytes_accessed=2 * sum(a.size * 2 for a in arrays), transcendentals=0),
        name="load",
    )(*arrays)


def project_kernel(count, keeps, *refs):
    pieces, (key_matrix, value_matrix), outs = refs[:count], refs[count : count + 2], refs[count + 2 :]
    rows = pieces[0][...] if count == 1 else jnp.concatenate([piece[...] for piece in pieces], axis=0)
    width = key_matrix.shape[1]
    sub = outs[0].shape[0]
    keys = jnp.dot(rows, key_matrix[...], preferred_element_type=jnp.float32)
    values = jnp.dot(rows, value_matrix[...], preferred_element_type=jnp.float32)
    for k, out in enumerate(outs):
        key, value = keys[k * sub : (k + 1) * sub], values[k * sub : (k + 1) * sub]
        if keeps and k == 0:
            out[:, :width], out[:, width:] = key, value
        else:
            high = key.astype(out.dtype)
            out[:, :width], out[:, width : 2 * width] = high, (key - high.astype(jnp.float32)).astype(out.dtype)
            out[:, 2 * width :] = value.astype(out.dtype)


def project(pieces, key_matrix, value_matrix, keeps):
    sub, width = pieces[0].shape[0], key_matrix.shape[1]
    given = pieces if sub % 16 == 0 else [jnp.concatenate(pieces, axis=0)]
    shapes = [jax.ShapeDtypeStruct((sub, 3 * width), jnp.bfloat16)] * len(pieces)
    if keeps:
        shapes[0] = jax.ShapeDtypeStruct((sub, 2 * width), jnp.float32)
    return pl.pallas_call(
        functools.partial(project_kernel, len(given), keeps),
        out_shape=shapes,
        in_specs=[VMEM] * (len(given) + 2),
        out_specs=[VMEM] * len(pieces),
        compiler_params=params(),
        cost_estimate=pl.CostEstimate(
            flops=4 * len(pieces) * sub * key_matrix.size, bytes_accessed=4 * key_matrix.size, transcendentals=0
        ),
        name="project",
    )(*given, key_matrix, value_matrix)


def total_kernel(count, heads_of, *refs):
    (own, *parts), outs = refs[:count], refs[count:]
    width = own.shape[1] // 2
    for k, out in enumerate(outs):
        first = pl.multiple_of(heads_of[k] * HEAD_WIDTH, HEAD_WIDTH)

        def columns(ref, third):
            return ref[:, pl.ds(third * width + first, HEAD_WIDTH)].astype(jnp.float32)

        key, value = columns(own, 0), columns(own, 1)
        for part in parts:
            key = key + (columns(part, 0) + columns(part, 1))
            value = value + columns(part, 2)
        out[:, :HEAD_WIDTH], out[:, HEAD_WIDTH:] = key.astype(out.dtype), value.astype(out.dtype)


def total(parts, heads_of, receivers):
    rows = parts[0].shape[0]
    return pl.pallas_call(
        lambda heads_ref, *refs: total_kernel(len(parts), heads_ref, *refs),
        out_shape=[jax.ShapeDtypeStruct((rows, 2 * HEAD_WIDTH), jnp.bfloat16)] * receivers,
        in_specs=[SMEM] + [VMEM] * len(parts),
        out_specs=[VMEM] * receivers,
        compiler_params=params(),
        name="total",
    )(heads_of, *parts)


def stack_kernel(count, *refs):
    blocks, (keys, values) = refs[:count], refs[count:]
    tokens = blocks[0].shape[0]
    for b, block in enumerate(blocks):
        keys[b * tokens : (b + 1) * tokens, :] = block[:, :HEAD_WIDTH]
        values[b * tokens : (b + 1) * tokens, :] = block[:, HEAD_WIDTH:]


def attend_kernel(count, offsets, head_index, queries, query_pos, key_pos, *refs):
    if count:
        outs, (keys, values) = refs[count:-2], refs[-2:]
        stack_kernel(count, *refs[:count], keys, values)
    else:
        (keys, values), outs = refs[:2], refs[2:]
    sub = outs[0].shape[0]
    per_device = queries.shape[1] // HEAD_WIDTH
    length = keys.shape[0]
    factor = math.log2(math.e) / math.sqrt(HEAD_WIDTH)
    for k, out in zip(offsets, outs):
        first = pl.multiple_of((head_index[0] ^ k) * sub, sub)
        rows = queries[pl.ds(first, sub), :]
        stacked = jnp.concatenate([rows[:, i * HEAD_WIDTH : (i + 1) * HEAD_WIDTH] for i in range(per_device)], axis=0)
        scores = lax.dot_general(stacked, keys[...], (((1,), (1,)), ((), ())), preferred_element_type=jnp.float32)
        allowed = key_pos[...] <= query_pos[pl.ds(first, sub), :]
        scores = jnp.where(allowed[None], scores.reshape(per_device, sub, length), -1e30)
        largest = jnp.max(scores, axis=2, keepdims=True)
        unnormed = jnp.exp2((scores - largest) * factor)
        totals = jnp.sum(unnormed, axis=2, keepdims=True)
        weights = unnormed.astype(jnp.bfloat16).reshape(per_device * sub, length)
        mixed = jnp.dot(weights, values[...], preferred_element_type=jnp.float32)
        mixed = mixed.reshape(per_device, sub, HEAD_WIDTH) / totals
        for i in range(per_device):
            out[:, i * HEAD_WIDTH : (i + 1) * HEAD_WIDTH] = mixed[i].astype(out.dtype)


def attend(offsets, receivers, head_index, queries, query_pos, key_pos, blocks, stacked=()):
    tokens, width = queries.shape
    length = key_pos.shape[1]
    count = 0 if stacked else len(blocks)
    given = stacked or blocks
    piece = jax.ShapeDtypeStruct((tokens // receivers, width), jnp.bfloat16)
    held = [] if stacked else [jax.ShapeDtypeStruct((length, HEAD_WIDTH), jnp.bfloat16)] * 2
    rows = tokens * len(offsets) // receivers
    work = rows * length * width
    return pl.pallas_call(
        functools.partial(attend_kernel, count, offsets),
        out_shape=[piece] * len(offsets) + held,
        in_specs=[SMEM] + [VMEM] * (3 + len(given)),
        out_specs=[VMEM] * (len(offsets) + len(held)),
        compiler_params=params(),
        cost_estimate=pl.CostEstimate(
            flops=16 * work, bytes_accessed=4 * length * HEAD_WIDTH, transcendentals=work // HEAD_WIDTH
        ),
        name="attend",
    )(head_index, queries, query_pos, key_pos, *given)


def join_kernel(count, head_index, *refs):
    pieces, (out, sems) = refs[:count], refs[count:]
    width = pieces[0].shape[1]
    copies(
        [
            (piece, out.at[0, 0, :, pl.ds(pl.multiple_of((head_index[0] ^ k) * width, width), width)])
            for k, piece in enumerate(pieces)
        ],
        sems,
    )


def join(head_index, pieces):
    rows, width = pieces[0].shape
    return pl.pallas_call(
        functools.partial(join_kernel, len(pieces)),
        out_shape=jax.ShapeDtypeStruct((1, 1, rows, width * len(pieces)), jnp.bfloat16),
        in_specs=[SMEM] + [VMEM] * len(pieces),
        out_specs=HBM,
        scratch_shapes=[pltpu.SemaphoreType.DMA((len(pieces),))],
        compiler_params=params(),
        name="join",
    )(head_index, *pieces)


def body(activations, key_matrix, value_matrix, queries, block_order):
    heads, inner, outer = (lax.axis_size(name) for name in ("head", "inner", "outer"))
    head, z, x = (lax.axis_index(name) for name in ("head", "inner", "outer"))
    tokens = activations.shape[0]
    sub = tokens // heads
    depth = key_matrix.shape[0]
    sharing = heads // KEY_VALUE_HEADS
    head_index = jnp.reshape(head, (1,))

    pieces = [
        lax.dynamic_slice(activations, (head * sub, (z ^ k) * depth), (sub, depth)) for k in range(inner)
    ]
    pieces[0], matrices = lax.optimization_barrier((pieces[0], (key_matrix, value_matrix)))
    arrived = swap_all(pieces, "inner")
    matrices = load(*matrices)
    half = max(inner // 2, 1)
    partial = [*project(arrived[:half], *matrices, True), *(project(arrived[half:], *matrices, False) if inner > 1 else [])]
    heads_of = (head ^ jnp.arange(heads, dtype=jnp.int32)) // sharing
    parts = swap_all(partial, "inner")
    shares = total(parts, heads_of, heads)
    own = jnp.concatenate(swap_all(shares, "head"), axis=0)

    nearby = swap_all([own] * inner, "inner")
    blocks, cycle = [], []
    for j in range(outer):
        for k in range(inner):
            blocks.append(nearby[k] if j == 0 else swap(nearby[k], "outer", j))
            cycle.append((z ^ k) * outer + (x ^ j))

    block_size = tokens // 2
    row = jnp.arange(tokens, dtype=jnp.int32)
    order = block_order.reshape(-1, 2)

    def positions(shard):
        return (lax.dynamic_index_in_dim(order, shard, 0, False)[:, None] * block_size + row[None, :block_size]).reshape(
            tokens
        )

    query_pos = positions(z * outer + x)
    shards = jnp.stack(cycle)
    rows_of = ((head ^ jnp.arange(heads, dtype=jnp.int32))[:, None] * sub + row[None, :sub]).reshape(tokens)
    one_hot = shards[:, None] == jnp.arange(order.shape[0], dtype=jnp.int32)[None, :]
    firsts = jnp.sum(jnp.where(one_hot[:, :, None], order[None], 0), axis=1)
    block_of = jnp.where(rows_of[None, :] < block_size, firsts[:, :1], firsts[:, 1:])
    key_pos = (block_of * block_size + rows_of[None, :] % block_size).reshape(1, -1)

    place = head_index, queries, query_pos[:, None], key_pos, blocks
    *leaving, keys, values = attend(range(1, heads), heads, *place)
    own_rows = attend(range(1), heads, *place, stacked=(keys, values))
    return join(head_index, swap_all([*own_rows, *leaving], "head"))


def solution(mesh):
    placed = (
        P(("inner", "outer"), None),
        P("inner", None),
        P("inner", None),
        P(("inner", "outer"), "head"),
        P(),
    )
    return jax.shard_map(
        body,
        mesh=mesh,
        in_specs=placed,
        out_specs=P(("inner", "outer"), "head", None, None),
        check_vma=False,
    )
```

```python
import functools
import math

import jax
import jax.numpy as jnp
from jax import lax
from jax.experimental import pallas as pl
from jax.experimental.pallas import tpu as pltpu
from jax.sharding import PartitionSpec as P

QUERY_HEADS = 32
KEY_VALUE_HEADS = 4
HEAD_WIDTH = 128
VMEM = pl.BlockSpec(memory_space=pltpu.VMEM)
SMEM = pl.BlockSpec(memory_space=pltpu.SMEM)
HBM = pl.BlockSpec(memory_space=pltpu.HBM)
LIMIT = 16 * 1024 * 1024


def params():
    return pltpu.CompilerParams(vmem_limit_bytes=LIMIT)


def swap(piece, axis, offset):
    return lax.ppermute(piece, axis, [(i, i ^ offset) for i in range(lax.axis_size(axis))])


def swap_all(pieces, axis):
    got = {k: swap(pieces[k], axis, k) for k in reversed(range(1, len(pieces)))}
    return [pieces[0]] + [got[k] for k in range(1, len(pieces))]


def copies(pairs, sems):
    started = [pltpu.make_async_copy(source, target, sems.at[i]) for i, (source, target) in enumerate(pairs)]
    for copy in started:
        copy.start()
    for copy in started:
        copy.wait()


def load_kernel(*refs):
    half = len(refs) // 2
    copies(list(zip(refs[:half], refs[half : 2 * half])), refs[-1])


def load(*arrays):
    return pl.pallas_call(
        load_kernel,
        out_shape=[jax.ShapeDtypeStruct(a.shape, a.dtype) for a in arrays],
        in_specs=[HBM] * len(arrays),
        out_specs=[VMEM] * len(arrays),
        scratch_shapes=[pltpu.SemaphoreType.DMA((len(arrays),))],
        compiler_params=params(),
        cost_estimate=pl.CostEstimate(flops=0, bytes_accessed=2 * sum(a.size * 2 for a in arrays), transcendentals=0),
        name="load",
    )(*arrays)


def project_kernel(count, *refs):
    pieces, (key_matrix, value_matrix), outs = refs[:count], refs[count : count + 2], refs[count + 2 :]
    rows = pieces[0][...] if count == 1 else jnp.concatenate([piece[...] for piece in pieces], axis=0)
    width = key_matrix.shape[1]
    sub = outs[0].shape[0]
    keys = jnp.dot(rows, key_matrix[...], preferred_element_type=jnp.float32)
    values = jnp.dot(rows, value_matrix[...], preferred_element_type=jnp.float32)
    for k, out in enumerate(outs):
        key, value = keys[k * sub : (k + 1) * sub], values[k * sub : (k + 1) * sub]
        if k == 0:
            out[:, :width], out[:, width:] = key, value
        else:
            high = key.astype(out.dtype)
            out[:, :width], out[:, width : 2 * width] = high, (key - high.astype(jnp.float32)).astype(out.dtype)
            out[:, 2 * width :] = value.astype(out.dtype)


def project(pieces, key_matrix, value_matrix):
    sub, width = pieces[0].shape[0], key_matrix.shape[1]
    given = pieces if sub % 16 == 0 else [jnp.concatenate(pieces, axis=0)]
    kept = jax.ShapeDtypeStruct((sub, 2 * width), jnp.float32)
    sent = jax.ShapeDtypeStruct((sub, 3 * width), jnp.bfloat16)
    return pl.pallas_call(
        functools.partial(project_kernel, len(given)),
        out_shape=[kept] + [sent] * (len(pieces) - 1),
        in_specs=[VMEM] * (len(given) + 2),
        out_specs=[VMEM] * len(pieces),
        compiler_params=params(),
        cost_estimate=pl.CostEstimate(
            flops=4 * len(pieces) * sub * key_matrix.size, bytes_accessed=4 * key_matrix.size, transcendentals=0
        ),
        name="project",
    )(*given, key_matrix, value_matrix)


def total_kernel(count, heads_of, *refs):
    (own, *parts), outs = refs[:count], refs[count:]
    width = own.shape[1] // 2
    for k, out in enumerate(outs):
        first = pl.multiple_of(heads_of[k] * HEAD_WIDTH, HEAD_WIDTH)

        def columns(ref, third):
            return ref[:, pl.ds(third * width + first, HEAD_WIDTH)].astype(jnp.float32)

        key, value = columns(own, 0), columns(own, 1)
        for part in parts:
            key = key + (columns(part, 0) + columns(part, 1))
            value = value + columns(part, 2)
        out[:, :HEAD_WIDTH], out[:, HEAD_WIDTH:] = key.astype(out.dtype), value.astype(out.dtype)


def total(parts, heads_of, receivers):
    rows = parts[0].shape[0]
    return pl.pallas_call(
        lambda heads_ref, *refs: total_kernel(len(parts), heads_ref, *refs),
        out_shape=[jax.ShapeDtypeStruct((rows, 2 * HEAD_WIDTH), jnp.bfloat16)] * receivers,
        in_specs=[SMEM] + [VMEM] * len(parts),
        out_specs=[VMEM] * receivers,
        compiler_params=params(),
        name="total",
    )(heads_of, *parts)


def stack_kernel(count, *refs):
    blocks, (keys, values) = refs[:count], refs[count:]
    tokens = blocks[0].shape[0]
    for b, block in enumerate(blocks):
        keys[b * tokens : (b + 1) * tokens, :] = block[:, :HEAD_WIDTH]
        values[b * tokens : (b + 1) * tokens, :] = block[:, HEAD_WIDTH:]


def attend_kernel(count, offsets, head_index, queries, query_pos, key_pos, *refs):
    if count:
        outs, (keys, values) = refs[count:-2], refs[-2:]
        stack_kernel(count, *refs[:count], keys, values)
    else:
        (keys, values), outs = refs[:2], refs[2:]
    sub = outs[0].shape[0]
    per_device = queries.shape[1] // HEAD_WIDTH
    length = keys.shape[0]
    factor = math.log2(math.e) / math.sqrt(HEAD_WIDTH)
    for k, out in zip(offsets, outs):
        first = pl.multiple_of((head_index[0] ^ k) * sub, sub)
        rows = queries[pl.ds(first, sub), :]
        stacked = jnp.concatenate([rows[:, i * HEAD_WIDTH : (i + 1) * HEAD_WIDTH] for i in range(per_device)], axis=0)
        scores = lax.dot_general(stacked, keys[...], (((1,), (1,)), ((), ())), preferred_element_type=jnp.float32)
        allowed = key_pos[...] <= query_pos[pl.ds(first, sub), :]
        scores = jnp.where(allowed[None], scores.reshape(per_device, sub, length), -1e30)
        largest = jnp.max(scores, axis=2, keepdims=True)
        unnormed = jnp.exp2((scores - largest) * factor)
        totals = jnp.sum(unnormed, axis=2, keepdims=True)
        weights = unnormed.astype(jnp.bfloat16).reshape(per_device * sub, length)
        mixed = jnp.dot(weights, values[...], preferred_element_type=jnp.float32)
        mixed = mixed.reshape(per_device, sub, HEAD_WIDTH) / totals
        for i in range(per_device):
            out[:, i * HEAD_WIDTH : (i + 1) * HEAD_WIDTH] = mixed[i].astype(out.dtype)


def attend(offsets, receivers, head_index, queries, query_pos, key_pos, blocks, stacked=()):
    tokens, width = queries.shape
    length = key_pos.shape[1]
    count = 0 if stacked else len(blocks)
    given = stacked or blocks
    piece = jax.ShapeDtypeStruct((tokens // receivers, width), jnp.bfloat16)
    held = [] if stacked else [jax.ShapeDtypeStruct((length, HEAD_WIDTH), jnp.bfloat16)] * 2
    rows = tokens * len(offsets) // receivers
    work = rows * length * width
    return pl.pallas_call(
        functools.partial(attend_kernel, count, offsets),
        out_shape=[piece] * len(offsets) + held,
        in_specs=[SMEM] + [VMEM] * (3 + len(given)),
        out_specs=[VMEM] * (len(offsets) + len(held)),
        compiler_params=params(),
        cost_estimate=pl.CostEstimate(
            flops=16 * work, bytes_accessed=4 * length * HEAD_WIDTH, transcendentals=work // HEAD_WIDTH
        ),
        name="attend",
    )(head_index, queries, query_pos, key_pos, *given)


def join_kernel(count, head_index, *refs):
    pieces, (out, sems) = refs[:count], refs[count:]
    width = pieces[0].shape[1]
    copies(
        [
            (piece, out.at[0, 0, :, pl.ds(pl.multiple_of((head_index[0] ^ k) * width, width), width)])
            for k, piece in enumerate(pieces)
        ],
        sems,
    )


def join(head_index, pieces):
    rows, width = pieces[0].shape
    return pl.pallas_call(
        functools.partial(join_kernel, len(pieces)),
        out_shape=jax.ShapeDtypeStruct((1, 1, rows, width * len(pieces)), jnp.bfloat16),
        in_specs=[SMEM] + [VMEM] * len(pieces),
        out_specs=HBM,
        scratch_shapes=[pltpu.SemaphoreType.DMA((len(pieces),))],
        compiler_params=params(),
        name="join",
    )(head_index, *pieces)


def body(activations, key_matrix, value_matrix, queries, block_order):
    heads, inner, outer = (lax.axis_size(name) for name in ("head", "inner", "outer"))
    head, z, x = (lax.axis_index(name) for name in ("head", "inner", "outer"))
    tokens = activations.shape[0]
    sub = tokens // heads
    depth = key_matrix.shape[0]
    sharing = heads // KEY_VALUE_HEADS
    head_index = jnp.reshape(head, (1,))

    pieces = [
        lax.dynamic_slice(activations, (head * sub, (z ^ k) * depth), (sub, depth)) for k in range(inner)
    ]
    pieces[0], matrices = lax.optimization_barrier((pieces[0], (key_matrix, value_matrix)))
    arrived = swap_all(pieces, "inner")
    matrices = load(*matrices)
    partial = project(arrived, *matrices)
    heads_of = (head ^ jnp.arange(heads, dtype=jnp.int32)) // sharing
    parts = swap_all(partial, "inner")
    shares = total(parts, heads_of, heads)
    own = jnp.concatenate(swap_all(shares, "head"), axis=0)

    nearby = swap_all([own] * inner, "inner")
    blocks, cycle = [], []
    for j in range(outer):
        for k in range(inner):
            blocks.append(nearby[k] if j == 0 else swap(nearby[k], "outer", j))
            cycle.append((z ^ k) * outer + (x ^ j))

    block_size = tokens // 2
    row = jnp.arange(tokens, dtype=jnp.int32)
    order = block_order.reshape(-1, 2)

    def positions(shard):
        return (lax.dynamic_index_in_dim(order, shard, 0, False)[:, None] * block_size + row[None, :block_size]).reshape(
            tokens
        )

    query_pos = positions(z * outer + x)
    shards = jnp.stack(cycle)
    rows_of = ((head ^ jnp.arange(heads, dtype=jnp.int32))[:, None] * sub + row[None, :sub]).reshape(tokens)
    one_hot = shards[:, None] == jnp.arange(order.shape[0], dtype=jnp.int32)[None, :]
    firsts = jnp.sum(jnp.where(one_hot[:, :, None], order[None], 0), axis=1)
    block_of = jnp.where(rows_of[None, :] < block_size, firsts[:, :1], firsts[:, 1:])
    key_pos = (block_of * block_size + rows_of[None, :] % block_size).reshape(1, -1)

    place = head_index, queries, query_pos[:, None], key_pos, blocks
    *leaving, keys, values = attend(range(1, heads), heads, *place)
    own_rows = attend(range(1), heads, *place, stacked=(keys, values))
    return join(head_index, swap_all([*own_rows, *leaving], "head"))


def solution(mesh):
    placed = (
        P(("inner", "outer"), None),
        P("inner", None),
        P("inner", None),
        P(("inner", "outer"), "head"),
        P(),
    )
    return jax.shard_map(
        body,
        mesh=mesh,
        in_specs=placed,
        out_specs=P(("inner", "outer"), "head", None, None),
        check_vma=False,
    )
```

```python
import functools
import math

import jax
import jax.numpy as jnp
from jax import lax
from jax.experimental import pallas as pl
from jax.experimental.pallas import tpu as pltpu
from jax.sharding import PartitionSpec as P

QUERY_HEADS = 32
KEY_VALUE_HEADS = 4
HEAD_WIDTH = 128
VMEM = pl.BlockSpec(memory_space=pltpu.VMEM)
SMEM = pl.BlockSpec(memory_space=pltpu.SMEM)
HBM = pl.BlockSpec(memory_space=pltpu.HBM)
LIMIT = 16 * 1024 * 1024


def params():
    return pltpu.CompilerParams(vmem_limit_bytes=LIMIT)


def swap(piece, axis, offset):
    return lax.ppermute(piece, axis, [(i, i ^ offset) for i in range(lax.axis_size(axis))])


def swap_all(pieces, axis):
    got = {k: swap(pieces[k], axis, k) for k in reversed(range(1, len(pieces)))}
    return [pieces[0]] + [got[k] for k in range(1, len(pieces))]


def copies(pairs, sems):
    started = [pltpu.make_async_copy(source, target, sems.at[i]) for i, (source, target) in enumerate(pairs)]
    for copy in started:
        copy.start()
    for copy in started:
        copy.wait()


def project_kernel(count, keeps, *refs):
    pieces, (key_matrix, value_matrix), outs = refs[:count], refs[count : count + 2], refs[count + 2 :]
    rows = pieces[0][...] if count == 1 else jnp.concatenate([piece[...] for piece in pieces], axis=0)
    width = key_matrix.shape[1]
    sub = outs[0].shape[0]
    keys = jnp.dot(rows, key_matrix[...], preferred_element_type=jnp.float32)
    values = jnp.dot(rows, value_matrix[...], preferred_element_type=jnp.float32)
    for k, out in enumerate(outs):
        key, value = keys[k * sub : (k + 1) * sub], values[k * sub : (k + 1) * sub]
        if keeps and k == 0:
            out[:, :width], out[:, width:] = key, value
        else:
            high = key.astype(out.dtype)
            out[:, :width], out[:, width : 2 * width] = high, (key - high.astype(jnp.float32)).astype(out.dtype)
            out[:, 2 * width :] = value.astype(out.dtype)


def project(pieces, key_matrix, value_matrix, keeps):
    sub, width = pieces[0].shape[0], key_matrix.shape[1]
    given = pieces if sub % 16 == 0 else [jnp.concatenate(pieces, axis=0)]
    kept = jax.ShapeDtypeStruct((sub, 2 * width), jnp.float32)
    sent = jax.ShapeDtypeStruct((sub, 3 * width), jnp.bfloat16)
    return pl.pallas_call(
        functools.partial(project_kernel, len(given), keeps),
        out_shape=[kept if keeps and k == 0 else sent for k in range(len(pieces))],
        in_specs=[VMEM] * (len(given) + 2),
        out_specs=[VMEM] * len(pieces),
        compiler_params=params(),
        cost_estimate=pl.CostEstimate(
            flops=4 * len(pieces) * sub * key_matrix.size, bytes_accessed=4 * key_matrix.size, transcendentals=0
        ),
        name="project",
    )(*given, key_matrix, value_matrix)


def total_kernel(count, heads_of, *refs):
    (own, *parts), outs = refs[:count], refs[count:]
    width = own.shape[1] // 2
    for k, out in enumerate(outs):
        first = pl.multiple_of(heads_of[k] * HEAD_WIDTH, HEAD_WIDTH)

        def columns(ref, third):
            return ref[:, pl.ds(third * width + first, HEAD_WIDTH)].astype(jnp.float32)

        key, value = columns(own, 0), columns(own, 1)
        for part in parts:
            key = key + (columns(part, 0) + columns(part, 1))
            value = value + columns(part, 2)
        out[:, :HEAD_WIDTH], out[:, HEAD_WIDTH:] = key.astype(out.dtype), value.astype(out.dtype)


def total(parts, heads_of, receivers):
    rows = parts[0].shape[0]
    return pl.pallas_call(
        lambda heads_ref, *refs: total_kernel(len(parts), heads_ref, *refs),
        out_shape=[jax.ShapeDtypeStruct((rows, 2 * HEAD_WIDTH), jnp.bfloat16)] * receivers,
        in_specs=[SMEM] + [VMEM] * len(parts),
        out_specs=[VMEM] * receivers,
        compiler_params=params(),
        name="total",
    )(heads_of, *parts)


def stack_kernel(count, *refs):
    blocks, (keys, values) = refs[:count], refs[count:]
    tokens = blocks[0].shape[0]
    for b, block in enumerate(blocks):
        keys[b * tokens : (b + 1) * tokens, :] = block[:, :HEAD_WIDTH]
        values[b * tokens : (b + 1) * tokens, :] = block[:, HEAD_WIDTH:]


def attend_kernel(count, offsets, head_index, queries, query_pos, key_pos, *refs):
    if count:
        outs, (keys, values) = refs[count:-2], refs[-2:]
        stack_kernel(count, *refs[:count], keys, values)
    else:
        (keys, values), outs = refs[:2], refs[2:]
    sub = outs[0].shape[0]
    per_device = queries.shape[1] // HEAD_WIDTH
    length = keys.shape[0]
    factor = math.log2(math.e) / math.sqrt(HEAD_WIDTH)
    for k, out in zip(offsets, outs):
        first = pl.multiple_of((head_index[0] ^ k) * sub, sub)
        rows = queries[pl.ds(first, sub), :]
        stacked = jnp.concatenate([rows[:, i * HEAD_WIDTH : (i + 1) * HEAD_WIDTH] for i in range(per_device)], axis=0)
        scores = lax.dot_general(stacked, keys[...], (((1,), (1,)), ((), ())), preferred_element_type=jnp.float32)
        allowed = key_pos[...] <= query_pos[pl.ds(first, sub), :]
        scores = jnp.where(allowed[None], scores.reshape(per_device, sub, length), -1e30)
        largest = jnp.max(scores, axis=2, keepdims=True)
        unnormed = jnp.exp2((scores - largest) * factor)
        totals = jnp.sum(unnormed, axis=2, keepdims=True)
        weights = unnormed.astype(jnp.bfloat16).reshape(per_device * sub, length)
        mixed = jnp.dot(weights, values[...], preferred_element_type=jnp.float32)
        mixed = mixed.reshape(per_device, sub, HEAD_WIDTH) / totals
        for i in range(per_device):
            out[:, i * HEAD_WIDTH : (i + 1) * HEAD_WIDTH] = mixed[i].astype(out.dtype)


def attend(offsets, receivers, head_index, queries, query_pos, key_pos, blocks, stacked=()):
    tokens, width = queries.shape
    length = key_pos.shape[1]
    count = 0 if stacked else len(blocks)
    given = stacked or blocks
    piece = jax.ShapeDtypeStruct((tokens // receivers, width), jnp.bfloat16)
    held = [] if stacked else [jax.ShapeDtypeStruct((length, HEAD_WIDTH), jnp.bfloat16)] * 2
    rows = tokens * len(offsets) // receivers
    work = rows * length * width
    return pl.pallas_call(
        functools.partial(attend_kernel, count, offsets),
        out_shape=[piece] * len(offsets) + held,
        in_specs=[SMEM] + [VMEM] * (3 + len(given)),
        out_specs=[VMEM] * (len(offsets) + len(held)),
        compiler_params=params(),
        cost_estimate=pl.CostEstimate(
            flops=16 * work, bytes_accessed=4 * length * HEAD_WIDTH, transcendentals=work // HEAD_WIDTH
        ),
        name="attend",
    )(head_index, queries, query_pos, key_pos, *given)


def join_kernel(count, head_index, *refs):
    pieces, (out, sems) = refs[:count], refs[count:]
    width = pieces[0].shape[1]
    copies(
        [
            (piece, out.at[0, 0, :, pl.ds(pl.multiple_of((head_index[0] ^ k) * width, width), width)])
            for k, piece in enumerate(pieces)
        ],
        sems,
    )


def join(head_index, pieces):
    rows, width = pieces[0].shape
    return pl.pallas_call(
        functools.partial(join_kernel, len(pieces)),
        out_shape=jax.ShapeDtypeStruct((1, 1, rows, width * len(pieces)), jnp.bfloat16),
        in_specs=[SMEM] + [VMEM] * len(pieces),
        out_specs=HBM,
        scratch_shapes=[pltpu.SemaphoreType.DMA((len(pieces),))],
        compiler_params=params(),
        name="join",
    )(head_index, *pieces)


def body(activations, key_matrix, value_matrix, queries, block_order):
    heads, inner, outer = (lax.axis_size(name) for name in ("head", "inner", "outer"))
    head, z, x = (lax.axis_index(name) for name in ("head", "inner", "outer"))
    tokens = activations.shape[0]
    sub = tokens // heads
    depth = key_matrix.shape[0]
    sharing = heads // KEY_VALUE_HEADS
    head_index = jnp.reshape(head, (1,))

    pieces = [
        lax.dynamic_slice(activations, (head * sub, (z ^ k) * depth), (sub, depth)) for k in range(inner)
    ]
    arrived = swap_all(pieces, "inner")
    half = max(inner // 2, 1)
    partial = project(arrived[:half], key_matrix, value_matrix, True)
    if inner > 1:
        partial, far = lax.optimization_barrier((partial, arrived[half:]))
        partial = [*partial, *project(far, key_matrix, value_matrix, False)]
    heads_of = (head ^ jnp.arange(heads, dtype=jnp.int32)) // sharing
    parts = swap_all(partial, "inner")
    shares = total(parts, heads_of, heads)
    own = jnp.concatenate(swap_all(shares, "head"), axis=0)

    nearby = swap_all([own] * inner, "inner")
    blocks, cycle = [], []
    for j in range(outer):
        for k in range(inner):
            blocks.append(nearby[k] if j == 0 else swap(nearby[k], "outer", j))
            cycle.append((z ^ k) * outer + (x ^ j))

    block_size = tokens // 2
    row = jnp.arange(tokens, dtype=jnp.int32)
    order = block_order.reshape(-1, 2)

    def positions(shard):
        return (lax.dynamic_index_in_dim(order, shard, 0, False)[:, None] * block_size + row[None, :block_size]).reshape(
            tokens
        )

    query_pos = positions(z * outer + x)
    shards = jnp.stack(cycle)
    rows_of = ((head ^ jnp.arange(heads, dtype=jnp.int32))[:, None] * sub + row[None, :sub]).reshape(tokens)
    one_hot = shards[:, None] == jnp.arange(order.shape[0], dtype=jnp.int32)[None, :]
    firsts = jnp.sum(jnp.where(one_hot[:, :, None], order[None], 0), axis=1)
    block_of = jnp.where(rows_of[None, :] < block_size, firsts[:, :1], firsts[:, 1:])
    key_pos = (block_of * block_size + rows_of[None, :] % block_size).reshape(1, -1)

    place = head_index, queries, query_pos[:, None], key_pos, blocks
    *leaving, keys, values = attend(range(1, heads), heads, *place)
    own_rows = attend(range(1), heads, *place, stacked=(keys, values))
    return join(head_index, swap_all([*own_rows, *leaving], "head"))


def solution(mesh):
    placed = (
        P(("inner", "outer"), None),
        P("inner", None),
        P("inner", None),
        P(("inner", "outer"), "head"),
        P(),
    )
    return jax.shard_map(
        body,
        mesh=mesh,
        in_specs=placed,
        out_specs=P(("inner", "outer"), "head", None, None),
        check_vma=False,
    )
```

```python
import functools
import math

import jax
import jax.numpy as jnp
from jax import lax
from jax.experimental import pallas as pl
from jax.experimental.pallas import tpu as pltpu
from jax.sharding import PartitionSpec as P

QUERY_HEADS = 32
KEY_VALUE_HEADS = 4
HEAD_WIDTH = 128
VMEM = pl.BlockSpec(memory_space=pltpu.VMEM)
SMEM = pl.BlockSpec(memory_space=pltpu.SMEM)
HBM = pl.BlockSpec(memory_space=pltpu.HBM)
LIMIT = 16 * 1024 * 1024
CUT_LIMIT = 52 * 1024 * 1024
LOAD_LIMIT = 48 * 1024 * 1024


def params(limit=LIMIT):
    return pltpu.CompilerParams(vmem_limit_bytes=limit)


def swap(piece, axis, offset):
    return lax.ppermute(piece, axis, [(i, i ^ offset) for i in range(lax.axis_size(axis))])


def swap_all(pieces, axis):
    got = {k: swap(pieces[k], axis, k) for k in reversed(range(1, len(pieces)))}
    return [pieces[0]] + [got[k] for k in range(1, len(pieces))]


def copies(pairs, sems):
    started = [pltpu.make_async_copy(source, target, sems.at[i]) for i, (source, target) in enumerate(pairs)]
    for copy in started:
        copy.start()
    for copy in started:
        copy.wait()


def cut_kernel(place, activations, *refs):
    outs, sems = refs[:-1], refs[-1]
    sub, depth = outs[0].shape
    first = pl.multiple_of(place[0] * sub, sub)
    copies(
        [
            (activations.at[pl.ds(first, sub), pl.ds(pl.multiple_of((place[1] ^ k) * depth, depth), depth)], outs[k])
            for k in reversed(range(len(outs)))
        ],
        sems,
    )


def cut(place, activations, count, sub, depth):
    if sub % 16:
        return [
            lax.dynamic_slice(activations, (place[0] * sub, (place[1] ^ k) * depth), (sub, depth))
            for k in range(count)
        ]
    return pl.pallas_call(
        cut_kernel,
        out_shape=[jax.ShapeDtypeStruct((sub, depth), activations.dtype)] * count,
        in_specs=[SMEM, HBM],
        out_specs=[VMEM] * count,
        scratch_shapes=[pltpu.SemaphoreType.DMA((count,))],
        compiler_params=params(CUT_LIMIT),
        name="cut",
    )(place, activations)


def load_kernel(*refs):
    half = len(refs) // 2
    copies(list(zip(refs[:half], refs[half : 2 * half])), refs[-1])


def load(*arrays):
    return pl.pallas_call(
        load_kernel,
        out_shape=[jax.ShapeDtypeStruct(a.shape, a.dtype) for a in arrays],
        in_specs=[HBM] * len(arrays),
        out_specs=[VMEM] * len(arrays),
        scratch_shapes=[pltpu.SemaphoreType.DMA((len(arrays),))],
        compiler_params=params(LOAD_LIMIT),
        cost_estimate=pl.CostEstimate(flops=0, bytes_accessed=2 * sum(a.size * 2 for a in arrays), transcendentals=0),
        name="load",
    )(*arrays)


def project_kernel(count, keeps, *refs):
    pieces, (key_matrix, value_matrix), outs = refs[:count], refs[count : count + 2], refs[count + 2 :]
    rows = pieces[0][...] if count == 1 else jnp.concatenate([piece[...] for piece in pieces], axis=0)
    width = key_matrix.shape[1]
    sub = outs[0].shape[0]
    keys = jnp.dot(rows, key_matrix[...], preferred_element_type=jnp.float32)
    values = jnp.dot(rows, value_matrix[...], preferred_element_type=jnp.float32)
    for k, out in enumerate(outs):
        key, value = keys[k * sub : (k + 1) * sub], values[k * sub : (k + 1) * sub]
        if keeps and k == 0:
            out[:, :width], out[:, width:] = key, value
        else:
            high = key.astype(out.dtype)
            out[:, :width], out[:, width : 2 * width] = high, (key - high.astype(jnp.float32)).astype(out.dtype)
            out[:, 2 * width :] = value.astype(out.dtype)


def project(pieces, key_matrix, value_matrix, keeps):
    sub, width = pieces[0].shape[0], key_matrix.shape[1]
    given = pieces if sub % 16 == 0 else [jnp.concatenate(pieces, axis=0)]
    kept = jax.ShapeDtypeStruct((sub, 2 * width), jnp.float32)
    sent = jax.ShapeDtypeStruct((sub, 3 * width), jnp.bfloat16)
    return pl.pallas_call(
        functools.partial(project_kernel, len(given), keeps),
        out_shape=[kept if keeps and k == 0 else sent for k in range(len(pieces))],
        in_specs=[VMEM] * (len(given) + 2),
        out_specs=[VMEM] * len(pieces),
        compiler_params=params(),
        cost_estimate=pl.CostEstimate(
            flops=4 * len(pieces) * sub * key_matrix.size, bytes_accessed=4 * key_matrix.size, transcendentals=0
        ),
        name="project",
    )(*given, key_matrix, value_matrix)


def total_kernel(count, heads_of, *refs):
    (own, *parts), outs = refs[:count], refs[count:]
    width = own.shape[1] // 2
    for k, out in enumerate(outs):
        first = pl.multiple_of(heads_of[k] * HEAD_WIDTH, HEAD_WIDTH)

        def columns(ref, third):
            return ref[:, pl.ds(third * width + first, HEAD_WIDTH)].astype(jnp.float32)

        key, value = columns(own, 0), columns(own, 1)
        for part in parts:
            key = key + (columns(part, 0) + columns(part, 1))
            value = value + columns(part, 2)
        out[:, :HEAD_WIDTH], out[:, HEAD_WIDTH:] = key.astype(out.dtype), value.astype(out.dtype)


def total(parts, heads_of, receivers):
    rows = parts[0].shape[0]
    return pl.pallas_call(
        lambda heads_ref, *refs: total_kernel(len(parts), heads_ref, *refs),
        out_shape=[jax.ShapeDtypeStruct((rows, 2 * HEAD_WIDTH), jnp.bfloat16)] * receivers,
        in_specs=[SMEM] + [VMEM] * len(parts),
        out_specs=[VMEM] * receivers,
        compiler_params=params(),
        name="total",
    )(heads_of, *parts)


def stack_kernel(count, *refs):
    blocks, (keys, values) = refs[:count], refs[count:]
    tokens = blocks[0].shape[0]
    for b, block in enumerate(blocks):
        keys[b * tokens : (b + 1) * tokens, :] = block[:, :HEAD_WIDTH]
        values[b * tokens : (b + 1) * tokens, :] = block[:, HEAD_WIDTH:]


def attend_kernel(count, offsets, head_index, queries, query_pos, key_pos, *refs):
    if count:
        outs, (keys, values) = refs[count:-2], refs[-2:]
        stack_kernel(count, *refs[:count], keys, values)
    else:
        (keys, values), outs = refs[:2], refs[2:]
    sub = outs[0].shape[0]
    per_device = queries.shape[1] // HEAD_WIDTH
    length = keys.shape[0]
    factor = math.log2(math.e) / math.sqrt(HEAD_WIDTH)
    for k, out in zip(offsets, outs):
        first = pl.multiple_of((head_index[0] ^ k) * sub, sub)
        rows = queries[pl.ds(first, sub), :]
        stacked = jnp.concatenate([rows[:, i * HEAD_WIDTH : (i + 1) * HEAD_WIDTH] for i in range(per_device)], axis=0)
        scores = lax.dot_general(stacked, keys[...], (((1,), (1,)), ((), ())), preferred_element_type=jnp.float32)
        allowed = key_pos[...] <= query_pos[pl.ds(first, sub), :]
        scores = jnp.where(allowed[None], scores.reshape(per_device, sub, length), -1e30)
        largest = jnp.max(scores, axis=2, keepdims=True)
        unnormed = jnp.exp2((scores - largest) * factor)
        totals = jnp.sum(unnormed, axis=2, keepdims=True)
        weights = unnormed.astype(jnp.bfloat16).reshape(per_device * sub, length)
        mixed = jnp.dot(weights, values[...], preferred_element_type=jnp.float32)
        mixed = mixed.reshape(per_device, sub, HEAD_WIDTH) / totals
        for i in range(per_device):
            out[:, i * HEAD_WIDTH : (i + 1) * HEAD_WIDTH] = mixed[i].astype(out.dtype)


def attend(offsets, receivers, head_index, queries, query_pos, key_pos, blocks, stacked=()):
    tokens, width = queries.shape
    length = key_pos.shape[1]
    count = 0 if stacked else len(blocks)
    given = stacked or blocks
    piece = jax.ShapeDtypeStruct((tokens // receivers, width), jnp.bfloat16)
    held = [] if stacked else [jax.ShapeDtypeStruct((length, HEAD_WIDTH), jnp.bfloat16)] * 2
    rows = tokens * len(offsets) // receivers
    work = rows * length * width
    return pl.pallas_call(
        functools.partial(attend_kernel, count, offsets),
        out_shape=[piece] * len(offsets) + held,
        in_specs=[SMEM] + [VMEM] * (3 + len(given)),
        out_specs=[VMEM] * (len(offsets) + len(held)),
        compiler_params=params(),
        cost_estimate=pl.CostEstimate(
            flops=16 * work, bytes_accessed=4 * length * HEAD_WIDTH, transcendentals=work // HEAD_WIDTH
        ),
        name="attend",
    )(head_index, queries, query_pos, key_pos, *given)


def join_kernel(count, head_index, *refs):
    pieces, (out, sems) = refs[:count], refs[count:]
    width = pieces[0].shape[1]
    copies(
        [
            (piece, out.at[0, 0, :, pl.ds(pl.multiple_of((head_index[0] ^ k) * width, width), width)])
            for k, piece in enumerate(pieces)
        ],
        sems,
    )


def join(head_index, pieces):
    rows, width = pieces[0].shape
    return pl.pallas_call(
        functools.partial(join_kernel, len(pieces)),
        out_shape=jax.ShapeDtypeStruct((1, 1, rows, width * len(pieces)), jnp.bfloat16),
        in_specs=[SMEM] + [VMEM] * len(pieces),
        out_specs=HBM,
        scratch_shapes=[pltpu.SemaphoreType.DMA((len(pieces),))],
        compiler_params=params(),
        name="join",
    )(head_index, *pieces)


def body(activations, key_matrix, value_matrix, queries, block_order):
    heads, inner, outer = (lax.axis_size(name) for name in ("head", "inner", "outer"))
    head, z, x = (lax.axis_index(name) for name in ("head", "inner", "outer"))
    tokens = activations.shape[0]
    sub = tokens // heads
    depth = key_matrix.shape[0]
    sharing = heads // KEY_VALUE_HEADS
    head_index = jnp.reshape(head, (1,))

    pieces = list(cut(jnp.stack([head, z]), activations, inner, sub, depth))
    pieces[0], matrices = lax.optimization_barrier((pieces[0], (key_matrix, value_matrix)))
    matrices = load(*matrices)
    arrived = swap_all(pieces, "inner")
    half = max(inner // 2, 1)
    partial = project(arrived[:half], *matrices, True)
    if inner > 1:
        _, far = lax.optimization_barrier((partial, arrived[half:]))
        partial = [*partial, *project(far, *matrices, False)]
    heads_of = (head ^ jnp.arange(heads, dtype=jnp.int32)) // sharing
    parts = swap_all(partial, "inner")
    shares = total(parts, heads_of, heads)
    own = jnp.concatenate(swap_all(shares, "head"), axis=0)

    nearby = swap_all([own] * inner, "inner")
    blocks, cycle = [], []
    for j in range(outer):
        for k in range(inner):
            blocks.append(nearby[k] if j == 0 else swap(nearby[k], "outer", j))
            cycle.append((z ^ k) * outer + (x ^ j))

    block_size = tokens // 2
    row = jnp.arange(tokens, dtype=jnp.int32)
    order = block_order.reshape(-1, 2)

    def positions(shard):
        return (lax.dynamic_index_in_dim(order, shard, 0, False)[:, None] * block_size + row[None, :block_size]).reshape(
            tokens
        )

    query_pos = positions(z * outer + x)
    shards = jnp.stack(cycle)
    rows_of = ((head ^ jnp.arange(heads, dtype=jnp.int32))[:, None] * sub + row[None, :sub]).reshape(tokens)
    one_hot = shards[:, None] == jnp.arange(order.shape[0], dtype=jnp.int32)[None, :]
    firsts = jnp.sum(jnp.where(one_hot[:, :, None], order[None], 0), axis=1)
    block_of = jnp.where(rows_of[None, :] < block_size, firsts[:, :1], firsts[:, 1:])
    key_pos = (block_of * block_size + rows_of[None, :] % block_size).reshape(1, -1)

    place = head_index, queries, query_pos[:, None], key_pos, blocks
    *leaving, keys, values = attend(range(1, heads), heads, *place)
    own_rows = attend(range(1), heads, *place, stacked=(keys, values))
    return join(head_index, swap_all([*own_rows, *leaving], "head"))


def solution(mesh):
    placed = (
        P(("inner", "outer"), None),
        P("inner", None),
        P("inner", None),
        P(("inner", "outer"), "head"),
        P(),
    )
    return jax.shard_map(
        body,
        mesh=mesh,
        in_specs=placed,
        out_specs=P(("inner", "outer"), "head", None, None),
        check_vma=False,
    )
```

```python
import functools
import math

import jax
import jax.numpy as jnp
from jax import lax
from jax.experimental import pallas as pl
from jax.experimental.pallas import tpu as pltpu
from jax.sharding import PartitionSpec as P

QUERY_HEADS = 32
KEY_VALUE_HEADS = 4
HEAD_WIDTH = 128
VMEM = pl.BlockSpec(memory_space=pltpu.VMEM)
SMEM = pl.BlockSpec(memory_space=pltpu.SMEM)
HBM = pl.BlockSpec(memory_space=pltpu.HBM)
LIMIT = 16 * 1024 * 1024
LOAD_LIMIT = 48 * 1024 * 1024


def params(limit=LIMIT):
    return pltpu.CompilerParams(vmem_limit_bytes=limit)


def swap(piece, axis, offset):
    return lax.ppermute(piece, axis, [(i, i ^ offset) for i in range(lax.axis_size(axis))])


def swap_all(pieces, axis):
    got = {k: swap(pieces[k], axis, k) for k in reversed(range(1, len(pieces)))}
    return [pieces[0]] + [got[k] for k in range(1, len(pieces))]


def swap_pairs(near, far, axis, after=()):
    rows = near.shape[0]
    got = [(swap(near, axis, 1), 0)]
    for f, both in enumerate(far, 1):
        mine = swap(both, axis, 2 * f)
        ready, _ = lax.optimization_barrier((mine, after))
        got += [(mine, 0), (swap(ready, axis, 1), rows)]
    return got


def copies(pairs, sems):
    started = [pltpu.make_async_copy(source, target, sems.at[i]) for i, (source, target) in enumerate(pairs)]
    for copy in started:
        copy.start()
    for copy in started:
        copy.wait()


def load_kernel(*refs):
    half = len(refs) // 2
    copies(list(zip(refs[:half], refs[half : 2 * half])), refs[-1])


def load(*arrays):
    return pl.pallas_call(
        load_kernel,
        out_shape=[jax.ShapeDtypeStruct(a.shape, a.dtype) for a in arrays],
        in_specs=[HBM] * len(arrays),
        out_specs=[VMEM] * len(arrays),
        scratch_shapes=[pltpu.SemaphoreType.DMA((len(arrays),))],
        compiler_params=params(LOAD_LIMIT),
        cost_estimate=pl.CostEstimate(flops=0, bytes_accessed=2 * sum(a.size * 2 for a in arrays), transcendentals=0),
        name="load",
    )(*arrays)


def project_kernel(count, keeps, *refs):
    pieces, (key_matrix, value_matrix), outs = refs[:count], refs[count : count + 2], refs[count + 2 :]
    rows = pieces[0][...] if count == 1 else jnp.concatenate([piece[...] for piece in pieces], axis=0)
    width = key_matrix.shape[1]
    sub = outs[0].shape[0]
    keys = jnp.dot(rows, key_matrix[...], preferred_element_type=jnp.float32)
    values = jnp.dot(rows, value_matrix[...], preferred_element_type=jnp.float32)
    for k, out in enumerate(outs):
        key, value = keys[k * sub : (k + 1) * sub], values[k * sub : (k + 1) * sub]
        if keeps and k == 0:
            out[:, :width], out[:, width:] = key, value
        else:
            high = key.astype(out.dtype)
            out[:, :width], out[:, width : 2 * width] = high, (key - high.astype(jnp.float32)).astype(out.dtype)
            out[:, 2 * width :] = value.astype(out.dtype)


def project(pieces, key_matrix, value_matrix, keeps):
    sub, width = pieces[0].shape[0], key_matrix.shape[1]
    given = pieces if sub % 16 == 0 else [jnp.concatenate(pieces, axis=0)]
    kept = jax.ShapeDtypeStruct((sub, 2 * width), jnp.float32)
    sent = jax.ShapeDtypeStruct((sub, 3 * width), jnp.bfloat16)
    return pl.pallas_call(
        functools.partial(project_kernel, len(given), keeps),
        out_shape=[kept if keeps and k == 0 else sent for k in range(len(pieces))],
        in_specs=[VMEM] * (len(given) + 2),
        out_specs=[VMEM] * len(pieces),
        compiler_params=params(),
        cost_estimate=pl.CostEstimate(
            flops=4 * len(pieces) * sub * key_matrix.size, bytes_accessed=4 * key_matrix.size, transcendentals=0
        ),
        name="project",
    )(*given, key_matrix, value_matrix)


def total_kernel(count, heads_of, *refs):
    (own, *parts), outs = refs[:count], refs[count:]
    width, rows = own.shape[1] // 2, own.shape[0]
    k = 0
    for out in outs:
        shares = []
        for _ in range(out.shape[0] // rows):
            first = pl.multiple_of(heads_of[k] * HEAD_WIDTH, HEAD_WIDTH)

            def columns(ref, third):
                return ref[:, pl.ds(third * width + first, HEAD_WIDTH)].astype(jnp.float32)

            key, value = columns(own, 0), columns(own, 1)
            for part in parts:
                key = key + (columns(part, 0) + columns(part, 1))
                value = value + columns(part, 2)
            shares.append((key, value))
            k += 1
        for half in range(2):
            stacked = jnp.concatenate([share[half] for share in shares], axis=0)
            out[:, half * HEAD_WIDTH : (half + 1) * HEAD_WIDTH] = stacked.astype(out.dtype)


def total(parts, heads_of, receivers):
    rows = parts[0].shape[0]
    sizes = [rows, rows] + [2 * rows] * (receivers // 2 - 1)
    return pl.pallas_call(
        lambda heads_ref, *refs: total_kernel(len(parts), heads_ref, *refs),
        out_shape=[jax.ShapeDtypeStruct((size, 2 * HEAD_WIDTH), jnp.bfloat16) for size in sizes],
        in_specs=[SMEM] + [VMEM] * len(parts),
        out_specs=[VMEM] * len(sizes),
        compiler_params=params(),
        name="total",
    )(heads_of, *parts)


def stack_kernel(count, *refs):
    blocks, (keys, values) = refs[:count], refs[count:]
    tokens = blocks[0].shape[0]
    for b, block in enumerate(blocks):
        keys[b * tokens : (b + 1) * tokens, :] = block[:, :HEAD_WIDTH]
        values[b * tokens : (b + 1) * tokens, :] = block[:, HEAD_WIDTH:]


def attend_kernel(count, offsets, head_index, queries, query_pos, key_pos, *refs):
    if count:
        outs, (keys, values) = refs[count:-2], refs[-2:]
        stack_kernel(count, *refs[:count], keys, values)
    else:
        (keys, values), outs = refs[:2], refs[2:]
    sub = outs[0].shape[0] // len(offsets[0])
    per_device = queries.shape[1] // HEAD_WIDTH
    length = keys.shape[0]
    factor = math.log2(math.e) / math.sqrt(HEAD_WIDTH)
    for k, at, out in [(k, at, out) for ks, out in zip(offsets, outs) for at, k in enumerate(ks)]:
        first = pl.multiple_of((head_index[0] ^ k) * sub, sub)
        rows = queries[pl.ds(first, sub), :]
        stacked = jnp.concatenate([rows[:, i * HEAD_WIDTH : (i + 1) * HEAD_WIDTH] for i in range(per_device)], axis=0)
        scores = lax.dot_general(stacked, keys[...], (((1,), (1,)), ((), ())), preferred_element_type=jnp.float32)
        allowed = key_pos[...] <= query_pos[pl.ds(first, sub), :]
        scores = jnp.where(allowed[None], scores.reshape(per_device, sub, length), -1e30)
        largest = jnp.max(scores, axis=2, keepdims=True)
        unnormed = jnp.exp2((scores - largest) * factor)
        totals = jnp.sum(unnormed, axis=2, keepdims=True)
        weights = unnormed.astype(jnp.bfloat16).reshape(per_device * sub, length)
        mixed = jnp.dot(weights, values[...], preferred_element_type=jnp.float32)
        mixed = mixed.reshape(per_device, sub, HEAD_WIDTH) / totals
        for i in range(per_device):
            out[at * sub : (at + 1) * sub, i * HEAD_WIDTH : (i + 1) * HEAD_WIDTH] = mixed[i].astype(out.dtype)


def attend(offsets, receivers, head_index, queries, query_pos, key_pos, blocks, stacked=()):
    tokens, width = queries.shape
    sub = tokens // receivers
    length = key_pos.shape[1]
    count = 0 if stacked else len(blocks)
    given = stacked or blocks
    pieces = [jax.ShapeDtypeStruct((len(group) * sub, width), jnp.bfloat16) for group in offsets]
    held = [] if stacked else [jax.ShapeDtypeStruct((length, HEAD_WIDTH), jnp.bfloat16)] * 2
    rows = sub * sum(len(group) for group in offsets)
    work = rows * length * width
    return pl.pallas_call(
        functools.partial(attend_kernel, count, offsets),
        out_shape=pieces + held,
        in_specs=[SMEM] + [VMEM] * (3 + len(given)),
        out_specs=[VMEM] * (len(offsets) + len(held)),
        compiler_params=params(),
        cost_estimate=pl.CostEstimate(
            flops=16 * work, bytes_accessed=4 * length * HEAD_WIDTH, transcendentals=work // HEAD_WIDTH
        ),
        name="attend",
    )(head_index, queries, query_pos, key_pos, *given)


def join_kernel(firsts, head_index, *refs):
    pieces, (out, sems) = refs[: len(firsts)], refs[len(firsts) :]
    rows, width = out.shape[2], out.shape[3] // len(firsts)
    copies(
        [
            (
                piece.at[pl.ds(first, rows), :],
                out.at[0, 0, :, pl.ds(pl.multiple_of((head_index[0] ^ k) * width, width), width)],
            )
            for k, (piece, first) in enumerate(zip(pieces, firsts))
        ],
        sems,
    )


def join(head_index, rows, pieces):
    width = pieces[0][0].shape[1]
    return pl.pallas_call(
        functools.partial(join_kernel, [first for _, first in pieces]),
        out_shape=jax.ShapeDtypeStruct((1, 1, rows, width * len(pieces)), jnp.bfloat16),
        in_specs=[SMEM] + [VMEM] * len(pieces),
        out_specs=HBM,
        scratch_shapes=[pltpu.SemaphoreType.DMA((len(pieces),))],
        compiler_params=params(),
        name="join",
    )(head_index, *[array for array, _ in pieces])


def body(activations, key_matrix, value_matrix, queries, block_order):
    heads, inner, outer = (lax.axis_size(name) for name in ("head", "inner", "outer"))
    head, z, x = (lax.axis_index(name) for name in ("head", "inner", "outer"))
    tokens = activations.shape[0]
    sub = tokens // heads
    depth = key_matrix.shape[0]
    sharing = heads // KEY_VALUE_HEADS
    head_index = jnp.reshape(head, (1,))

    pieces = [
        lax.dynamic_slice(activations, (head * sub, (z ^ k) * depth), (sub, depth)) for k in range(inner)
    ]
    pieces[0], matrices = lax.optimization_barrier((pieces[0], (key_matrix, value_matrix)))
    matrices = load(*matrices)
    arrived = swap_all(pieces, "inner")
    half = max(inner // 2, 1)
    partial = project(arrived[:half], *matrices, True)
    if inner > 1:
        _, far = lax.optimization_barrier((partial, arrived[half:]))
        partial = [*partial, *project(far, *matrices, False)]
    heads_of = (head ^ jnp.arange(heads, dtype=jnp.int32)) // sharing
    parts = swap_all(partial, "inner")
    shares = total(parts, heads_of, heads)
    got = swap_pairs(shares[1], shares[2:], "head")
    own = jnp.concatenate([shares[0]] + [array[first : first + sub] for array, first in got], axis=0)

    nearby = swap_all([own] * inner, "inner")
    blocks, cycle = [], []
    for j in range(outer):
        for k in range(inner):
            blocks.append(nearby[k] if j == 0 else swap(nearby[k], "outer", j))
            cycle.append((z ^ k) * outer + (x ^ j))

    block_size = tokens // 2
    row = jnp.arange(tokens, dtype=jnp.int32)
    order = block_order.reshape(-1, 2)

    def positions(shard):
        return (lax.dynamic_index_in_dim(order, shard, 0, False)[:, None] * block_size + row[None, :block_size]).reshape(
            tokens
        )

    query_pos = positions(z * outer + x)
    shards = jnp.stack(cycle)
    rows_of = ((head ^ jnp.arange(heads, dtype=jnp.int32))[:, None] * sub + row[None, :sub]).reshape(tokens)
    one_hot = shards[:, None] == jnp.arange(order.shape[0], dtype=jnp.int32)[None, :]
    firsts = jnp.sum(jnp.where(one_hot[:, :, None], order[None], 0), axis=1)
    block_of = jnp.where(rows_of[None, :] < block_size, firsts[:, :1], firsts[:, 1:])
    key_pos = (block_of * block_size + rows_of[None, :] % block_size).reshape(1, -1)

    place = head_index, queries, query_pos[:, None], key_pos, blocks
    *far_rows, keys, values = attend([(2 * f, 2 * f + 1) for f in range(1, heads // 2)], heads, *place)
    own_rows, near_rows = attend([(0,), (1,)], heads, *place, stacked=(keys, values))
    return join(head_index, sub, [(own_rows, 0), *swap_pairs(near_rows, far_rows, "head", after=own_rows)])


def solution(mesh):
    placed = (
        P(("inner", "outer"), None),
        P("inner", None),
        P("inner", None),
        P(("inner", "outer"), "head"),
        P(),
    )
    return jax.shard_map(
        body,
        mesh=mesh,
        in_specs=placed,
        out_specs=P(("inner", "outer"), "head", None, None),
        check_vma=False,
    )
```

```python
import functools
import math

import jax
import jax.numpy as jnp
from jax import lax
from jax.experimental import pallas as pl
from jax.experimental.pallas import tpu as pltpu
from jax.sharding import PartitionSpec as P

QUERY_HEADS = 32
KEY_VALUE_HEADS = 4
HEAD_WIDTH = 128
VMEM = pl.BlockSpec(memory_space=pltpu.VMEM)
SMEM = pl.BlockSpec(memory_space=pltpu.SMEM)
HBM = pl.BlockSpec(memory_space=pltpu.HBM)
LIMIT = 16 * 1024 * 1024
LOAD_LIMIT = 48 * 1024 * 1024


def params(limit=LIMIT):
    return pltpu.CompilerParams(vmem_limit_bytes=limit)


def swap(piece, axis, offset):
    return lax.ppermute(piece, axis, [(i, i ^ offset) for i in range(lax.axis_size(axis))])


def swap_all(pieces, axis):
    got = {k: swap(pieces[k], axis, k) for k in reversed(range(1, len(pieces)))}
    return [pieces[0]] + [got[k] for k in range(1, len(pieces))]


def copies(pairs, sems):
    started = [pltpu.make_async_copy(source, target, sems.at[i]) for i, (source, target) in enumerate(pairs)]
    for copy in started:
        copy.start()
    for copy in started:
        copy.wait()


def load_kernel(*refs):
    half = len(refs) // 2
    copies(list(zip(refs[:half], refs[half : 2 * half])), refs[-1])


def load(*arrays):
    return pl.pallas_call(
        load_kernel,
        out_shape=[jax.ShapeDtypeStruct(a.shape, a.dtype) for a in arrays],
        in_specs=[HBM] * len(arrays),
        out_specs=[VMEM] * len(arrays),
        scratch_shapes=[pltpu.SemaphoreType.DMA((len(arrays),))],
        compiler_params=params(LOAD_LIMIT),
        cost_estimate=pl.CostEstimate(flops=0, bytes_accessed=2 * sum(a.size * 2 for a in arrays), transcendentals=0),
        name="load",
    )(*arrays)


def project_kernel(count, keeps, *refs):
    pieces, (key_matrix, value_matrix), outs = refs[:count], refs[count : count + 2], refs[count + 2 :]
    rows = pieces[0][...] if count == 1 else jnp.concatenate([piece[...] for piece in pieces], axis=0)
    width = key_matrix.shape[1]
    sub = outs[0].shape[0]
    keys = jnp.dot(rows, key_matrix[...], preferred_element_type=jnp.float32)
    values = jnp.dot(rows, value_matrix[...], preferred_element_type=jnp.float32)
    for k, out in enumerate(outs):
        key, value = keys[k * sub : (k + 1) * sub], values[k * sub : (k + 1) * sub]
        if keeps and k == 0:
            out[:, :width], out[:, width:] = key, value
        else:
            high = key.astype(out.dtype)
            out[:, :width], out[:, width : 2 * width] = high, (key - high.astype(jnp.float32)).astype(out.dtype)
            out[:, 2 * width :] = value.astype(out.dtype)


def project(pieces, key_matrix, value_matrix, keeps):
    sub, width = pieces[0].shape[0], key_matrix.shape[1]
    given = pieces if sub % 16 == 0 else [jnp.concatenate(pieces, axis=0)]
    kept = jax.ShapeDtypeStruct((sub, 2 * width), jnp.float32)
    sent = jax.ShapeDtypeStruct((sub, 3 * width), jnp.bfloat16)
    return pl.pallas_call(
        functools.partial(project_kernel, len(given), keeps),
        out_shape=[kept if keeps and k == 0 else sent for k in range(len(pieces))],
        in_specs=[VMEM] * (len(given) + 2),
        out_specs=[VMEM] * len(pieces),
        compiler_params=params(),
        cost_estimate=pl.CostEstimate(
            flops=4 * len(pieces) * sub * key_matrix.size, bytes_accessed=4 * key_matrix.size, transcendentals=0
        ),
        name="project",
    )(*given, key_matrix, value_matrix)


def total_kernel(count, heads_of, *refs):
    (own, *parts), outs = refs[:count], refs[count:]
    width = own.shape[1] // 2
    for k, out in enumerate(outs):
        first = pl.multiple_of(heads_of[k] * HEAD_WIDTH, HEAD_WIDTH)

        def columns(ref, third):
            return ref[:, pl.ds(third * width + first, HEAD_WIDTH)].astype(jnp.float32)

        key, value = columns(own, 0), columns(own, 1)
        for part in parts:
            key = key + (columns(part, 0) + columns(part, 1))
            value = value + columns(part, 2)
        out[:, :HEAD_WIDTH], out[:, HEAD_WIDTH:] = key.astype(out.dtype), value.astype(out.dtype)


def total(parts, heads_of, receivers):
    rows = parts[0].shape[0]
    return pl.pallas_call(
        lambda heads_ref, *refs: total_kernel(len(parts), heads_ref, *refs),
        out_shape=[jax.ShapeDtypeStruct((rows, 2 * HEAD_WIDTH), jnp.bfloat16)] * receivers,
        in_specs=[SMEM] + [VMEM] * len(parts),
        out_specs=[VMEM] * receivers,
        compiler_params=params(),
        name="total",
    )(heads_of, *parts)


def stack_kernel(count, *refs):
    blocks, (keys, values) = refs[:count], refs[count:]
    tokens = blocks[0].shape[0]
    for b, block in enumerate(blocks):
        keys[b * tokens : (b + 1) * tokens, :] = block[:, :HEAD_WIDTH]
        values[b * tokens : (b + 1) * tokens, :] = block[:, HEAD_WIDTH:]


def attend_kernel(count, offsets, head_index, queries, query_pos, key_pos, *refs):
    if count:
        outs, (keys, values) = refs[count:-2], refs[-2:]
        stack_kernel(count, *refs[:count], keys, values)
    else:
        (keys, values), outs = refs[:2], refs[2:]
    sub = outs[0].shape[0]
    per_device = queries.shape[1] // HEAD_WIDTH
    length = keys.shape[0]
    factor = math.log2(math.e) / math.sqrt(HEAD_WIDTH)
    for k, out in zip(offsets, outs):
        first = pl.multiple_of((head_index[0] ^ k) * sub, sub)
        rows = queries[pl.ds(first, sub), :]
        stacked = jnp.concatenate([rows[:, i * HEAD_WIDTH : (i + 1) * HEAD_WIDTH] for i in range(per_device)], axis=0)
        scores = lax.dot_general(stacked, keys[...], (((1,), (1,)), ((), ())), preferred_element_type=jnp.float32)
        allowed = key_pos[...] <= query_pos[pl.ds(first, sub), :]
        scores = jnp.where(allowed[None], scores.reshape(per_device, sub, length), -1e30)
        largest = jnp.max(scores, axis=2, keepdims=True)
        unnormed = jnp.exp2((scores - largest) * factor)
        totals = jnp.sum(unnormed, axis=2, keepdims=True)
        weights = unnormed.astype(jnp.bfloat16).reshape(per_device * sub, length)
        mixed = jnp.dot(weights, values[...], preferred_element_type=jnp.float32)
        mixed = mixed.reshape(per_device, sub, HEAD_WIDTH) / totals
        for i in range(per_device):
            out[:, i * HEAD_WIDTH : (i + 1) * HEAD_WIDTH] = mixed[i].astype(out.dtype)


def attend(offsets, receivers, head_index, queries, query_pos, key_pos, blocks, stacked=()):
    tokens, width = queries.shape
    length = key_pos.shape[1]
    count = 0 if stacked else len(blocks)
    given = stacked or blocks
    piece = jax.ShapeDtypeStruct((tokens // receivers, width), jnp.bfloat16)
    held = [] if stacked else [jax.ShapeDtypeStruct((length, HEAD_WIDTH), jnp.bfloat16)] * 2
    rows = tokens * len(offsets) // receivers
    work = rows * length * width
    return pl.pallas_call(
        functools.partial(attend_kernel, count, offsets),
        out_shape=[piece] * len(offsets) + held,
        in_specs=[SMEM] + [VMEM] * (3 + len(given)),
        out_specs=[VMEM] * (len(offsets) + len(held)),
        compiler_params=params(),
        cost_estimate=pl.CostEstimate(
            flops=16 * work, bytes_accessed=4 * length * HEAD_WIDTH, transcendentals=work // HEAD_WIDTH
        ),
        name="attend",
    )(head_index, queries, query_pos, key_pos, *given)


def join_kernel(count, head_index, *refs):
    pieces, (out, sems) = refs[:count], refs[count:]
    width = pieces[0].shape[1]
    copies(
        [
            (piece, out.at[0, 0, :, pl.ds(pl.multiple_of((head_index[0] ^ k) * width, width), width)])
            for k, piece in enumerate(pieces)
        ],
        sems,
    )


def join(head_index, pieces):
    rows, width = pieces[0].shape
    return pl.pallas_call(
        functools.partial(join_kernel, len(pieces)),
        out_shape=jax.ShapeDtypeStruct((1, 1, rows, width * len(pieces)), jnp.bfloat16),
        in_specs=[SMEM] + [VMEM] * len(pieces),
        out_specs=HBM,
        scratch_shapes=[pltpu.SemaphoreType.DMA((len(pieces),))],
        compiler_params=params(),
        name="join",
    )(head_index, *pieces)


def body(activations, key_matrix, value_matrix, queries, block_order):
    heads, inner, outer = (lax.axis_size(name) for name in ("head", "inner", "outer"))
    head, z, x = (lax.axis_index(name) for name in ("head", "inner", "outer"))
    tokens = activations.shape[0]
    sub = tokens // heads
    depth = key_matrix.shape[0]
    sharing = heads // KEY_VALUE_HEADS
    head_index = jnp.reshape(head, (1,))

    pieces = [
        lax.dynamic_slice(activations, (head * sub, (z ^ k) * depth), (sub, depth)) for k in range(inner)
    ]
    pieces[0], matrices = lax.optimization_barrier((pieces[0], (key_matrix, value_matrix)))
    matrices = load(*matrices)
    arrived = swap_all(pieces, "inner")
    bounds = sorted({0, inner // 2, inner * 3 // 4, inner})
    partial = []
    for first, last in zip(bounds, bounds[1:]):
        _, rows = lax.optimization_barrier((partial, arrived[first:last]))
        partial = partial + list(project(rows, *matrices, first == 0))
    heads_of = (head ^ jnp.arange(heads, dtype=jnp.int32)) // sharing
    parts = swap_all(partial, "inner")
    shares = total(parts, heads_of, heads)
    own = jnp.concatenate(swap_all(shares, "head"), axis=0)

    nearby = swap_all([own] * inner, "inner")
    blocks, cycle = [], []
    for j in range(outer):
        for k in range(inner):
            blocks.append(nearby[k] if j == 0 else swap(nearby[k], "outer", j))
            cycle.append((z ^ k) * outer + (x ^ j))

    block_size = tokens // 2
    row = jnp.arange(tokens, dtype=jnp.int32)
    order = block_order.reshape(-1, 2)

    def positions(shard):
        return (lax.dynamic_index_in_dim(order, shard, 0, False)[:, None] * block_size + row[None, :block_size]).reshape(
            tokens
        )

    query_pos = positions(z * outer + x)
    shards = jnp.stack(cycle)
    rows_of = ((head ^ jnp.arange(heads, dtype=jnp.int32))[:, None] * sub + row[None, :sub]).reshape(tokens)
    one_hot = shards[:, None] == jnp.arange(order.shape[0], dtype=jnp.int32)[None, :]
    firsts = jnp.sum(jnp.where(one_hot[:, :, None], order[None], 0), axis=1)
    block_of = jnp.where(rows_of[None, :] < block_size, firsts[:, :1], firsts[:, 1:])
    key_pos = (block_of * block_size + rows_of[None, :] % block_size).reshape(1, -1)

    place = head_index, queries, query_pos[:, None], key_pos, blocks
    *leaving, keys, values = attend(range(1, heads), heads, *place)
    own_rows = attend(range(1), heads, *place, stacked=(keys, values))
    return join(head_index, swap_all([*own_rows, *leaving], "head"))


def solution(mesh):
    placed = (
        P(("inner", "outer"), None),
        P("inner", None),
        P("inner", None),
        P(("inner", "outer"), "head"),
        P(),
    )
    return jax.shard_map(
        body,
        mesh=mesh,
        in_specs=placed,
        out_specs=P(("inner", "outer"), "head", None, None),
        check_vma=False,
    )
```

```python
import functools
import math

import jax
import jax.numpy as jnp
from jax import lax
from jax.experimental import pallas as pl
from jax.experimental.pallas import tpu as pltpu
from jax.sharding import PartitionSpec as P

QUERY_HEADS = 32
KEY_VALUE_HEADS = 4
HEAD_WIDTH = 128
VMEM = pl.BlockSpec(memory_space=pltpu.VMEM)
SMEM = pl.BlockSpec(memory_space=pltpu.SMEM)
HBM = pl.BlockSpec(memory_space=pltpu.HBM)
LIMIT = 16 * 1024 * 1024
LOAD_LIMIT = 48 * 1024 * 1024


def params(limit=LIMIT):
    return pltpu.CompilerParams(vmem_limit_bytes=limit)


def swap(piece, axis, offset):
    return lax.ppermute(piece, axis, [(i, i ^ offset) for i in range(lax.axis_size(axis))])


def swap_both(piece, axis, offset, other_axis, other):
    sizes = lax.axis_size(axis), lax.axis_size(other_axis)
    order = [(i * sizes[1] + j, (i ^ offset) * sizes[1] + (j ^ other)) for i in range(sizes[0]) for j in range(sizes[1])]
    return lax.ppermute(piece, (axis, other_axis), order)


def swap_all(pieces, axis, unit=1):
    got = {k: swap(pieces[k], axis, k * unit) for k in reversed(range(1, len(pieces)))}
    return [pieces[0]] + [got[k] for k in range(1, len(pieces))]


def copies(pairs, sems):
    started = [pltpu.make_async_copy(source, target, sems.at[i]) for i, (source, target) in enumerate(pairs)]
    for copy in started:
        copy.start()
    for copy in started:
        copy.wait()


def load_kernel(heads_of, key_matrix, value_matrix, *refs):
    outs, sems = refs[:2], refs[2]
    pairs = []
    for j in range(heads_of.shape[0]):
        columns = pl.ds(pl.multiple_of(heads_of[j] * HEAD_WIDTH, HEAD_WIDTH), HEAD_WIDTH)
        for source, out in zip((key_matrix, value_matrix), outs):
            pairs.append((source.at[:, columns], out.at[:, pl.ds(j * HEAD_WIDTH, HEAD_WIDTH)]))
    copies(pairs, sems)


def load(heads_of, *matrices):
    depth, receivers = matrices[0].shape[0], heads_of.shape[0]
    loaded = jax.ShapeDtypeStruct((depth, receivers * HEAD_WIDTH), jnp.bfloat16)
    return pl.pallas_call(
        load_kernel,
        out_shape=[loaded] * 2,
        in_specs=[SMEM, HBM, HBM],
        out_specs=[VMEM] * 2,
        scratch_shapes=[pltpu.SemaphoreType.DMA((2 * receivers,))],
        compiler_params=params(LOAD_LIMIT),
        cost_estimate=pl.CostEstimate(flops=0, bytes_accessed=8 * loaded.size, transcendentals=0),
        name="load",
    )(heads_of, *matrices)


def encode(out, key, value):
    width = key.shape[1]
    high = key.astype(out.dtype)
    out[:, :width], out[:, width : 2 * width] = high, (key - high.astype(jnp.float32)).astype(out.dtype)
    out[:, 2 * width :] = value.astype(out.dtype)


def decode(part):
    width = part.shape[1] // 3
    high, low, value = (part[:, i * width : (i + 1) * width].astype(jnp.float32) for i in range(3))
    return high + low, value


def project_kernel(count, keeps, splits, *refs):
    pieces, (key_matrix, value_matrix), outs = refs[:count], refs[count : count + 2], refs[count + 2 :]
    rows = pieces[0][...] if count == 1 else jnp.concatenate([piece[...] for piece in pieces], axis=0)
    width = key_matrix.shape[1]
    sub = outs[0].shape[0]
    keys = jnp.dot(rows, key_matrix[...], preferred_element_type=jnp.float32)
    values = jnp.dot(rows, value_matrix[...], preferred_element_type=jnp.float32)
    each = 2 * HEAD_WIDTH if splits else width
    for i, out in enumerate(outs):
        k, f = divmod(i, width // each)
        at = slice(k * sub, (k + 1) * sub), slice(f * each, (f + 1) * each)
        if keeps and k == 0:
            out[:, :width], out[:, width:] = keys[at], values[at]
        else:
            encode(out, keys[at], values[at])


def project(pieces, key_matrix, value_matrix, keeps, splits):
    sub, width = pieces[0].shape[0], key_matrix.shape[1]
    given = pieces if sub % 16 == 0 else [jnp.concatenate(pieces, axis=0)]
    each = 2 * HEAD_WIDTH if splits else width
    kept = jax.ShapeDtypeStruct((sub, 2 * width), jnp.float32)
    sent = jax.ShapeDtypeStruct((sub, 3 * each), jnp.bfloat16)
    shapes = [kept if keeps and i == 0 else sent for i in range(len(pieces) * width // each)]
    outs = pl.pallas_call(
        functools.partial(project_kernel, len(given), keeps, splits),
        out_shape=shapes,
        in_specs=[VMEM] * (len(given) + 2),
        out_specs=[VMEM] * len(shapes),
        compiler_params=params(),
        cost_estimate=pl.CostEstimate(
            flops=4 * len(pieces) * sub * key_matrix.size, bytes_accessed=4 * key_matrix.size, transcendentals=0
        ),
        name="project",
    )(*given, key_matrix, value_matrix)
    pairs = width // each
    return [outs[i : i + pairs] for i in range(0, len(outs), pairs)] if splits else list(outs)


def gather_kernel(count, own, *refs):
    parts, outs = refs[:count], refs[count:]
    width = own.shape[1] // 2
    key, value = own[:, :width], own[:, width:]
    for part in parts:
        more = decode(part)
        key, value = key + more[0], value + more[1]
    each = outs[0].shape[1] // 2
    for f, out in enumerate(outs):
        out[:, :each], out[:, each:] = key[:, f * each : (f + 1) * each], value[:, f * each : (f + 1) * each]


def gather(own, parts):
    rows, width = own.shape
    pairs = width // (4 * HEAD_WIDTH)
    return pl.pallas_call(
        functools.partial(gather_kernel, len(parts)),
        out_shape=[jax.ShapeDtypeStruct((rows, 4 * HEAD_WIDTH), jnp.float32)] * pairs,
        in_specs=[VMEM] * (1 + len(parts)),
        out_specs=[VMEM] * pairs,
        compiler_params=params(),
        name="gather",
    )(own, *parts)


def total_kernel(pairs, *refs):
    sums, parts, outs = refs[:pairs], refs[pairs:-2], refs[-2:]
    count = len(parts) // pairs
    shares = []
    for f, share in enumerate(sums):
        width = share.shape[1] // 2
        key, value = share[:, :width], share[:, width:]
        for part in parts[f * count : (f + 1) * count]:
            more = decode(part)
            key, value = key + more[0], value + more[1]
        shares.append((key, value))
    for i, out in enumerate(outs):
        for half in range(2):
            columns = [share[half][:, i * HEAD_WIDTH : (i + 1) * HEAD_WIDTH] for share in shares]
            whole = jnp.concatenate(columns, axis=0)
            out[:, half * HEAD_WIDTH : (half + 1) * HEAD_WIDTH] = whole.astype(out.dtype)


def total(sums, parts):
    given = [*sums, *(part for row in parts for part in row)]
    share = jax.ShapeDtypeStruct((sums[0].shape[0] * len(sums), 2 * HEAD_WIDTH), jnp.bfloat16)
    return pl.pallas_call(
        functools.partial(total_kernel, len(sums)),
        out_shape=[share] * 2,
        in_specs=[VMEM] * len(given),
        out_specs=[VMEM] * 2,
        compiler_params=params(),
        name="total",
    )(*given)


def stack_kernel(count, *refs):
    blocks, (keys, values) = refs[:count], refs[count:]
    tokens = blocks[0].shape[0]
    for b, block in enumerate(blocks):
        keys[b * tokens : (b + 1) * tokens, :] = block[:, :HEAD_WIDTH]
        values[b * tokens : (b + 1) * tokens, :] = block[:, HEAD_WIDTH:]


def attend_kernel(count, offsets, head_index, queries, query_pos, key_pos, *refs):
    if count:
        outs, (keys, values) = refs[count:-2], refs[-2:]
        stack_kernel(count, *refs[:count], keys, values)
    else:
        (keys, values), outs = refs[:2], refs[2:]
    sub = outs[0].shape[0]
    per_device = queries.shape[1] // HEAD_WIDTH
    length = keys.shape[0]
    factor = math.log2(math.e) / math.sqrt(HEAD_WIDTH)
    for k, out in zip(offsets, outs):
        first = pl.multiple_of((head_index[0] ^ k) * sub, sub)
        rows = queries[pl.ds(first, sub), :]
        stacked = jnp.concatenate([rows[:, i * HEAD_WIDTH : (i + 1) * HEAD_WIDTH] for i in range(per_device)], axis=0)
        scores = lax.dot_general(stacked, keys[...], (((1,), (1,)), ((), ())), preferred_element_type=jnp.float32)
        allowed = key_pos[...] <= query_pos[pl.ds(first, sub), :]
        scores = jnp.where(allowed[None], scores.reshape(per_device, sub, length), -1e30)
        largest = jnp.max(scores, axis=2, keepdims=True)
        unnormed = jnp.exp2((scores - largest) * factor)
        totals = jnp.sum(unnormed, axis=2, keepdims=True)
        weights = unnormed.astype(jnp.bfloat16).reshape(per_device * sub, length)
        mixed = jnp.dot(weights, values[...], preferred_element_type=jnp.float32)
        mixed = mixed.reshape(per_device, sub, HEAD_WIDTH) / totals
        for i in range(per_device):
            out[:, i * HEAD_WIDTH : (i + 1) * HEAD_WIDTH] = mixed[i].astype(out.dtype)


def attend(offsets, receivers, head_index, queries, query_pos, key_pos, blocks, stacked=()):
    tokens, width = queries.shape
    length = key_pos.shape[1]
    count = 0 if stacked else len(blocks)
    given = stacked or blocks
    piece = jax.ShapeDtypeStruct((tokens // receivers, width), jnp.bfloat16)
    held = [] if stacked else [jax.ShapeDtypeStruct((length, HEAD_WIDTH), jnp.bfloat16)] * 2
    rows = tokens * len(offsets) // receivers
    work = rows * length * width
    return pl.pallas_call(
        functools.partial(attend_kernel, count, offsets),
        out_shape=[piece] * len(offsets) + held,
        in_specs=[SMEM] + [VMEM] * (3 + len(given)),
        out_specs=[VMEM] * (len(offsets) + len(held)),
        compiler_params=params(),
        cost_estimate=pl.CostEstimate(
            flops=16 * work, bytes_accessed=4 * length * HEAD_WIDTH, transcendentals=work // HEAD_WIDTH
        ),
        name="attend",
    )(head_index, queries, query_pos, key_pos, *given)


def join_kernel(count, head_index, *refs):
    pieces, (out, sems) = refs[:count], refs[count:]
    width = pieces[0].shape[1]
    copies(
        [
            (piece, out.at[0, 0, :, pl.ds(pl.multiple_of((head_index[0] ^ k) * width, width), width)])
            for k, piece in enumerate(pieces)
        ],
        sems,
    )


def join(head_index, pieces):
    rows, width = pieces[0].shape
    return pl.pallas_call(
        functools.partial(join_kernel, len(pieces)),
        out_shape=jax.ShapeDtypeStruct((1, 1, rows, width * len(pieces)), jnp.bfloat16),
        in_specs=[SMEM] + [VMEM] * len(pieces),
        out_specs=HBM,
        scratch_shapes=[pltpu.SemaphoreType.DMA((len(pieces),))],
        compiler_params=params(),
        name="join",
    )(head_index, *pieces)


def body(activations, key_matrix, value_matrix, queries, block_order):
    heads, inner, outer = (lax.axis_size(name) for name in ("head", "inner", "outer"))
    head, z, x = (lax.axis_index(name) for name in ("head", "inner", "outer"))
    tokens = activations.shape[0]
    sub = tokens // heads
    depth = key_matrix.shape[0]
    sharing = heads // KEY_VALUE_HEADS
    head_index = jnp.reshape(head, (1,))

    pieces = [
        lax.dynamic_slice(activations, (head * sub, (z ^ k) * depth), (sub, depth)) for k in range(inner)
    ]
    heads_of = (head ^ jnp.arange(heads, dtype=jnp.int32)) // sharing
    pieces[0], matrices = lax.optimization_barrier((pieces[0], (key_matrix, value_matrix)))
    matrices = load(heads_of, *matrices)
    arrived = swap_all(pieces, "inner")

    bounds = sorted({0, inner // 2, inner * 3 // 4, inner})
    partial = []
    for first, last in zip(bounds, bounds[1:-1]):
        _, rows = lax.optimization_barrier((partial, arrived[first:last]))
        partial = partial + project(rows, *matrices, first == 0, False)
    _, rows = lax.optimization_barrier((partial, arrived[bounds[-2] :]))
    split = project(rows, *matrices, False, True)
    pairs = range(heads // 2)
    late = [[swap_both(split[k - bounds[-2]][f], "head", 2 * f, "inner", k) for k in range(bounds[-2], inner)] for f in pairs]
    early = swap_all(partial, "inner")
    sums = swap_all(gather(early[0], early[1:]), "head", 2)
    mine, others = total(sums, late)
    own = jnp.concatenate([mine, swap(others, "head", 1)], axis=0)

    nearby = swap_all([own] * inner, "inner")
    blocks, cycle = [], []
    for j in range(outer):
        for k in range(inner):
            blocks.append(nearby[k] if j == 0 else swap(nearby[k], "outer", j))
            cycle.append((z ^ k) * outer + (x ^ j))

    block_size = tokens // 2
    row = jnp.arange(tokens, dtype=jnp.int32)
    order = block_order.reshape(-1, 2)

    def positions(shard):
        return (lax.dynamic_index_in_dim(order, shard, 0, False)[:, None] * block_size + row[None, :block_size]).reshape(
            tokens
        )

    query_pos = positions(z * outer + x)
    shards = jnp.stack(cycle)
    distance = jnp.arange(heads, dtype=jnp.int32).reshape(heads // 2, 2).T.reshape(heads)
    rows_of = ((head ^ distance)[:, None] * sub + row[None, :sub]).reshape(tokens)
    one_hot = shards[:, None] == jnp.arange(order.shape[0], dtype=jnp.int32)[None, :]
    firsts = jnp.sum(jnp.where(one_hot[:, :, None], order[None], 0), axis=1)
    block_of = jnp.where(rows_of[None, :] < block_size, firsts[:, :1], firsts[:, 1:])
    key_pos = (block_of * block_size + rows_of[None, :] % block_size).reshape(1, -1)

    place = head_index, queries, query_pos[:, None], key_pos, blocks
    *leaving, keys, values = attend(range(1, heads), heads, *place)
    own_rows = attend(range(1), heads, *place, stacked=(keys, values))
    return join(head_index, swap_all([*own_rows, *leaving], "head"))


def solution(mesh):
    placed = (
        P(("inner", "outer"), None),
        P("inner", None),
        P("inner", None),
        P(("inner", "outer"), "head"),
        P(),
    )
    return jax.shard_map(
        body,
        mesh=mesh,
        in_specs=placed,
        out_specs=P(("inner", "outer"), "head", None, None),
        check_vma=False,
    )
```

```python
import functools
import math

import jax
import jax.numpy as jnp
from jax import lax
from jax.experimental import pallas as pl
from jax.experimental.pallas import tpu as pltpu
from jax.sharding import PartitionSpec as P

QUERY_HEADS = 32
KEY_VALUE_HEADS = 4
HEAD_WIDTH = 128
VMEM = pl.BlockSpec(memory_space=pltpu.VMEM)
SMEM = pl.BlockSpec(memory_space=pltpu.SMEM)
HBM = pl.BlockSpec(memory_space=pltpu.HBM)
LIMIT = 16 * 1024 * 1024
LOAD_LIMIT = 48 * 1024 * 1024


def params(limit=LIMIT):
    return pltpu.CompilerParams(vmem_limit_bytes=limit)


def swap(piece, axis, offset):
    return lax.ppermute(piece, axis, [(i, i ^ offset) for i in range(lax.axis_size(axis))])


def swap_both(piece, axis, offset, other_axis, other):
    sizes = lax.axis_size(axis), lax.axis_size(other_axis)
    order = [(i * sizes[1] + j, (i ^ offset) * sizes[1] + (j ^ other)) for i in range(sizes[0]) for j in range(sizes[1])]
    return lax.ppermute(piece, (axis, other_axis), order)


def swap_all(pieces, axis, unit=1):
    got = {k: swap(pieces[k], axis, k * unit) for k in reversed(range(1, len(pieces)))}
    return [pieces[0]] + [got[k] for k in range(1, len(pieces))]


def copies(pairs, sems):
    started = [pltpu.make_async_copy(source, target, sems.at[i]) for i, (source, target) in enumerate(pairs)]
    for copy in started:
        copy.start()
    for copy in started:
        copy.wait()


def load_kernel(heads_of, key_matrix, value_matrix, *refs):
    outs, sems = refs[:2], refs[2]
    pairs = []
    for j in range(heads_of.shape[0]):
        columns = pl.ds(pl.multiple_of(heads_of[j] * HEAD_WIDTH, HEAD_WIDTH), HEAD_WIDTH)
        for source, out in zip((key_matrix, value_matrix), outs):
            pairs.append((source.at[:, columns], out.at[:, pl.ds(j * HEAD_WIDTH, HEAD_WIDTH)]))
    copies(pairs, sems)


def load(heads_of, *matrices):
    depth, receivers = matrices[0].shape[0], heads_of.shape[0]
    loaded = jax.ShapeDtypeStruct((depth, receivers * HEAD_WIDTH), jnp.bfloat16)
    return pl.pallas_call(
        load_kernel,
        out_shape=[loaded] * 2,
        in_specs=[SMEM, HBM, HBM],
        out_specs=[VMEM] * 2,
        scratch_shapes=[pltpu.SemaphoreType.DMA((2 * receivers,))],
        compiler_params=params(LOAD_LIMIT),
        cost_estimate=pl.CostEstimate(flops=0, bytes_accessed=8 * loaded.size, transcendentals=0),
        name="load",
    )(heads_of, *matrices)


def encode(out, key, value):
    width = key.shape[1]
    high = key.astype(out.dtype)
    out[:, :width], out[:, width : 2 * width] = high, (key - high.astype(jnp.float32)).astype(out.dtype)
    out[:, 2 * width :] = value.astype(out.dtype)


def decode(part):
    width = part.shape[1] // 3
    high, low, value = (part[:, i * width : (i + 1) * width].astype(jnp.float32) for i in range(3))
    return high + low, value


def project_kernel(count, keeps, splits, *refs):
    pieces, (key_matrix, value_matrix), outs = refs[:count], refs[count : count + 2], refs[count + 2 :]
    rows = pieces[0][...] if count == 1 else jnp.concatenate([piece[...] for piece in pieces], axis=0)
    width = key_matrix.shape[1]
    sub = outs[0].shape[0]
    keys = jnp.dot(rows, key_matrix[...], preferred_element_type=jnp.float32)
    values = jnp.dot(rows, value_matrix[...], preferred_element_type=jnp.float32)
    each = 2 * HEAD_WIDTH if splits else width
    for i, out in enumerate(outs):
        k, f = divmod(i, width // each)
        at = slice(k * sub, (k + 1) * sub), slice(f * each, (f + 1) * each)
        if keeps and k == 0:
            out[:, :width], out[:, width:] = keys[at], values[at]
        else:
            encode(out, keys[at], values[at])


def project(pieces, key_matrix, value_matrix, keeps, splits):
    sub, width = pieces[0].shape[0], key_matrix.shape[1]
    given = pieces if sub % 16 == 0 else [jnp.concatenate(pieces, axis=0)]
    each = 2 * HEAD_WIDTH if splits else width
    kept = jax.ShapeDtypeStruct((sub, 2 * width), jnp.float32)
    sent = jax.ShapeDtypeStruct((sub, 3 * each), jnp.bfloat16)
    shapes = [kept if keeps and i == 0 else sent for i in range(len(pieces) * width // each)]
    outs = pl.pallas_call(
        functools.partial(project_kernel, len(given), keeps, splits),
        out_shape=shapes,
        in_specs=[VMEM] * (len(given) + 2),
        out_specs=[VMEM] * len(shapes),
        compiler_params=params(),
        cost_estimate=pl.CostEstimate(
            flops=4 * len(pieces) * sub * key_matrix.size, bytes_accessed=4 * key_matrix.size, transcendentals=0
        ),
        name="project",
    )(*given, key_matrix, value_matrix)
    pairs = width // each
    return [outs[i : i + pairs] for i in range(0, len(outs), pairs)] if splits else list(outs)


def gather_kernel(count, own, *refs):
    parts, outs = refs[:count], refs[count:]
    width = own.shape[1] // 2
    key, value = own[:, :width], own[:, width:]
    for part in parts:
        more = decode(part)
        key, value = key + more[0], value + more[1]
    each = outs[0].shape[1] // 2
    for f, out in enumerate(outs):
        at = slice(f * each, (f + 1) * each)
        if f == 0:
            out[:, :each], out[:, each:] = key[:, at], value[:, at]
        else:
            encode(out, key[:, at], value[:, at])


def gather(own, parts):
    rows, width = own.shape
    pairs = width // (4 * HEAD_WIDTH)
    return pl.pallas_call(
        functools.partial(gather_kernel, len(parts)),
        out_shape=[jax.ShapeDtypeStruct((rows, 4 * HEAD_WIDTH), jnp.float32)]
        + [jax.ShapeDtypeStruct((rows, 6 * HEAD_WIDTH), jnp.bfloat16)] * (pairs - 1),
        in_specs=[VMEM] * (1 + len(parts)),
        out_specs=[VMEM] * pairs,
        compiler_params=params(),
        name="gather",
    )(own, *parts)


def total_kernel(pairs, *refs):
    sums, parts, outs = refs[:pairs], refs[pairs:-2], refs[-2:]
    count = len(parts) // pairs
    shares = []
    for f, share in enumerate(sums):
        width = share.shape[1] // 2
        key, value = (share[:, :width], share[:, width:]) if f == 0 else decode(share)
        for part in parts[f * count : (f + 1) * count]:
            more = decode(part)
            key, value = key + more[0], value + more[1]
        shares.append((key, value))
    for i, out in enumerate(outs):
        for half in range(2):
            columns = [share[half][:, i * HEAD_WIDTH : (i + 1) * HEAD_WIDTH] for share in shares]
            whole = jnp.concatenate(columns, axis=0)
            out[:, half * HEAD_WIDTH : (half + 1) * HEAD_WIDTH] = whole.astype(out.dtype)


def total(sums, parts):
    given = [*sums, *(part for row in parts for part in row)]
    share = jax.ShapeDtypeStruct((sums[0].shape[0] * len(sums), 2 * HEAD_WIDTH), jnp.bfloat16)
    return pl.pallas_call(
        functools.partial(total_kernel, len(sums)),
        out_shape=[share] * 2,
        in_specs=[VMEM] * len(given),
        out_specs=[VMEM] * 2,
        compiler_params=params(),
        name="total",
    )(*given)


def stack_kernel(count, *refs):
    blocks, (keys, values) = refs[:count], refs[count:]
    tokens = blocks[0].shape[0]
    for b, block in enumerate(blocks):
        keys[b * tokens : (b + 1) * tokens, :] = block[:, :HEAD_WIDTH]
        values[b * tokens : (b + 1) * tokens, :] = block[:, HEAD_WIDTH:]


def attend_kernel(count, offsets, head_index, queries, query_pos, key_pos, *refs):
    if count:
        outs, (keys, values) = refs[count:-2], refs[-2:]
        stack_kernel(count, *refs[:count], keys, values)
    else:
        (keys, values), outs = refs[:2], refs[2:]
    sub = outs[0].shape[0]
    per_device = queries.shape[1] // HEAD_WIDTH
    length = keys.shape[0]
    factor = math.log2(math.e) / math.sqrt(HEAD_WIDTH)
    for k, out in zip(offsets, outs):
        first = pl.multiple_of((head_index[0] ^ k) * sub, sub)
        rows = queries[pl.ds(first, sub), :]
        stacked = jnp.concatenate([rows[:, i * HEAD_WIDTH : (i + 1) * HEAD_WIDTH] for i in range(per_device)], axis=0)
        scores = lax.dot_general(stacked, keys[...], (((1,), (1,)), ((), ())), preferred_element_type=jnp.float32)
        allowed = key_pos[...] <= query_pos[pl.ds(first, sub), :]
        scores = jnp.where(allowed[None], scores.reshape(per_device, sub, length), -1e30)
        largest = jnp.max(scores, axis=2, keepdims=True)
        unnormed = jnp.exp2((scores - largest) * factor)
        totals = jnp.sum(unnormed, axis=2, keepdims=True)
        weights = unnormed.astype(jnp.bfloat16).reshape(per_device * sub, length)
        mixed = jnp.dot(weights, values[...], preferred_element_type=jnp.float32)
        mixed = mixed.reshape(per_device, sub, HEAD_WIDTH) / totals
        for i in range(per_device):
            out[:, i * HEAD_WIDTH : (i + 1) * HEAD_WIDTH] = mixed[i].astype(out.dtype)


def attend(offsets, receivers, head_index, queries, query_pos, key_pos, blocks, stacked=()):
    tokens, width = queries.shape
    length = key_pos.shape[1]
    count = 0 if stacked else len(blocks)
    given = stacked or blocks
    piece = jax.ShapeDtypeStruct((tokens // receivers, width), jnp.bfloat16)
    held = [] if stacked else [jax.ShapeDtypeStruct((length, HEAD_WIDTH), jnp.bfloat16)] * 2
    rows = tokens * len(offsets) // receivers
    work = rows * length * width
    return pl.pallas_call(
        functools.partial(attend_kernel, count, offsets),
        out_shape=[piece] * len(offsets) + held,
        in_specs=[SMEM] + [VMEM] * (3 + len(given)),
        out_specs=[VMEM] * (len(offsets) + len(held)),
        compiler_params=params(),
        cost_estimate=pl.CostEstimate(
            flops=16 * work, bytes_accessed=4 * length * HEAD_WIDTH, transcendentals=work // HEAD_WIDTH
        ),
        name="attend",
    )(head_index, queries, query_pos, key_pos, *given)


def join_kernel(count, head_index, *refs):
    pieces, (out, sems) = refs[:count], refs[count:]
    width = pieces[0].shape[1]
    copies(
        [
            (piece, out.at[0, 0, :, pl.ds(pl.multiple_of((head_index[0] ^ k) * width, width), width)])
            for k, piece in enumerate(pieces)
        ],
        sems,
    )


def join(head_index, pieces):
    rows, width = pieces[0].shape
    return pl.pallas_call(
        functools.partial(join_kernel, len(pieces)),
        out_shape=jax.ShapeDtypeStruct((1, 1, rows, width * len(pieces)), jnp.bfloat16),
        in_specs=[SMEM] + [VMEM] * len(pieces),
        out_specs=HBM,
        scratch_shapes=[pltpu.SemaphoreType.DMA((len(pieces),))],
        compiler_params=params(),
        name="join",
    )(head_index, *pieces)


def body(activations, key_matrix, value_matrix, queries, block_order):
    heads, inner, outer = (lax.axis_size(name) for name in ("head", "inner", "outer"))
    head, z, x = (lax.axis_index(name) for name in ("head", "inner", "outer"))
    tokens = activations.shape[0]
    sub = tokens // heads
    depth = key_matrix.shape[0]
    sharing = heads // KEY_VALUE_HEADS
    head_index = jnp.reshape(head, (1,))

    pieces = [
        lax.dynamic_slice(activations, (head * sub, (z ^ k) * depth), (sub, depth)) for k in range(inner)
    ]
    heads_of = (head ^ jnp.arange(heads, dtype=jnp.int32)) // sharing
    pieces[0], matrices = lax.optimization_barrier((pieces[0], (key_matrix, value_matrix)))
    matrices = load(heads_of, *matrices)
    arrived = swap_all(pieces, "inner")

    bounds = sorted({0, inner // 2, inner * 3 // 4, inner})
    partial = []
    for first, last in zip(bounds, bounds[1:-1]):
        _, rows = lax.optimization_barrier((partial, arrived[first:last]))
        partial = partial + project(rows, *matrices, first == 0, False)
    _, rows = lax.optimization_barrier((partial, arrived[bounds[-2] :]))
    split = project(rows, *matrices, False, True)
    pairs = range(heads // 2)
    late = [[swap_both(split[k - bounds[-2]][f], "head", 2 * f, "inner", k) for k in range(bounds[-2], inner)] for f in pairs]
    early = swap_all(partial, "inner")
    sums = swap_all(gather(early[0], early[1:]), "head", 2)
    mine, others = total(sums, late)
    own = jnp.concatenate([mine, swap(others, "head", 1)], axis=0)

    nearby = swap_all([own] * inner, "inner")
    blocks, cycle = [], []
    for j in range(outer):
        for k in range(inner):
            if j == 0:
                blocks.append(nearby[k])
            elif k in (1, inner - 1):
                blocks.append(swap_both(own, "inner", k, "outer", j))
            else:
                blocks.append(swap(nearby[k], "outer", j))
            cycle.append((z ^ k) * outer + (x ^ j))

    block_size = tokens // 2
    row = jnp.arange(tokens, dtype=jnp.int32)
    order = block_order.reshape(-1, 2)

    def positions(shard):
        return (lax.dynamic_index_in_dim(order, shard, 0, False)[:, None] * block_size + row[None, :block_size]).reshape(
            tokens
        )

    query_pos = positions(z * outer + x)
    shards = jnp.stack(cycle)
    distance = jnp.arange(heads, dtype=jnp.int32).reshape(heads // 2, 2).T.reshape(heads)
    rows_of = ((head ^ distance)[:, None] * sub + row[None, :sub]).reshape(tokens)
    one_hot = shards[:, None] == jnp.arange(order.shape[0], dtype=jnp.int32)[None, :]
    firsts = jnp.sum(jnp.where(one_hot[:, :, None], order[None], 0), axis=1)
    block_of = jnp.where(rows_of[None, :] < block_size, firsts[:, :1], firsts[:, 1:])
    key_pos = (block_of * block_size + rows_of[None, :] % block_size).reshape(1, -1)

    place = head_index, queries, query_pos[:, None], key_pos, blocks
    *leaving, keys, values = attend(range(1, heads), heads, *place)
    own_rows = attend(range(1), heads, *place, stacked=(keys, values))
    return join(head_index, swap_all([*own_rows, *leaving], "head"))


def solution(mesh):
    placed = (
        P(("inner", "outer"), None),
        P("inner", None),
        P("inner", None),
        P(("inner", "outer"), "head"),
        P(),
    )
    return jax.shard_map(
        body,
        mesh=mesh,
        in_specs=placed,
        out_specs=P(("inner", "outer"), "head", None, None),
        check_vma=False,
    )
```

```python
import functools
import math

import jax
import jax.numpy as jnp
from jax import lax
from jax.experimental import pallas as pl
from jax.experimental.pallas import tpu as pltpu
from jax.sharding import PartitionSpec as P

QUERY_HEADS = 32
KEY_VALUE_HEADS = 4
HEAD_WIDTH = 128
VMEM = pl.BlockSpec(memory_space=pltpu.VMEM)
SMEM = pl.BlockSpec(memory_space=pltpu.SMEM)
HBM = pl.BlockSpec(memory_space=pltpu.HBM)
LIMIT = 16 * 1024 * 1024
LOAD_LIMIT = 48 * 1024 * 1024


def params(limit=LIMIT):
    return pltpu.CompilerParams(vmem_limit_bytes=limit)


def swap(piece, axis, offset):
    return lax.ppermute(piece, axis, [(i, i ^ offset) for i in range(lax.axis_size(axis))])


def swap_both(piece, axis, offset, other_axis, other):
    sizes = lax.axis_size(axis), lax.axis_size(other_axis)
    order = [(i * sizes[1] + j, (i ^ offset) * sizes[1] + (j ^ other)) for i in range(sizes[0]) for j in range(sizes[1])]
    return lax.ppermute(piece, (axis, other_axis), order)


def swap_all(pieces, axis, unit=1):
    got = {k: swap(pieces[k], axis, k * unit) for k in reversed(range(1, len(pieces)))}
    return [pieces[0]] + [got[k] for k in range(1, len(pieces))]


def copies(pairs, sems):
    started = [pltpu.make_async_copy(source, target, sems.at[i]) for i, (source, target) in enumerate(pairs)]
    for copy in started:
        copy.start()
    for copy in started:
        copy.wait()


def load_kernel(heads_of, key_matrix, value_matrix, *refs):
    outs, sems = refs[:2], refs[2]
    pairs = []
    for j in range(heads_of.shape[0]):
        columns = pl.ds(pl.multiple_of(heads_of[j] * HEAD_WIDTH, HEAD_WIDTH), HEAD_WIDTH)
        for source, out in zip((key_matrix, value_matrix), outs):
            pairs.append((source.at[:, columns], out.at[:, pl.ds(j * HEAD_WIDTH, HEAD_WIDTH)]))
    copies(pairs, sems)


def load(heads_of, *matrices):
    depth, receivers = matrices[0].shape[0], heads_of.shape[0]
    loaded = jax.ShapeDtypeStruct((depth, receivers * HEAD_WIDTH), jnp.bfloat16)
    return pl.pallas_call(
        load_kernel,
        out_shape=[loaded] * 2,
        in_specs=[SMEM, HBM, HBM],
        out_specs=[VMEM] * 2,
        scratch_shapes=[pltpu.SemaphoreType.DMA((2 * receivers,))],
        compiler_params=params(LOAD_LIMIT),
        cost_estimate=pl.CostEstimate(flops=0, bytes_accessed=8 * loaded.size, transcendentals=0),
        name="load",
    )(heads_of, *matrices)


def encode(out, key, value):
    width = key.shape[1]
    high = key.astype(out.dtype)
    out[:, :width], out[:, width : 2 * width] = high, (key - high.astype(jnp.float32)).astype(out.dtype)
    out[:, 2 * width :] = value.astype(out.dtype)


def decode(part):
    width = part.shape[1] // 3
    high, low, value = (part[:, i * width : (i + 1) * width].astype(jnp.float32) for i in range(3))
    return high + low, value


def project_kernel(count, keeps, splits, *refs):
    pieces, (key_matrix, value_matrix), outs = refs[:count], refs[count : count + 2], refs[count + 2 :]
    rows = pieces[0][...] if count == 1 else jnp.concatenate([piece[...] for piece in pieces], axis=0)
    width = key_matrix.shape[1]
    sub = outs[0].shape[0]
    keys = jnp.dot(rows, key_matrix[...], preferred_element_type=jnp.float32)
    values = jnp.dot(rows, value_matrix[...], preferred_element_type=jnp.float32)
    each = 2 * HEAD_WIDTH if splits else width
    for i, out in enumerate(outs):
        k, f = divmod(i, width // each)
        at = slice(k * sub, (k + 1) * sub), slice(f * each, (f + 1) * each)
        if keeps and k == 0:
            out[:, :width], out[:, width:] = keys[at], values[at]
        else:
            encode(out, keys[at], values[at])


def project(pieces, key_matrix, value_matrix, keeps, splits):
    sub, width = pieces[0].shape[0], key_matrix.shape[1]
    given = pieces if sub % 16 == 0 else [jnp.concatenate(pieces, axis=0)]
    each = 2 * HEAD_WIDTH if splits else width
    kept = jax.ShapeDtypeStruct((sub, 2 * width), jnp.float32)
    sent = jax.ShapeDtypeStruct((sub, 3 * each), jnp.bfloat16)
    shapes = [kept if keeps and i == 0 else sent for i in range(len(pieces) * width // each)]
    outs = pl.pallas_call(
        functools.partial(project_kernel, len(given), keeps, splits),
        out_shape=shapes,
        in_specs=[VMEM] * (len(given) + 2),
        out_specs=[VMEM] * len(shapes),
        compiler_params=params(),
        cost_estimate=pl.CostEstimate(
            flops=4 * len(pieces) * sub * key_matrix.size, bytes_accessed=4 * key_matrix.size, transcendentals=0
        ),
        name="project",
    )(*given, key_matrix, value_matrix)
    pairs = width // each
    return [outs[i : i + pairs] for i in range(0, len(outs), pairs)] if splits else list(outs)


def gather_kernel(count, own, *refs):
    parts, outs = refs[:count], refs[count:]
    width = own.shape[1] // 2
    key, value = own[:, :width], own[:, width:]
    for part in parts:
        more = decode(part)
        key, value = key + more[0], value + more[1]
    each = outs[0].shape[1] // 2
    for f, out in enumerate(outs):
        at = slice(f * each, (f + 1) * each)
        if f == 0:
            out[:, :each], out[:, each:] = key[:, at], value[:, at]
        else:
            encode(out, key[:, at], value[:, at])


def gather(own, parts):
    rows, width = own.shape
    pairs = width // (4 * HEAD_WIDTH)
    return pl.pallas_call(
        functools.partial(gather_kernel, len(parts)),
        out_shape=[jax.ShapeDtypeStruct((rows, 4 * HEAD_WIDTH), jnp.float32)]
        + [jax.ShapeDtypeStruct((rows, 6 * HEAD_WIDTH), jnp.bfloat16)] * (pairs - 1),
        in_specs=[VMEM] * (1 + len(parts)),
        out_specs=[VMEM] * pairs,
        compiler_params=params(),
        name="gather",
    )(own, *parts)


def total_kernel(pairs, *refs):
    sums, parts, outs = refs[:pairs], refs[pairs:-2], refs[-2:]
    count = len(parts) // pairs
    shares = []
    for f, share in enumerate(sums):
        width = share.shape[1] // 2
        key, value = (share[:, :width], share[:, width:]) if f == 0 else decode(share)
        for part in parts[f * count : (f + 1) * count]:
            more = decode(part)
            key, value = key + more[0], value + more[1]
        shares.append((key, value))
    for i, out in enumerate(outs):
        for half in range(2):
            columns = [share[half][:, i * HEAD_WIDTH : (i + 1) * HEAD_WIDTH] for share in shares]
            whole = jnp.concatenate(columns, axis=0)
            out[:, half * HEAD_WIDTH : (half + 1) * HEAD_WIDTH] = whole.astype(out.dtype)


def total(sums, parts):
    given = [*sums, *(part for row in parts for part in row)]
    share = jax.ShapeDtypeStruct((sums[0].shape[0] * len(sums), 2 * HEAD_WIDTH), jnp.bfloat16)
    return pl.pallas_call(
        functools.partial(total_kernel, len(sums)),
        out_shape=[share] * 2,
        in_specs=[VMEM] * len(given),
        out_specs=[VMEM] * 2,
        compiler_params=params(),
        name="total",
    )(*given)


def stack_kernel(count, *refs):
    blocks, (keys, values) = refs[:count], refs[count:]
    tokens = blocks[0].shape[0]
    for b, block in enumerate(blocks):
        keys[b * tokens : (b + 1) * tokens, :] = block[:, :HEAD_WIDTH]
        values[b * tokens : (b + 1) * tokens, :] = block[:, HEAD_WIDTH:]


def attend_kernel(count, offsets, head_index, queries, query_pos, key_pos, *refs):
    if count:
        outs, (keys, values) = refs[count:-2], refs[-2:]
        stack_kernel(count, *refs[:count], keys, values)
    else:
        (keys, values), outs = refs[:2], refs[2:]
    sub = outs[0].shape[0]
    per_device = queries.shape[1] // HEAD_WIDTH
    length = keys.shape[0]
    factor = math.log2(math.e) / math.sqrt(HEAD_WIDTH)
    for k, out in zip(offsets, outs):
        first = pl.multiple_of((head_index[0] ^ k) * sub, sub)
        rows = queries[pl.ds(first, sub), :]
        stacked = jnp.concatenate([rows[:, i * HEAD_WIDTH : (i + 1) * HEAD_WIDTH] for i in range(per_device)], axis=0)
        scores = lax.dot_general(stacked, keys[...], (((1,), (1,)), ((), ())), preferred_element_type=jnp.float32)
        allowed = key_pos[...] <= query_pos[pl.ds(first, sub), :]
        scores = jnp.where(allowed[None], scores.reshape(per_device, sub, length), -1e30)
        largest = jnp.max(scores, axis=2, keepdims=True)
        unnormed = jnp.exp2((scores - largest) * factor)
        totals = jnp.sum(unnormed, axis=2, keepdims=True)
        weights = unnormed.astype(jnp.bfloat16).reshape(per_device * sub, length)
        mixed = jnp.dot(weights, values[...], preferred_element_type=jnp.float32)
        mixed = mixed.reshape(per_device, sub, HEAD_WIDTH) / totals
        for i in range(per_device):
            out[:, i * HEAD_WIDTH : (i + 1) * HEAD_WIDTH] = mixed[i].astype(out.dtype)


def attend(offsets, receivers, head_index, queries, query_pos, key_pos, blocks, stacked=()):
    tokens, width = queries.shape
    length = key_pos.shape[1]
    count = 0 if stacked else len(blocks)
    given = stacked or blocks
    piece = jax.ShapeDtypeStruct((tokens // receivers, width), jnp.bfloat16)
    held = [] if stacked else [jax.ShapeDtypeStruct((length, HEAD_WIDTH), jnp.bfloat16)] * 2
    rows = tokens * len(offsets) // receivers
    work = rows * length * width
    return pl.pallas_call(
        functools.partial(attend_kernel, count, offsets),
        out_shape=[piece] * len(offsets) + held,
        in_specs=[SMEM] + [VMEM] * (3 + len(given)),
        out_specs=[VMEM] * (len(offsets) + len(held)),
        compiler_params=params(),
        cost_estimate=pl.CostEstimate(
            flops=16 * work, bytes_accessed=4 * length * HEAD_WIDTH, transcendentals=work // HEAD_WIDTH
        ),
        name="attend",
    )(head_index, queries, query_pos, key_pos, *given)


def join_kernel(count, head_index, *refs):
    pieces, (_, out, sems) = refs[:count], refs[count:]
    width = pieces[0].shape[1]
    copies(
        [
            (piece, out.at[0, 0, :, pl.ds(pl.multiple_of((head_index[0] ^ k) * width, width), width)])
            for k, piece in enumerate(pieces)
        ],
        sems,
    )


def join(head_index, pieces, corner):
    rows, width = pieces[0].shape
    return pl.pallas_call(
        functools.partial(join_kernel, len(pieces)),
        out_shape=jax.ShapeDtypeStruct((1, 1, rows, width * len(pieces)), jnp.bfloat16),
        in_specs=[SMEM] + [VMEM] * len(pieces) + [HBM],
        out_specs=HBM,
        scratch_shapes=[pltpu.SemaphoreType.DMA((len(pieces),))],
        compiler_params=params(),
        name="join",
    )(head_index, *pieces, corner)


def body(activations, key_matrix, value_matrix, queries, block_order):
    heads, inner, outer = (lax.axis_size(name) for name in ("head", "inner", "outer"))
    head, z, x = (lax.axis_index(name) for name in ("head", "inner", "outer"))
    tokens = activations.shape[0]
    sub = tokens // heads
    depth = key_matrix.shape[0]
    sharing = heads // KEY_VALUE_HEADS
    head_index = jnp.reshape(head, (1,))

    pieces = [
        lax.dynamic_slice(activations, (head * sub, (z ^ k) * depth), (sub, depth)) for k in range(inner)
    ]
    heads_of = (head ^ jnp.arange(heads, dtype=jnp.int32)) // sharing
    pieces[0], matrices = lax.optimization_barrier((pieces[0], (key_matrix, value_matrix)))
    matrices = load(heads_of, *matrices)
    arrived = swap_all(pieces, "inner")

    bounds = sorted({0, inner // 2, inner * 3 // 4, inner})
    partial = []
    for first, last in zip(bounds, bounds[1:-1]):
        _, rows = lax.optimization_barrier((partial, arrived[first:last]))
        partial = partial + project(rows, *matrices, first == 0, False)
    _, rows = lax.optimization_barrier((partial, arrived[bounds[-2] :]))
    split = project(rows, *matrices, False, True)
    pairs = range(heads // 2)
    late = [[swap_both(split[k - bounds[-2]][f], "head", 2 * f, "inner", k) for k in range(bounds[-2], inner)] for f in pairs]
    early = swap_all(partial, "inner")
    sums = swap_all(gather(early[0], early[1:]), "head", 2)
    mine, others = total(sums, late)
    own = jnp.concatenate([mine, swap(others, "head", 1)], axis=0)

    nearby = swap_all([own] * inner, "inner")
    blocks, cycle = [], []
    for j in range(outer):
        for k in range(inner):
            if j == 0:
                blocks.append(nearby[k])
            elif k in (1, inner - 1):
                blocks.append(swap_both(own, "inner", k, "outer", j))
            else:
                blocks.append(swap(nearby[k], "outer", j))
            cycle.append((z ^ k) * outer + (x ^ j))

    block_size = tokens // 2
    row = jnp.arange(tokens, dtype=jnp.int32)
    order = block_order.reshape(-1, 2)

    def positions(shard):
        return (lax.dynamic_index_in_dim(order, shard, 0, False)[:, None] * block_size + row[None, :block_size]).reshape(
            tokens
        )

    query_pos = positions(z * outer + x)
    shards = jnp.stack(cycle)
    distance = jnp.arange(heads, dtype=jnp.int32).reshape(heads // 2, 2).T.reshape(heads)
    rows_of = ((head ^ distance)[:, None] * sub + row[None, :sub]).reshape(tokens)
    one_hot = shards[:, None] == jnp.arange(order.shape[0], dtype=jnp.int32)[None, :]
    firsts = jnp.sum(jnp.where(one_hot[:, :, None], order[None], 0), axis=1)
    block_of = jnp.where(rows_of[None, :] < block_size, firsts[:, :1], firsts[:, 1:])
    key_pos = (block_of * block_size + rows_of[None, :] % block_size).reshape(1, -1)

    place = head_index, queries, query_pos[:, None], key_pos, blocks
    half = max(heads // 2, 1)
    *far_rows, keys, values = attend(range(half, heads), heads, *place)
    near_rows = attend(range(half), heads, *place, stacked=(keys, values))
    far = [swap(rows, "head", k) for k, rows in zip(range(half, heads), far_rows)]
    near = swap_all(near_rows, "head")
    corner = sum(rows[:8, :HEAD_WIDTH] for rows in far)
    return join(head_index, near + far, corner)


def solution(mesh):
    placed = (
        P(("inner", "outer"), None),
        P("inner", None),
        P("inner", None),
        P(("inner", "outer"), "head"),
        P(),
    )
    return jax.shard_map(
        body,
        mesh=mesh,
        in_specs=placed,
        out_specs=P(("inner", "outer"), "head", None, None),
        check_vma=False,
    )
```

```python
import functools
import math

import jax
import jax.numpy as jnp
from jax import lax
from jax.experimental import pallas as pl
from jax.experimental.pallas import tpu as pltpu
from jax.sharding import PartitionSpec as P

QUERY_HEADS = 32
KEY_VALUE_HEADS = 4
HEAD_WIDTH = 128
VMEM = pl.BlockSpec(memory_space=pltpu.VMEM)
SMEM = pl.BlockSpec(memory_space=pltpu.SMEM)
HBM = pl.BlockSpec(memory_space=pltpu.HBM)
LIMIT = 16 * 1024 * 1024
LOAD_LIMIT = 48 * 1024 * 1024


def params(limit=LIMIT):
    return pltpu.CompilerParams(vmem_limit_bytes=limit)


def swap(piece, axis, offset):
    return lax.ppermute(piece, axis, [(i, i ^ offset) for i in range(lax.axis_size(axis))])


def swap_both(piece, axis, offset, other_axis, other):
    sizes = lax.axis_size(axis), lax.axis_size(other_axis)
    order = [(i * sizes[1] + j, (i ^ offset) * sizes[1] + (j ^ other)) for i in range(sizes[0]) for j in range(sizes[1])]
    return lax.ppermute(piece, (axis, other_axis), order)


def swap_all(pieces, axis, unit=1):
    got = {k: swap(pieces[k], axis, k * unit) for k in reversed(range(1, len(pieces)))}
    return [pieces[0]] + [got[k] for k in range(1, len(pieces))]


def copies(pairs, sems):
    started = [pltpu.make_async_copy(source, target, sems.at[i]) for i, (source, target) in enumerate(pairs)]
    for copy in started:
        copy.start()
    for copy in started:
        copy.wait()


def load_kernel(heads_of, key_matrix, value_matrix, *refs):
    outs, sems = refs[:2], refs[2]
    pairs = []
    for j in range(heads_of.shape[0]):
        columns = pl.ds(pl.multiple_of(heads_of[j] * HEAD_WIDTH, HEAD_WIDTH), HEAD_WIDTH)
        for source, out in zip((key_matrix, value_matrix), outs):
            pairs.append((source.at[:, columns], out.at[:, pl.ds(j * HEAD_WIDTH, HEAD_WIDTH)]))
    copies(pairs, sems)


def load(heads_of, *matrices):
    depth, receivers = matrices[0].shape[0], heads_of.shape[0]
    loaded = jax.ShapeDtypeStruct((depth, receivers * HEAD_WIDTH), jnp.bfloat16)
    return pl.pallas_call(
        load_kernel,
        out_shape=[loaded] * 2,
        in_specs=[SMEM, HBM, HBM],
        out_specs=[VMEM] * 2,
        scratch_shapes=[pltpu.SemaphoreType.DMA((2 * receivers,))],
        compiler_params=params(LOAD_LIMIT),
        cost_estimate=pl.CostEstimate(flops=0, bytes_accessed=8 * loaded.size, transcendentals=0),
        name="load",
    )(heads_of, *matrices)


def encode(out, key, value):
    width = key.shape[1]
    high = key.astype(out.dtype)
    out[:, :width], out[:, width : 2 * width] = high, (key - high.astype(jnp.float32)).astype(out.dtype)
    out[:, 2 * width :] = value.astype(out.dtype)


def decode(part):
    width = part.shape[1] // 3
    high, low, value = (part[:, i * width : (i + 1) * width].astype(jnp.float32) for i in range(3))
    return high + low, value


def project_kernel(count, keeps, splits, *refs):
    pieces, (key_matrix, value_matrix), outs = refs[:count], refs[count : count + 2], refs[count + 2 :]
    rows = pieces[0][...] if count == 1 else jnp.concatenate([piece[...] for piece in pieces], axis=0)
    width = key_matrix.shape[1]
    sub = outs[0].shape[0]
    keys = jnp.dot(rows, key_matrix[...], preferred_element_type=jnp.float32)
    values = jnp.dot(rows, value_matrix[...], preferred_element_type=jnp.float32)
    each = 2 * HEAD_WIDTH if splits else width
    for i, out in enumerate(outs):
        k, f = divmod(i, width // each)
        at = slice(k * sub, (k + 1) * sub), slice(f * each, (f + 1) * each)
        if keeps and k == 0:
            out[:, :width], out[:, width:] = keys[at], values[at]
        else:
            encode(out, keys[at], values[at])


def project(pieces, key_matrix, value_matrix, keeps, splits):
    sub, width = pieces[0].shape[0], key_matrix.shape[1]
    given = pieces if sub % 16 == 0 else [jnp.concatenate(pieces, axis=0)]
    each = 2 * HEAD_WIDTH if splits else width
    kept = jax.ShapeDtypeStruct((sub, 2 * width), jnp.float32)
    sent = jax.ShapeDtypeStruct((sub, 3 * each), jnp.bfloat16)
    shapes = [kept if keeps and i == 0 else sent for i in range(len(pieces) * width // each)]
    outs = pl.pallas_call(
        functools.partial(project_kernel, len(given), keeps, splits),
        out_shape=shapes,
        in_specs=[VMEM] * (len(given) + 2),
        out_specs=[VMEM] * len(shapes),
        compiler_params=params(),
        cost_estimate=pl.CostEstimate(
            flops=4 * len(pieces) * sub * key_matrix.size, bytes_accessed=4 * key_matrix.size, transcendentals=0
        ),
        name="project",
    )(*given, key_matrix, value_matrix)
    pairs = width // each
    return [outs[i : i + pairs] for i in range(0, len(outs), pairs)] if splits else list(outs)


def gather_kernel(count, own, *refs):
    parts, outs = refs[:count], refs[count:]
    width = own.shape[1] // 2
    key, value = own[:, :width], own[:, width:]
    for part in parts:
        more = decode(part)
        key, value = key + more[0], value + more[1]
    each = outs[0].shape[1] // 2
    for f, out in enumerate(outs):
        at = slice(f * each, (f + 1) * each)
        if f == 0:
            out[:, :each], out[:, each:] = key[:, at], value[:, at]
        else:
            encode(out, key[:, at], value[:, at])


def gather(own, parts):
    rows, width = own.shape
    pairs = width // (4 * HEAD_WIDTH)
    return pl.pallas_call(
        functools.partial(gather_kernel, len(parts)),
        out_shape=[jax.ShapeDtypeStruct((rows, 4 * HEAD_WIDTH), jnp.float32)]
        + [jax.ShapeDtypeStruct((rows, 6 * HEAD_WIDTH), jnp.bfloat16)] * (pairs - 1),
        in_specs=[VMEM] * (1 + len(parts)),
        out_specs=[VMEM] * pairs,
        compiler_params=params(),
        name="gather",
    )(own, *parts)


def total_kernel(pairs, *refs):
    sums, parts, outs = refs[:pairs], refs[pairs:-2], refs[-2:]
    count = len(parts) // pairs
    shares = []
    for f, share in enumerate(sums):
        width = share.shape[1] // 2
        key, value = (share[:, :width], share[:, width:]) if f == 0 else decode(share)
        for part in parts[f * count : (f + 1) * count]:
            more = decode(part)
            key, value = key + more[0], value + more[1]
        shares.append((key, value))
    for i, out in enumerate(outs):
        for half in range(2):
            columns = [share[half][:, i * HEAD_WIDTH : (i + 1) * HEAD_WIDTH] for share in shares]
            whole = jnp.concatenate(columns, axis=0)
            out[:, half * HEAD_WIDTH : (half + 1) * HEAD_WIDTH] = whole.astype(out.dtype)


def total(sums, parts):
    given = [*sums, *(part for row in parts for part in row)]
    share = jax.ShapeDtypeStruct((sums[0].shape[0] * len(sums), 2 * HEAD_WIDTH), jnp.bfloat16)
    return pl.pallas_call(
        functools.partial(total_kernel, len(sums)),
        out_shape=[share] * 2,
        in_specs=[VMEM] * len(given),
        out_specs=[VMEM] * 2,
        compiler_params=params(),
        name="total",
    )(*given)


def stack_kernel(count, *refs):
    blocks, (keys, values) = refs[:count], refs[count:]
    tokens = blocks[0].shape[0]
    for b, block in enumerate(blocks):
        keys[b * tokens : (b + 1) * tokens, :] = block[:, :HEAD_WIDTH]
        values[b * tokens : (b + 1) * tokens, :] = block[:, HEAD_WIDTH:]


def attend_kernel(count, offsets, head_index, queries, query_pos, key_pos, *refs):
    if count:
        outs, (keys, values) = refs[count:-2], refs[-2:]
        stack_kernel(count, *refs[:count], keys, values)
    else:
        (keys, values), outs = refs[:2], refs[2:]
    sub = outs[0].shape[0]
    per_device = queries.shape[1] // HEAD_WIDTH
    length = keys.shape[0]
    factor = math.log2(math.e) / math.sqrt(HEAD_WIDTH)
    for k, out in zip(offsets, outs):
        first = pl.multiple_of((head_index[0] ^ k) * sub, sub)
        rows = queries[pl.ds(first, sub), :]
        stacked = jnp.concatenate([rows[:, i * HEAD_WIDTH : (i + 1) * HEAD_WIDTH] for i in range(per_device)], axis=0)
        scores = lax.dot_general(stacked, keys[...], (((1,), (1,)), ((), ())), preferred_element_type=jnp.float32)
        allowed = key_pos[...] <= query_pos[pl.ds(first, sub), :]
        scores = jnp.where(allowed[None], scores.reshape(per_device, sub, length), -1e30)
        largest = jnp.max(scores, axis=2, keepdims=True)
        unnormed = jnp.exp2((scores - largest) * factor)
        totals = jnp.sum(unnormed, axis=2, keepdims=True)
        weights = unnormed.astype(jnp.bfloat16).reshape(per_device * sub, length)
        mixed = jnp.dot(weights, values[...], preferred_element_type=jnp.float32)
        mixed = mixed.reshape(per_device, sub, HEAD_WIDTH) / totals
        for i in range(per_device):
            out[:, i * HEAD_WIDTH : (i + 1) * HEAD_WIDTH] = mixed[i].astype(out.dtype)


def attend(offsets, receivers, head_index, queries, query_pos, key_pos, blocks, stacked=()):
    tokens, width = queries.shape
    length = key_pos.shape[1]
    count = 0 if stacked else len(blocks)
    given = stacked or blocks
    piece = jax.ShapeDtypeStruct((tokens // receivers, width), jnp.bfloat16)
    held = [] if stacked else [jax.ShapeDtypeStruct((length, HEAD_WIDTH), jnp.bfloat16)] * 2
    rows = tokens * len(offsets) // receivers
    work = rows * length * width
    return pl.pallas_call(
        functools.partial(attend_kernel, count, offsets),
        out_shape=[piece] * len(offsets) + held,
        in_specs=[SMEM] + [VMEM] * (3 + len(given)),
        out_specs=[VMEM] * (len(offsets) + len(held)),
        compiler_params=params(),
        cost_estimate=pl.CostEstimate(
            flops=16 * work, bytes_accessed=4 * length * HEAD_WIDTH, transcendentals=work // HEAD_WIDTH
        ),
        name="attend",
    )(head_index, queries, query_pos, key_pos, *given)


def join_kernel(count, head_index, *refs):
    pieces, (_, out, sems) = refs[:count], refs[count:]
    width = pieces[0].shape[1]
    copies(
        [
            (piece, out.at[0, 0, :, pl.ds(pl.multiple_of((head_index[0] ^ k) * width, width), width)])
            for k, piece in enumerate(pieces)
        ],
        sems,
    )


def join(head_index, pieces, corner):
    rows, width = pieces[0].shape
    return pl.pallas_call(
        functools.partial(join_kernel, len(pieces)),
        out_shape=jax.ShapeDtypeStruct((1, 1, rows, width * len(pieces)), jnp.bfloat16),
        in_specs=[SMEM] + [VMEM] * len(pieces) + [HBM],
        out_specs=HBM,
        scratch_shapes=[pltpu.SemaphoreType.DMA((len(pieces),))],
        compiler_params=params(),
        name="join",
    )(head_index, *pieces, corner)


def body(activations, key_matrix, value_matrix, queries, block_order):
    heads, inner, outer = (lax.axis_size(name) for name in ("head", "inner", "outer"))
    head, z, x = (lax.axis_index(name) for name in ("head", "inner", "outer"))
    tokens = activations.shape[0]
    sub = tokens // heads
    depth = key_matrix.shape[0]
    sharing = heads // KEY_VALUE_HEADS
    head_index = jnp.reshape(head, (1,))

    ring = [0]
    while len(ring) < inner:
        ring = [2 * k for k in ring] + [2 * k + 1 for k in ring]
    pieces = [lax.dynamic_slice(activations, (head * sub, (z ^ k) * depth), (sub, depth)) for k in ring]
    heads_of = (head ^ jnp.arange(heads, dtype=jnp.int32)) // sharing
    pieces[0], matrices = lax.optimization_barrier((pieces[0], (key_matrix, value_matrix)))
    matrices = load(heads_of, *matrices)
    arrived = [pieces[0]] + [swap(piece, "inner", k) for piece, k in list(zip(pieces, ring))[1:]]

    bounds = sorted({0, inner // 2, inner * 3 // 4, inner})
    partial = []
    for first, last in zip(bounds, bounds[1:-1]):
        _, rows = lax.optimization_barrier((partial, arrived[first:last]))
        partial = partial + project(rows, *matrices, first == 0, False)
    _, rows = lax.optimization_barrier((partial, arrived[bounds[-2] :]))
    split = project(rows, *matrices, False, True)
    pairs = range(heads // 2)
    late = [[swap_both(split[i - bounds[-2]][f], "head", 2 * f, "inner", ring[i]) for i in range(bounds[-2], inner)] for f in pairs]
    early = [partial[0]] + [swap(part, "inner", k) for part, k in list(zip(partial, ring))[1:]]
    sums = swap_all(gather(early[0], early[1:]), "head", 2)
    mine, others = total(sums, late)
    own = jnp.concatenate([mine, swap(others, "head", 1)], axis=0)

    nearby = swap_all([own] * inner, "inner")
    blocks, cycle = [], []
    for j in range(outer):
        for k in range(inner):
            if j == 0:
                blocks.append(nearby[k])
            elif k in (1, inner - 1):
                blocks.append(swap_both(own, "inner", k, "outer", j))
            else:
                blocks.append(swap(nearby[k], "outer", j))
            cycle.append((z ^ k) * outer + (x ^ j))

    block_size = tokens // 2
    row = jnp.arange(tokens, dtype=jnp.int32)
    order = block_order.reshape(-1, 2)

    def positions(shard):
        return (lax.dynamic_index_in_dim(order, shard, 0, False)[:, None] * block_size + row[None, :block_size]).reshape(
            tokens
        )

    query_pos = positions(z * outer + x)
    shards = jnp.stack(cycle)
    distance = jnp.arange(heads, dtype=jnp.int32).reshape(heads // 2, 2).T.reshape(heads)
    rows_of = ((head ^ distance)[:, None] * sub + row[None, :sub]).reshape(tokens)
    one_hot = shards[:, None] == jnp.arange(order.shape[0], dtype=jnp.int32)[None, :]
    firsts = jnp.sum(jnp.where(one_hot[:, :, None], order[None], 0), axis=1)
    block_of = jnp.where(rows_of[None, :] < block_size, firsts[:, :1], firsts[:, 1:])
    key_pos = (block_of * block_size + rows_of[None, :] % block_size).reshape(1, -1)

    place = head_index, queries, query_pos[:, None], key_pos, blocks
    half = max(heads // 2, 1)
    *far_rows, keys, values = attend(range(half, heads), heads, *place)
    near_rows = attend(range(half), heads, *place, stacked=(keys, values))
    far = [swap(rows, "head", k) for k, rows in zip(range(half, heads), far_rows)]
    near = swap_all(near_rows, "head")
    corner = sum(rows[:8, :HEAD_WIDTH] for rows in far)
    return join(head_index, near + far, corner)


def solution(mesh):
    placed = (
        P(("inner", "outer"), None),
        P("inner", None),
        P("inner", None),
        P(("inner", "outer"), "head"),
        P(),
    )
    return jax.shard_map(
        body,
        mesh=mesh,
        in_specs=placed,
        out_specs=P(("inner", "outer"), "head", None, None),
        check_vma=False,
    )
```

```python
import functools
import math

import jax
import jax.numpy as jnp
from jax import lax
from jax.experimental import pallas as pl
from jax.experimental.pallas import tpu as pltpu
from jax.sharding import PartitionSpec as P

QUERY_HEADS = 32
KEY_VALUE_HEADS = 4
HEAD_WIDTH = 128
VMEM = pl.BlockSpec(memory_space=pltpu.VMEM)
SMEM = pl.BlockSpec(memory_space=pltpu.SMEM)
HBM = pl.BlockSpec(memory_space=pltpu.HBM)
LIMIT = 16 * 1024 * 1024
LOAD_LIMIT = 48 * 1024 * 1024


def params(limit=LIMIT):
    return pltpu.CompilerParams(vmem_limit_bytes=limit)


def swap(piece, axis, offset):
    return lax.ppermute(piece, axis, [(i, i ^ offset) for i in range(lax.axis_size(axis))])


def swap_both(piece, axis, offset, other_axis, other):
    sizes = lax.axis_size(axis), lax.axis_size(other_axis)
    order = [(i * sizes[1] + j, (i ^ offset) * sizes[1] + (j ^ other)) for i in range(sizes[0]) for j in range(sizes[1])]
    return lax.ppermute(piece, (axis, other_axis), order)


def swap_all(pieces, axis, unit=1):
    got = {k: swap(pieces[k], axis, k * unit) for k in reversed(range(1, len(pieces)))}
    return [pieces[0]] + [got[k] for k in range(1, len(pieces))]


def copies(pairs, sems):
    started = [pltpu.make_async_copy(source, target, sems.at[i]) for i, (source, target) in enumerate(pairs)]
    for copy in started:
        copy.start()
    for copy in started:
        copy.wait()


def load_kernel(heads_of, key_matrix, value_matrix, *refs):
    outs, sems = refs[:2], refs[2]
    pairs = []
    for j in range(heads_of.shape[0]):
        columns = pl.ds(pl.multiple_of(heads_of[j] * HEAD_WIDTH, HEAD_WIDTH), HEAD_WIDTH)
        for source, out in zip((key_matrix, value_matrix), outs):
            pairs.append((source.at[:, columns], out.at[:, pl.ds(j * HEAD_WIDTH, HEAD_WIDTH)]))
    copies(pairs, sems)


def load(heads_of, *matrices):
    depth, receivers = matrices[0].shape[0], heads_of.shape[0]
    loaded = jax.ShapeDtypeStruct((depth, receivers * HEAD_WIDTH), jnp.bfloat16)
    return pl.pallas_call(
        load_kernel,
        out_shape=[loaded] * 2,
        in_specs=[SMEM, HBM, HBM],
        out_specs=[VMEM] * 2,
        scratch_shapes=[pltpu.SemaphoreType.DMA((2 * receivers,))],
        compiler_params=params(LOAD_LIMIT),
        cost_estimate=pl.CostEstimate(flops=0, bytes_accessed=8 * loaded.size, transcendentals=0),
        name="load",
    )(heads_of, *matrices)


def encode(out, key, value):
    width = key.shape[1]
    high = key.astype(out.dtype)
    out[:, :width], out[:, width : 2 * width] = high, (key - high.astype(jnp.float32)).astype(out.dtype)
    out[:, 2 * width :] = value.astype(out.dtype)


def decode(part):
    width = part.shape[1] // 3
    high, low, value = (part[:, i * width : (i + 1) * width].astype(jnp.float32) for i in range(3))
    return high + low, value


def project_kernel(count, keeps, splits, *refs):
    pieces, (key_matrix, value_matrix), outs = refs[:count], refs[count : count + 2], refs[count + 2 :]
    rows = pieces[0][...] if count == 1 else jnp.concatenate([piece[...] for piece in pieces], axis=0)
    width = key_matrix.shape[1]
    sub = outs[0].shape[0]
    keys = jnp.dot(rows, key_matrix[...], preferred_element_type=jnp.float32)
    values = jnp.dot(rows, value_matrix[...], preferred_element_type=jnp.float32)
    each = 2 * HEAD_WIDTH if splits else width
    for i, out in enumerate(outs):
        k, f = divmod(i, width // each)
        at = slice(k * sub, (k + 1) * sub), slice(f * each, (f + 1) * each)
        if keeps and k == 0:
            out[:, :width], out[:, width:] = keys[at], values[at]
        else:
            encode(out, keys[at], values[at])


def project(pieces, key_matrix, value_matrix, keeps, splits):
    sub, width = pieces[0].shape[0], key_matrix.shape[1]
    given = pieces if sub % 16 == 0 else [jnp.concatenate(pieces, axis=0)]
    each = 2 * HEAD_WIDTH if splits else width
    kept = jax.ShapeDtypeStruct((sub, 2 * width), jnp.float32)
    sent = jax.ShapeDtypeStruct((sub, 3 * each), jnp.bfloat16)
    shapes = [kept if keeps and i == 0 else sent for i in range(len(pieces) * width // each)]
    outs = pl.pallas_call(
        functools.partial(project_kernel, len(given), keeps, splits),
        out_shape=shapes,
        in_specs=[VMEM] * (len(given) + 2),
        out_specs=[VMEM] * len(shapes),
        compiler_params=params(),
        cost_estimate=pl.CostEstimate(
            flops=4 * len(pieces) * sub * key_matrix.size, bytes_accessed=4 * key_matrix.size, transcendentals=0
        ),
        name="project",
    )(*given, key_matrix, value_matrix)
    pairs = width // each
    return [outs[i : i + pairs] for i in range(0, len(outs), pairs)] if splits else list(outs)


def gather_kernel(count, own, *refs):
    parts, outs = refs[:count], refs[count:]
    width = own.shape[1] // 2
    key, value = own[:, :width], own[:, width:]
    for part in parts:
        more = decode(part)
        key, value = key + more[0], value + more[1]
    each = outs[0].shape[1] // 2
    for f, out in enumerate(outs):
        at = slice(f * each, (f + 1) * each)
        if f == 0:
            out[:, :each], out[:, each:] = key[:, at], value[:, at]
        else:
            encode(out, key[:, at], value[:, at])


def gather(own, parts):
    rows, width = own.shape
    pairs = width // (4 * HEAD_WIDTH)
    return pl.pallas_call(
        functools.partial(gather_kernel, len(parts)),
        out_shape=[jax.ShapeDtypeStruct((rows, 4 * HEAD_WIDTH), jnp.float32)]
        + [jax.ShapeDtypeStruct((rows, 6 * HEAD_WIDTH), jnp.bfloat16)] * (pairs - 1),
        in_specs=[VMEM] * (1 + len(parts)),
        out_specs=[VMEM] * pairs,
        compiler_params=params(),
        name="gather",
    )(own, *parts)


def total_kernel(pairs, *refs):
    sums, parts, outs = refs[:pairs], refs[pairs:-2], refs[-2:]
    count = len(parts) // pairs
    shares = []
    for f, share in enumerate(sums):
        width = share.shape[1] // 2
        key, value = (share[:, :width], share[:, width:]) if f == 0 else decode(share)
        for part in parts[f * count : (f + 1) * count]:
            more = decode(part)
            key, value = key + more[0], value + more[1]
        shares.append((key, value))
    for i, out in enumerate(outs):
        for half in range(2):
            columns = [share[half][:, i * HEAD_WIDTH : (i + 1) * HEAD_WIDTH] for share in shares]
            whole = jnp.concatenate(columns, axis=0)
            out[:, half * HEAD_WIDTH : (half + 1) * HEAD_WIDTH] = whole.astype(out.dtype)


def total(sums, parts):
    given = [*sums, *(part for row in parts for part in row)]
    share = jax.ShapeDtypeStruct((sums[0].shape[0] * len(sums), 2 * HEAD_WIDTH), jnp.bfloat16)
    return pl.pallas_call(
        functools.partial(total_kernel, len(sums)),
        out_shape=[share] * 2,
        in_specs=[VMEM] * len(given),
        out_specs=[VMEM] * 2,
        compiler_params=params(),
        name="total",
    )(*given)


def stack_kernel(count, *refs):
    blocks, (keys, values) = refs[:count], refs[count:]
    tokens = blocks[0].shape[0]
    for b, block in enumerate(blocks):
        keys[b * tokens : (b + 1) * tokens, :] = block[:, :HEAD_WIDTH]
        values[b * tokens : (b + 1) * tokens, :] = block[:, HEAD_WIDTH:]


def attend_kernel(count, offsets, head_index, queries, query_pos, key_pos, *refs):
    if count:
        outs, (keys, values) = refs[count:-2], refs[-2:]
        stack_kernel(count, *refs[:count], keys, values)
    else:
        (keys, values), outs = refs[:2], refs[2:]
    sub = outs[0].shape[0]
    per_device = queries.shape[1] // HEAD_WIDTH
    length = keys.shape[0]
    factor = math.log2(math.e) / math.sqrt(HEAD_WIDTH)
    for k, out in zip(offsets, outs):
        first = pl.multiple_of((head_index[0] ^ k) * sub, sub)
        rows = queries[pl.ds(first, sub), :]
        stacked = jnp.concatenate([rows[:, i * HEAD_WIDTH : (i + 1) * HEAD_WIDTH] for i in range(per_device)], axis=0)
        scores = lax.dot_general(stacked, keys[...], (((1,), (1,)), ((), ())), preferred_element_type=jnp.float32)
        allowed = key_pos[...] <= query_pos[pl.ds(first, sub), :]
        scores = jnp.where(allowed[None], scores.reshape(per_device, sub, length), -1e30)
        largest = jnp.max(scores, axis=2, keepdims=True)
        unnormed = jnp.exp2((scores - largest) * factor)
        totals = jnp.sum(unnormed, axis=2, keepdims=True)
        weights = unnormed.astype(jnp.bfloat16).reshape(per_device * sub, length)
        mixed = jnp.dot(weights, values[...], preferred_element_type=jnp.float32)
        mixed = mixed.reshape(per_device, sub, HEAD_WIDTH) / totals
        for i in range(per_device):
            out[:, i * HEAD_WIDTH : (i + 1) * HEAD_WIDTH] = mixed[i].astype(out.dtype)


def attend(offsets, receivers, head_index, queries, query_pos, key_pos, blocks, stacked=()):
    tokens, width = queries.shape
    length = key_pos.shape[1]
    count = 0 if stacked else len(blocks)
    given = stacked or blocks
    piece = jax.ShapeDtypeStruct((tokens // receivers, width), jnp.bfloat16)
    held = [] if stacked else [jax.ShapeDtypeStruct((length, HEAD_WIDTH), jnp.bfloat16)] * 2
    rows = tokens * len(offsets) // receivers
    work = rows * length * width
    return pl.pallas_call(
        functools.partial(attend_kernel, count, offsets),
        out_shape=[piece] * len(offsets) + held,
        in_specs=[SMEM] + [VMEM] * (3 + len(given)),
        out_specs=[VMEM] * (len(offsets) + len(held)),
        compiler_params=params(),
        cost_estimate=pl.CostEstimate(
            flops=16 * work, bytes_accessed=4 * length * HEAD_WIDTH, transcendentals=work // HEAD_WIDTH
        ),
        name="attend",
    )(head_index, queries, query_pos, key_pos, *given)


def join_kernel(count, head_index, *refs):
    pieces, (_, out, sems) = refs[:count], refs[count:]
    width = pieces[0].shape[1]
    copies(
        [
            (piece, out.at[0, 0, :, pl.ds(pl.multiple_of((head_index[0] ^ k) * width, width), width)])
            for k, piece in enumerate(pieces)
        ],
        sems,
    )


def join(head_index, pieces, corner):
    rows, width = pieces[0].shape
    return pl.pallas_call(
        functools.partial(join_kernel, len(pieces)),
        out_shape=jax.ShapeDtypeStruct((1, 1, rows, width * len(pieces)), jnp.bfloat16),
        in_specs=[SMEM] + [VMEM] * len(pieces) + [HBM],
        out_specs=HBM,
        scratch_shapes=[pltpu.SemaphoreType.DMA((len(pieces),))],
        compiler_params=params(),
        name="join",
    )(head_index, *pieces, corner)


def body(activations, key_matrix, value_matrix, queries, block_order):
    heads, inner, outer = (lax.axis_size(name) for name in ("head", "inner", "outer"))
    head, z, x = (lax.axis_index(name) for name in ("head", "inner", "outer"))
    tokens = activations.shape[0]
    sub = tokens // heads
    depth = key_matrix.shape[0]
    sharing = heads // KEY_VALUE_HEADS
    head_index = jnp.reshape(head, (1,))

    ring = [0]
    while len(ring) < inner:
        ring = [2 * k for k in ring] + [2 * k + 1 for k in ring]
    pieces = [lax.dynamic_slice(activations, (head * sub, (z ^ k) * depth), (sub, depth)) for k in ring]
    heads_of = (head ^ jnp.arange(heads, dtype=jnp.int32)) // sharing
    pieces[0], matrices = lax.optimization_barrier((pieces[0], (key_matrix, value_matrix)))
    matrices = load(heads_of, *matrices)
    arrived = [pieces[0]] + [swap(piece, "inner", k) for piece, k in list(zip(pieces, ring))[1:]]

    bounds = sorted({0, inner // 2, inner * 3 // 4, inner})
    partial = []
    for first, last in zip(bounds, bounds[1:-1]):
        _, rows = lax.optimization_barrier((partial, arrived[first:last]))
        partial = partial + project(rows, *matrices, first == 0, False)
    _, rows = lax.optimization_barrier((partial, arrived[bounds[-2] :]))
    split = project(rows, *matrices, False, True)
    pairs = range(heads // 2)
    late = [[swap_both(split[i - bounds[-2]][f], "head", 2 * f, "inner", ring[i]) for i in range(bounds[-2], inner)] for f in pairs]
    early = [partial[0]] + [swap(part, "inner", k) for part, k in list(zip(partial, ring))[1:]]
    sums = swap_all(gather(early[0], early[1:]), "head", 2)
    mine, others = total(sums, late)
    own = jnp.concatenate([mine, swap(others, "head", 1)], axis=0)

    got = dict(enumerate(swap_all([own] * inner, "inner")))
    blocks, cycle = [], []
    for j in range(outer):
        if j > 0:
            beside = swap(own, "outer", j)
        for k in range(inner):
            if j == 0:
                block = got[k]
            elif k == 0:
                block = beside
            elif k < inner - 1:
                block = swap(beside, "inner", k)
            else:
                block = swap(got[k], "outer", j)
            blocks.append(block)
            cycle.append((z ^ k) * outer + (x ^ j))

    block_size = tokens // 2
    row = jnp.arange(tokens, dtype=jnp.int32)
    order = block_order.reshape(-1, 2)

    def positions(shard):
        return (lax.dynamic_index_in_dim(order, shard, 0, False)[:, None] * block_size + row[None, :block_size]).reshape(
            tokens
        )

    query_pos = positions(z * outer + x)
    shards = jnp.stack(cycle)
    distance = jnp.arange(heads, dtype=jnp.int32).reshape(heads // 2, 2).T.reshape(heads)
    rows_of = ((head ^ distance)[:, None] * sub + row[None, :sub]).reshape(tokens)
    one_hot = shards[:, None] == jnp.arange(order.shape[0], dtype=jnp.int32)[None, :]
    firsts = jnp.sum(jnp.where(one_hot[:, :, None], order[None], 0), axis=1)
    block_of = jnp.where(rows_of[None, :] < block_size, firsts[:, :1], firsts[:, 1:])
    key_pos = (block_of * block_size + rows_of[None, :] % block_size).reshape(1, -1)

    place = head_index, queries, query_pos[:, None], key_pos, blocks
    half = max(heads // 2, 1)
    *far_rows, keys, values = attend(range(half, heads), heads, *place)
    near_rows = attend(range(half), heads, *place, stacked=(keys, values))
    far = [swap(rows, "head", k) for k, rows in zip(range(half, heads), far_rows)]
    near = swap_all(near_rows, "head")
    corner = sum(rows[:8, :HEAD_WIDTH] for rows in far)
    return join(head_index, near + far, corner)


def solution(mesh):
    placed = (
        P(("inner", "outer"), None),
        P("inner", None),
        P("inner", None),
        P(("inner", "outer"), "head"),
        P(),
    )
    return jax.shard_map(
        body,
        mesh=mesh,
        in_specs=placed,
        out_specs=P(("inner", "outer"), "head", None, None),
        check_vma=False,
    )
```

```python
import functools
import math

import jax
import jax.numpy as jnp
from jax import lax
from jax.experimental import pallas as pl
from jax.experimental.pallas import tpu as pltpu
from jax.sharding import PartitionSpec as P

QUERY_HEADS = 32
KEY_VALUE_HEADS = 4
HEAD_WIDTH = 128
VMEM = pl.BlockSpec(memory_space=pltpu.VMEM)
SMEM = pl.BlockSpec(memory_space=pltpu.SMEM)
HBM = pl.BlockSpec(memory_space=pltpu.HBM)
LIMIT = 4 * 1024 * 1024
LOAD_LIMIT = 48 * 1024 * 1024


def params(limit=LIMIT):
    return pltpu.CompilerParams(vmem_limit_bytes=limit)


def swap(piece, axis, offset):
    return lax.ppermute(piece, axis, [(i, i ^ offset) for i in range(lax.axis_size(axis))])


def swap_both(piece, axis, offset, other_axis, other):
    sizes = lax.axis_size(axis), lax.axis_size(other_axis)
    order = [(i * sizes[1] + j, (i ^ offset) * sizes[1] + (j ^ other)) for i in range(sizes[0]) for j in range(sizes[1])]
    return lax.ppermute(piece, (axis, other_axis), order)


def swap_all(pieces, axis, unit=1):
    got = {k: swap(pieces[k], axis, k * unit) for k in reversed(range(1, len(pieces)))}
    return [pieces[0]] + [got[k] for k in range(1, len(pieces))]


def copies(pairs, sems):
    started = [pltpu.make_async_copy(source, target, sems.at[i]) for i, (source, target) in enumerate(pairs)]
    for copy in started:
        copy.start()
    for copy in started:
        copy.wait()


def load_kernel(heads_of, key_matrix, value_matrix, *refs):
    outs, sems = refs[:2], refs[2]
    pairs = []
    for j in range(heads_of.shape[0]):
        columns = pl.ds(pl.multiple_of(heads_of[j] * HEAD_WIDTH, HEAD_WIDTH), HEAD_WIDTH)
        for source, out in zip((key_matrix, value_matrix), outs):
            pairs.append((source.at[:, columns], out.at[:, pl.ds(j * HEAD_WIDTH, HEAD_WIDTH)]))
    copies(pairs, sems)


def load(heads_of, *matrices):
    depth, receivers = matrices[0].shape[0], heads_of.shape[0]
    loaded = jax.ShapeDtypeStruct((depth, receivers * HEAD_WIDTH), jnp.bfloat16)
    return pl.pallas_call(
        load_kernel,
        out_shape=[loaded] * 2,
        in_specs=[SMEM, HBM, HBM],
        out_specs=[VMEM] * 2,
        scratch_shapes=[pltpu.SemaphoreType.DMA((2 * receivers,))],
        compiler_params=params(LOAD_LIMIT),
        cost_estimate=pl.CostEstimate(flops=0, bytes_accessed=8 * loaded.size, transcendentals=0),
        name="load",
    )(heads_of, *matrices)


def encode(out, key, value):
    width = key.shape[1]
    high = key.astype(out.dtype)
    out[:, :width], out[:, width : 2 * width] = high, (key - high.astype(jnp.float32)).astype(out.dtype)
    out[:, 2 * width :] = value.astype(out.dtype)


def decode(part):
    width = part.shape[1] // 3
    high, low, value = (part[:, i * width : (i + 1) * width].astype(jnp.float32) for i in range(3))
    return high + low, value


def project_kernel(count, keeps, pair, *refs):
    pieces, (key_matrix, value_matrix), outs = refs[:count], refs[count : count + 2], refs[count + 2 :]
    rows = pieces[0][...] if count == 1 else jnp.concatenate([piece[...] for piece in pieces], axis=0)
    columns = slice(0, key_matrix.shape[1]) if pair is None else slice(2 * pair * HEAD_WIDTH, 2 * (pair + 1) * HEAD_WIDTH)
    sub = outs[0].shape[0]
    keys = jnp.dot(rows, key_matrix[:, columns], preferred_element_type=jnp.float32)
    values = jnp.dot(rows, value_matrix[:, columns], preferred_element_type=jnp.float32)
    width = keys.shape[1]
    for k, out in enumerate(outs):
        at = slice(k * sub, (k + 1) * sub)
        if keeps and k == 0:
            out[:, :width], out[:, width:] = keys[at], values[at]
        else:
            encode(out, keys[at], values[at])


def project(pieces, key_matrix, value_matrix, keeps, pair=None):
    sub, width = pieces[0].shape[0], key_matrix.shape[1] if pair is None else 2 * HEAD_WIDTH
    given = pieces if sub % 16 == 0 else [jnp.concatenate(pieces, axis=0)]
    kept = jax.ShapeDtypeStruct((sub, 2 * width), jnp.float32)
    sent = jax.ShapeDtypeStruct((sub, 3 * width), jnp.bfloat16)
    return list(
        pl.pallas_call(
            functools.partial(project_kernel, len(given), keeps, pair),
            out_shape=[kept if keeps and k == 0 else sent for k in range(len(pieces))],
            in_specs=[VMEM] * (len(given) + 2),
            out_specs=[VMEM] * len(pieces),
            compiler_params=params(),
            cost_estimate=pl.CostEstimate(
                flops=4 * len(pieces) * sub * width * key_matrix.shape[0],
                bytes_accessed=4 * width * key_matrix.shape[0],
                transcendentals=0,
            ),
            name="project",
        )(*given, key_matrix, value_matrix)
    )


def gather_kernel(count, own, *refs):
    parts, outs = refs[:count], refs[count:]
    width = own.shape[1] // 2
    key, value = own[:, :width], own[:, width:]
    for part in parts:
        more = decode(part)
        key, value = key + more[0], value + more[1]
    each = outs[0].shape[1] // 2
    for f, out in enumerate(outs):
        at = slice(f * each, (f + 1) * each)
        if f == 0:
            out[:, :each], out[:, each:] = key[:, at], value[:, at]
        else:
            encode(out, key[:, at], value[:, at])


def gather(own, parts):
    rows, width = own.shape
    pairs = width // (4 * HEAD_WIDTH)
    return pl.pallas_call(
        functools.partial(gather_kernel, len(parts)),
        out_shape=[jax.ShapeDtypeStruct((rows, 4 * HEAD_WIDTH), jnp.float32)]
        + [jax.ShapeDtypeStruct((rows, 6 * HEAD_WIDTH), jnp.bfloat16)] * (pairs - 1),
        in_specs=[VMEM] * (1 + len(parts)),
        out_specs=[VMEM] * pairs,
        compiler_params=params(),
        name="gather",
    )(own, *parts)


def total_kernel(pairs, *refs):
    sums, parts, outs = refs[:pairs], refs[pairs:-2], refs[-2:]
    count = len(parts) // pairs
    shares = []
    for f, share in enumerate(sums):
        width = share.shape[1] // 2
        key, value = (share[:, :width], share[:, width:]) if f == 0 else decode(share)
        for part in parts[f * count : (f + 1) * count]:
            more = decode(part)
            key, value = key + more[0], value + more[1]
        shares.append((key, value))
    for i, out in enumerate(outs):
        for half in range(2):
            columns = [share[half][:, i * HEAD_WIDTH : (i + 1) * HEAD_WIDTH] for share in shares]
            whole = jnp.concatenate(columns, axis=0)
            out[:, half * HEAD_WIDTH : (half + 1) * HEAD_WIDTH] = whole.astype(out.dtype)


def total(sums, parts):
    given = [*sums, *(part for row in parts for part in row)]
    share = jax.ShapeDtypeStruct((sums[0].shape[0] * len(sums), 2 * HEAD_WIDTH), jnp.bfloat16)
    return pl.pallas_call(
        functools.partial(total_kernel, len(sums)),
        out_shape=[share] * 2,
        in_specs=[VMEM] * len(given),
        out_specs=[VMEM] * 2,
        compiler_params=params(),
        name="total",
    )(*given)


def stack_kernel(count, *refs):
    blocks, (keys, values) = refs[:count], refs[count:]
    tokens = blocks[0].shape[0]
    for b, block in enumerate(blocks):
        keys[b * tokens : (b + 1) * tokens, :] = block[:, :HEAD_WIDTH]
        values[b * tokens : (b + 1) * tokens, :] = block[:, HEAD_WIDTH:]


def attend_kernel(count, offsets, head_index, queries, query_pos, key_pos, *refs):
    if count:
        outs, (keys, values) = refs[count:-2], refs[-2:]
        stack_kernel(count, *refs[:count], keys, values)
    else:
        (keys, values), outs = refs[:2], refs[2:]
    sub = outs[0].shape[0]
    per_device = queries.shape[1] // HEAD_WIDTH
    length = keys.shape[0]
    factor = math.log2(math.e) / math.sqrt(HEAD_WIDTH)
    for k, out in zip(offsets, outs):
        first = pl.multiple_of((head_index[0] ^ k) * sub, sub)
        rows = queries[pl.ds(first, sub), :]
        stacked = jnp.concatenate([rows[:, i * HEAD_WIDTH : (i + 1) * HEAD_WIDTH] for i in range(per_device)], axis=0)
        scores = lax.dot_general(stacked, keys[...], (((1,), (1,)), ((), ())), preferred_element_type=jnp.float32)
        allowed = key_pos[...] <= query_pos[pl.ds(first, sub), :]
        scores = jnp.where(allowed[None], scores.reshape(per_device, sub, length), -1e30)
        largest = jnp.max(scores, axis=2, keepdims=True)
        unnormed = jnp.exp2((scores - largest) * factor)
        totals = jnp.sum(unnormed, axis=2, keepdims=True)
        weights = unnormed.astype(jnp.bfloat16).reshape(per_device * sub, length)
        mixed = jnp.dot(weights, values[...], preferred_element_type=jnp.float32)
        mixed = mixed.reshape(per_device, sub, HEAD_WIDTH) / totals
        for i in range(per_device):
            out[:, i * HEAD_WIDTH : (i + 1) * HEAD_WIDTH] = mixed[i].astype(out.dtype)


def attend(offsets, receivers, head_index, queries, query_pos, key_pos, blocks, stacked=()):
    tokens, width = queries.shape
    length = key_pos.shape[1]
    count = 0 if stacked else len(blocks)
    given = stacked or blocks
    piece = jax.ShapeDtypeStruct((tokens // receivers, width), jnp.bfloat16)
    held = [] if stacked else [jax.ShapeDtypeStruct((length, HEAD_WIDTH), jnp.bfloat16)] * 2
    rows = tokens * len(offsets) // receivers
    work = rows * length * width
    return pl.pallas_call(
        functools.partial(attend_kernel, count, offsets),
        out_shape=[piece] * len(offsets) + held,
        in_specs=[SMEM] + [VMEM] * (3 + len(given)),
        out_specs=[VMEM] * (len(offsets) + len(held)),
        compiler_params=params(),
        cost_estimate=pl.CostEstimate(
            flops=16 * work, bytes_accessed=4 * length * HEAD_WIDTH, transcendentals=work // HEAD_WIDTH
        ),
        name="attend",
    )(head_index, queries, query_pos, key_pos, *given)


def join_kernel(count, head_index, *refs):
    pieces, (_, out, sems) = refs[:count], refs[count:]
    width = pieces[0].shape[1]
    copies(
        [
            (piece, out.at[0, 0, :, pl.ds(pl.multiple_of((head_index[0] ^ k) * width, width), width)])
            for k, piece in enumerate(pieces)
        ],
        sems,
    )


def join(head_index, pieces, corner):
    rows, width = pieces[0].shape
    return pl.pallas_call(
        functools.partial(join_kernel, len(pieces)),
        out_shape=jax.ShapeDtypeStruct((1, 1, rows, width * len(pieces)), jnp.bfloat16),
        in_specs=[SMEM] + [VMEM] * len(pieces) + [HBM],
        out_specs=HBM,
        scratch_shapes=[pltpu.SemaphoreType.DMA((len(pieces),))],
        compiler_params=params(),
        name="join",
    )(head_index, *pieces, corner)


def body(activations, key_matrix, value_matrix, queries, block_order):
    heads, inner, outer = (lax.axis_size(name) for name in ("head", "inner", "outer"))
    head, z, x = (lax.axis_index(name) for name in ("head", "inner", "outer"))
    tokens = activations.shape[0]
    sub = tokens // heads
    depth = key_matrix.shape[0]
    sharing = heads // KEY_VALUE_HEADS
    head_index = jnp.reshape(head, (1,))

    ring = [0]
    while len(ring) < inner:
        ring = [2 * k for k in ring] + [2 * k + 1 for k in ring]
    pieces = [lax.dynamic_slice(activations, (head * sub, (z ^ k) * depth), (sub, depth)) for k in ring]
    heads_of = (head ^ jnp.arange(heads, dtype=jnp.int32)) // sharing
    pieces[0], matrices = lax.optimization_barrier((pieces[0], (key_matrix, value_matrix)))
    matrices = load(heads_of, *matrices)
    arrived = [pieces[0]] + [swap(piece, "inner", k) for piece, k in list(zip(pieces, ring))[1:]]

    bounds = sorted({0, inner // 2, inner * 3 // 4, inner})
    partial = []
    for first, last in zip(bounds, bounds[1:-1]):
        _, rows = lax.optimization_barrier((partial, arrived[first:last]))
        partial = partial + project(rows, *matrices, first == 0)
    _, rows = lax.optimization_barrier((partial, arrived[bounds[-2] :]))
    pairs = range(heads // 2)
    late, done = [None] * len(pairs), ()
    for f in reversed(pairs):
        _, given = lax.optimization_barrier((done, rows))
        done = project(given, *matrices, False, f)
        late[f] = [swap_both(part, "head", 2 * f, "inner", k) for part, k in zip(done, ring[bounds[-2] :])]
    early = [partial[0]] + [swap(part, "inner", k) for part, k in list(zip(partial, ring))[1:]]
    sums = swap_all(gather(early[0], early[1:]), "head", 2)
    mine, others = total(sums, late)
    own = jnp.concatenate([mine, swap(others, "head", 1)], axis=0)

    got = dict(enumerate(swap_all([own] * inner, "inner")))
    blocks, cycle = [], []
    for j in range(outer):
        if j > 0:
            beside = swap(own, "outer", j)
        for k in range(inner):
            if j == 0:
                block = got[k]
            elif k == 0:
                block = beside
            elif k < inner - 1:
                block = swap(beside, "inner", k)
            else:
                block = swap(got[k], "outer", j)
            blocks.append(block)
            cycle.append((z ^ k) * outer + (x ^ j))

    block_size = tokens // 2
    row = jnp.arange(tokens, dtype=jnp.int32)
    order = block_order.reshape(-1, 2)

    def positions(shard):
        return (lax.dynamic_index_in_dim(order, shard, 0, False)[:, None] * block_size + row[None, :block_size]).reshape(
            tokens
        )

    query_pos = positions(z * outer + x)
    shards = jnp.stack(cycle)
    distance = jnp.arange(heads, dtype=jnp.int32).reshape(heads // 2, 2).T.reshape(heads)
    rows_of = ((head ^ distance)[:, None] * sub + row[None, :sub]).reshape(tokens)
    one_hot = shards[:, None] == jnp.arange(order.shape[0], dtype=jnp.int32)[None, :]
    firsts = jnp.sum(jnp.where(one_hot[:, :, None], order[None], 0), axis=1)
    block_of = jnp.where(rows_of[None, :] < block_size, firsts[:, :1], firsts[:, 1:])
    key_pos = (block_of * block_size + rows_of[None, :] % block_size).reshape(1, -1)

    place = head_index, queries, query_pos[:, None], key_pos, blocks
    half = max(heads // 2, 1)
    *far_rows, keys, values = attend(range(half, heads), heads, *place)
    near_rows = attend(range(half), heads, *place, stacked=(keys, values))
    far = [swap(rows, "head", k) for k, rows in zip(range(half, heads), far_rows)]
    near = swap_all(near_rows, "head")
    corner = sum(rows[:8, :HEAD_WIDTH] for rows in far)
    return join(head_index, near + far, corner)


def solution(mesh):
    placed = (
        P(("inner", "outer"), None),
        P("inner", None),
        P("inner", None),
        P(("inner", "outer"), "head"),
        P(),
    )
    return jax.shard_map(
        body,
        mesh=mesh,
        in_specs=placed,
        out_specs=P(("inner", "outer"), "head", None, None),
        check_vma=False,
    )
```

```python
import functools
import math

import jax
import jax.numpy as jnp
from jax import lax
from jax.experimental import pallas as pl
from jax.experimental.pallas import tpu as pltpu
from jax.sharding import PartitionSpec as P

QUERY_HEADS = 32
KEY_VALUE_HEADS = 4
HEAD_WIDTH = 128
VMEM = pl.BlockSpec(memory_space=pltpu.VMEM)
SMEM = pl.BlockSpec(memory_space=pltpu.SMEM)
HBM = pl.BlockSpec(memory_space=pltpu.HBM)
LIMIT = 4 * 1024 * 1024
LOAD_LIMIT = 48 * 1024 * 1024


def params(limit=LIMIT):
    return pltpu.CompilerParams(vmem_limit_bytes=limit)


def swap(piece, axis, offset):
    return lax.ppermute(piece, axis, [(i, i ^ offset) for i in range(lax.axis_size(axis))])


def swap_both(piece, axis, offset, other_axis, other):
    sizes = lax.axis_size(axis), lax.axis_size(other_axis)
    order = [(i * sizes[1] + j, (i ^ offset) * sizes[1] + (j ^ other)) for i in range(sizes[0]) for j in range(sizes[1])]
    return lax.ppermute(piece, (axis, other_axis), order)


def swap_all(pieces, axis, unit=1):
    got = {k: swap(pieces[k], axis, k * unit) for k in reversed(range(1, len(pieces)))}
    return [pieces[0]] + [got[k] for k in range(1, len(pieces))]


def copies(pairs, sems):
    started = [pltpu.make_async_copy(source, target, sems.at[i]) for i, (source, target) in enumerate(pairs)]
    for copy in started:
        copy.start()
    for copy in started:
        copy.wait()


def load_kernel(receivers, key_matrix, value_matrix, *refs):
    sharing = lax.axis_size("head") // KEY_VALUE_HEADS
    outs, sems = refs[:2], refs[2]
    pairs = []
    for j in range(receivers):
        head = (lax.axis_index("head") ^ j) // sharing
        columns = pl.ds(pl.multiple_of(head * HEAD_WIDTH, HEAD_WIDTH), HEAD_WIDTH)
        for source, out in zip((key_matrix, value_matrix), outs):
            pairs.append((source.at[:, columns], out.at[:, pl.ds(j * HEAD_WIDTH, HEAD_WIDTH)]))
    copies(pairs, sems)


def load(receivers, *matrices):
    depth = matrices[0].shape[0]
    loaded = jax.ShapeDtypeStruct((depth, receivers * HEAD_WIDTH), jnp.bfloat16)
    return pl.pallas_call(
        functools.partial(load_kernel, receivers),
        out_shape=[loaded] * 2,
        in_specs=[HBM, HBM],
        out_specs=[VMEM] * 2,
        scratch_shapes=[pltpu.SemaphoreType.DMA((2 * receivers,))],
        compiler_params=params(LOAD_LIMIT),
        cost_estimate=pl.CostEstimate(flops=0, bytes_accessed=8 * loaded.size, transcendentals=0),
        name="load",
    )(*matrices)


def encode(out, key, value):
    width = key.shape[1]
    high = key.astype(out.dtype)
    out[:, :width], out[:, width : 2 * width] = high, (key - high.astype(jnp.float32)).astype(out.dtype)
    out[:, 2 * width :] = value.astype(out.dtype)


def decode(part):
    width = part.shape[1] // 3
    high, low, value = (part[:, i * width : (i + 1) * width].astype(jnp.float32) for i in range(3))
    return high + low, value


def project_kernel(count, keeps, pair, *refs):
    pieces, (key_matrix, value_matrix), outs = refs[:count], refs[count : count + 2], refs[count + 2 :]
    rows = pieces[0][...] if count == 1 else jnp.concatenate([piece[...] for piece in pieces], axis=0)
    columns = slice(0, key_matrix.shape[1]) if pair is None else slice(2 * pair * HEAD_WIDTH, 2 * (pair + 1) * HEAD_WIDTH)
    sub = outs[0].shape[0]
    keys = jnp.dot(rows, key_matrix[:, columns], preferred_element_type=jnp.float32)
    values = jnp.dot(rows, value_matrix[:, columns], preferred_element_type=jnp.float32)
    width = keys.shape[1]
    for k, out in enumerate(outs):
        at = slice(k * sub, (k + 1) * sub)
        if keeps and k == 0:
            out[:, :width], out[:, width:] = keys[at], values[at]
        else:
            encode(out, keys[at], values[at])


def project(pieces, key_matrix, value_matrix, keeps, pair=None):
    sub, width = pieces[0].shape[0], key_matrix.shape[1] if pair is None else 2 * HEAD_WIDTH
    given = pieces if sub % 16 == 0 else [jnp.concatenate(pieces, axis=0)]
    kept = jax.ShapeDtypeStruct((sub, 2 * width), jnp.float32)
    sent = jax.ShapeDtypeStruct((sub, 3 * width), jnp.bfloat16)
    return list(
        pl.pallas_call(
            functools.partial(project_kernel, len(given), keeps, pair),
            out_shape=[kept if keeps and k == 0 else sent for k in range(len(pieces))],
            in_specs=[VMEM] * (len(given) + 2),
            out_specs=[VMEM] * len(pieces),
            compiler_params=params(),
            cost_estimate=pl.CostEstimate(
                flops=4 * len(pieces) * sub * width * key_matrix.shape[0],
                bytes_accessed=4 * width * key_matrix.shape[0],
                transcendentals=0,
            ),
            name="project",
        )(*given, key_matrix, value_matrix)
    )


def gather_kernel(count, own, *refs):
    parts, outs = refs[:count], refs[count:]
    width = own.shape[1] // 2
    key, value = own[:, :width], own[:, width:]
    for part in parts:
        more = decode(part)
        key, value = key + more[0], value + more[1]
    each = outs[0].shape[1] // 2
    for f, out in enumerate(outs):
        at = slice(f * each, (f + 1) * each)
        if f == 0:
            out[:, :each], out[:, each:] = key[:, at], value[:, at]
        else:
            encode(out, key[:, at], value[:, at])


def gather(own, parts):
    rows, width = own.shape
    pairs = width // (4 * HEAD_WIDTH)
    return pl.pallas_call(
        functools.partial(gather_kernel, len(parts)),
        out_shape=[jax.ShapeDtypeStruct((rows, 4 * HEAD_WIDTH), jnp.float32)]
        + [jax.ShapeDtypeStruct((rows, 6 * HEAD_WIDTH), jnp.bfloat16)] * (pairs - 1),
        in_specs=[VMEM] * (1 + len(parts)),
        out_specs=[VMEM] * pairs,
        compiler_params=params(),
        name="gather",
    )(own, *parts)


def total_kernel(pairs, *refs):
    sums, parts, outs = refs[:pairs], refs[pairs:-2], refs[-2:]
    count = len(parts) // pairs
    shares = []
    for f, share in enumerate(sums):
        width = share.shape[1] // 2
        key, value = (share[:, :width], share[:, width:]) if f == 0 else decode(share)
        for part in parts[f * count : (f + 1) * count]:
            more = decode(part)
            key, value = key + more[0], value + more[1]
        shares.append((key, value))
    for i, out in enumerate(outs):
        for half in range(2):
            columns = [share[half][:, i * HEAD_WIDTH : (i + 1) * HEAD_WIDTH] for share in shares]
            whole = jnp.concatenate(columns, axis=0)
            out[:, half * HEAD_WIDTH : (half + 1) * HEAD_WIDTH] = whole.astype(out.dtype)


def total(sums, parts):
    given = [*sums, *(part for row in parts for part in row)]
    share = jax.ShapeDtypeStruct((sums[0].shape[0] * len(sums), 2 * HEAD_WIDTH), jnp.bfloat16)
    return pl.pallas_call(
        functools.partial(total_kernel, len(sums)),
        out_shape=[share] * 2,
        in_specs=[VMEM] * len(given),
        out_specs=[VMEM] * 2,
        compiler_params=params(),
        name="total",
    )(*given)


def stack_kernel(count, *refs):
    blocks, (keys, values) = refs[:count], refs[count:]
    tokens = blocks[0].shape[0]
    for b, block in enumerate(blocks):
        keys[b * tokens : (b + 1) * tokens, :] = block[:, :HEAD_WIDTH]
        values[b * tokens : (b + 1) * tokens, :] = block[:, HEAD_WIDTH:]


def attend_kernel(count, offsets, head_index, queries, query_pos, key_pos, *refs):
    if count:
        outs, (keys, values) = refs[count:-2], refs[-2:]
        stack_kernel(count, *refs[:count], keys, values)
    else:
        (keys, values), outs = refs[:2], refs[2:]
    sub = outs[0].shape[0]
    per_device = queries.shape[1] // HEAD_WIDTH
    length = keys.shape[0]
    factor = math.log2(math.e) / math.sqrt(HEAD_WIDTH)
    for k, out in zip(offsets, outs):
        first = pl.multiple_of((head_index[0] ^ k) * sub, sub)
        rows = queries[pl.ds(first, sub), :]
        stacked = jnp.concatenate([rows[:, i * HEAD_WIDTH : (i + 1) * HEAD_WIDTH] for i in range(per_device)], axis=0)
        scores = lax.dot_general(stacked, keys[...], (((1,), (1,)), ((), ())), preferred_element_type=jnp.float32)
        allowed = key_pos[...] <= query_pos[pl.ds(first, sub), :]
        scores = jnp.where(allowed[None], scores.reshape(per_device, sub, length), -1e30)
        largest = jnp.max(scores, axis=2, keepdims=True)
        unnormed = jnp.exp2((scores - largest) * factor)
        totals = jnp.sum(unnormed, axis=2, keepdims=True)
        weights = unnormed.astype(jnp.bfloat16).reshape(per_device * sub, length)
        mixed = jnp.dot(weights, values[...], preferred_element_type=jnp.float32)
        mixed = mixed.reshape(per_device, sub, HEAD_WIDTH) / totals
        for i in range(per_device):
            out[:, i * HEAD_WIDTH : (i + 1) * HEAD_WIDTH] = mixed[i].astype(out.dtype)


def attend(offsets, receivers, head_index, queries, query_pos, key_pos, blocks, stacked=()):
    tokens, width = queries.shape
    length = key_pos.shape[1]
    count = 0 if stacked else len(blocks)
    given = stacked or blocks
    piece = jax.ShapeDtypeStruct((tokens // receivers, width), jnp.bfloat16)
    held = [] if stacked else [jax.ShapeDtypeStruct((length, HEAD_WIDTH), jnp.bfloat16)] * 2
    rows = tokens * len(offsets) // receivers
    work = rows * length * width
    return pl.pallas_call(
        functools.partial(attend_kernel, count, offsets),
        out_shape=[piece] * len(offsets) + held,
        in_specs=[SMEM] + [VMEM] * (3 + len(given)),
        out_specs=[VMEM] * (len(offsets) + len(held)),
        compiler_params=params(),
        cost_estimate=pl.CostEstimate(
            flops=16 * work, bytes_accessed=4 * length * HEAD_WIDTH, transcendentals=work // HEAD_WIDTH
        ),
        name="attend",
    )(head_index, queries, query_pos, key_pos, *given)


def join_kernel(count, head_index, *refs):
    pieces, (_, out, sems) = refs[:count], refs[count:]
    width = pieces[0].shape[1]
    copies(
        [
            (piece, out.at[0, 0, :, pl.ds(pl.multiple_of((head_index[0] ^ k) * width, width), width)])
            for k, piece in enumerate(pieces)
        ],
        sems,
    )


def join(head_index, pieces, corner):
    rows, width = pieces[0].shape
    return pl.pallas_call(
        functools.partial(join_kernel, len(pieces)),
        out_shape=jax.ShapeDtypeStruct((1, 1, rows, width * len(pieces)), jnp.bfloat16),
        in_specs=[SMEM] + [VMEM] * len(pieces) + [HBM],
        out_specs=HBM,
        scratch_shapes=[pltpu.SemaphoreType.DMA((len(pieces),))],
        compiler_params=params(),
        name="join",
    )(head_index, *pieces, corner)


def body(activations, key_matrix, value_matrix, queries, block_order):
    heads, inner, outer = (lax.axis_size(name) for name in ("head", "inner", "outer"))
    head, z, x = (lax.axis_index(name) for name in ("head", "inner", "outer"))
    tokens = activations.shape[0]
    sub = tokens // heads
    depth = key_matrix.shape[0]
    head_index = jnp.reshape(head, (1,))

    ring = [0]
    while len(ring) < inner:
        ring = [2 * k for k in ring] + [2 * k + 1 for k in ring]
    pieces = [lax.dynamic_slice(activations, (head * sub, (z ^ k) * depth), (sub, depth)) for k in ring]
    pieces[0], matrices = lax.optimization_barrier((pieces[0], (key_matrix, value_matrix)))
    matrices = load(heads, *matrices)
    arrived = [pieces[0]] + [swap(piece, "inner", k) for piece, k in list(zip(pieces, ring))[1:]]

    bounds = sorted({0, inner // 2, inner * 3 // 4, inner})
    partial = []
    for first, last in zip(bounds, bounds[1:-1]):
        _, rows = lax.optimization_barrier((partial, arrived[first:last]))
        partial = partial + project(rows, *matrices, first == 0)
    _, rows = lax.optimization_barrier((partial, arrived[bounds[-2] :]))
    pairs = range(heads // 2)
    late, done = [None] * len(pairs), ()
    for f in reversed(pairs):
        _, given = lax.optimization_barrier((done, rows))
        done = project(given, *matrices, False, f)
        late[f] = [swap_both(part, "head", 2 * f, "inner", k) for part, k in zip(done, ring[bounds[-2] :])]
    early = [partial[0]] + [swap(part, "inner", k) for part, k in list(zip(partial, ring))[1:]]
    sums = swap_all(gather(early[0], early[1:]), "head", 2)
    mine, others = total(sums, late)
    own = jnp.concatenate([mine, swap(others, "head", 1)], axis=0)

    beside_all = {j: swap(own, "outer", j) for j in range(1, outer)}
    got = dict(enumerate(swap_all([own] * inner, "inner")))
    blocks, cycle = [], []
    for j in range(outer):
        if j > 0:
            beside = beside_all[j]
        for k in range(inner):
            if j == 0:
                block = got[k]
            elif k == 0:
                block = beside
            elif k < inner - 1:
                block = swap(beside, "inner", k)
            else:
                block = swap(got[k], "outer", j)
            blocks.append(block)
            cycle.append((z ^ k) * outer + (x ^ j))

    block_size = tokens // 2
    row = jnp.arange(tokens, dtype=jnp.int32)
    order = block_order.reshape(-1, 2)

    def positions(shard):
        return (lax.dynamic_index_in_dim(order, shard, 0, False)[:, None] * block_size + row[None, :block_size]).reshape(
            tokens
        )

    query_pos = positions(z * outer + x)
    shards = jnp.stack(cycle)
    distance = jnp.arange(heads, dtype=jnp.int32).reshape(heads // 2, 2).T.reshape(heads)
    rows_of = ((head ^ distance)[:, None] * sub + row[None, :sub]).reshape(tokens)
    one_hot = shards[:, None] == jnp.arange(order.shape[0], dtype=jnp.int32)[None, :]
    firsts = jnp.sum(jnp.where(one_hot[:, :, None], order[None], 0), axis=1)
    block_of = jnp.where(rows_of[None, :] < block_size, firsts[:, :1], firsts[:, 1:])
    key_pos = (block_of * block_size + rows_of[None, :] % block_size).reshape(1, -1)

    place = head_index, queries, query_pos[:, None], key_pos, blocks
    half = max(heads // 2, 1)
    *far_rows, keys, values = attend(range(half, heads), heads, *place)
    near_rows = attend(range(half), heads, *place, stacked=(keys, values))
    far = [swap(rows, "head", k) for k, rows in zip(range(half, heads), far_rows)]
    near = swap_all(near_rows, "head")
    corner = sum(rows[:8, :HEAD_WIDTH] for rows in far)
    return join(head_index, near + far, corner)


def solution(mesh):
    placed = (
        P(("inner", "outer"), None),
        P("inner", None),
        P("inner", None),
        P(("inner", "outer"), "head"),
        P(),
    )
    return jax.shard_map(
        body,
        mesh=mesh,
        in_specs=placed,
        out_specs=P(("inner", "outer"), "head", None, None),
        check_vma=False,
    )
```

```python
import functools
import math

import jax
import jax.numpy as jnp
from jax import lax
from jax.experimental import pallas as pl
from jax.experimental.pallas import tpu as pltpu
from jax.sharding import PartitionSpec as P

QUERY_HEADS = 32
KEY_VALUE_HEADS = 4
HEAD_WIDTH = 128
VMEM = pl.BlockSpec(memory_space=pltpu.VMEM)
SMEM = pl.BlockSpec(memory_space=pltpu.SMEM)
HBM = pl.BlockSpec(memory_space=pltpu.HBM)
LIMIT = 4 * 1024 * 1024
LOAD_LIMIT = 48 * 1024 * 1024


def params(limit=LIMIT):
    return pltpu.CompilerParams(vmem_limit_bytes=limit)


def swap(piece, axis, offset):
    return lax.ppermute(piece, axis, [(i, i ^ offset) for i in range(lax.axis_size(axis))])


def swap_both(piece, axis, offset, other_axis, other):
    sizes = lax.axis_size(axis), lax.axis_size(other_axis)
    order = [(i * sizes[1] + j, (i ^ offset) * sizes[1] + (j ^ other)) for i in range(sizes[0]) for j in range(sizes[1])]
    return lax.ppermute(piece, (axis, other_axis), order)


def swap_all(pieces, axis, unit=1):
    got = {k: swap(pieces[k], axis, k * unit) for k in reversed(range(1, len(pieces)))}
    return [pieces[0]] + [got[k] for k in range(1, len(pieces))]


def copies(pairs, sems):
    started = [pltpu.make_async_copy(source, target, sems.at[i]) for i, (source, target) in enumerate(pairs)]
    for copy in started:
        copy.start()
    for copy in started:
        copy.wait()


def load_kernel(receivers, key_matrix, value_matrix, *refs):
    sharing = lax.axis_size("head") // KEY_VALUE_HEADS
    outs, sems = refs[:2], refs[2]
    pairs = []
    for j in range(receivers):
        head = (lax.axis_index("head") ^ j) // sharing
        columns = pl.ds(pl.multiple_of(head * HEAD_WIDTH, HEAD_WIDTH), HEAD_WIDTH)
        for source, out in zip((key_matrix, value_matrix), outs):
            pairs.append((source.at[:, columns], out.at[:, pl.ds(j * HEAD_WIDTH, HEAD_WIDTH)]))
    copies(pairs, sems)


def load(receivers, *matrices):
    depth = matrices[0].shape[0]
    loaded = jax.ShapeDtypeStruct((depth, receivers * HEAD_WIDTH), jnp.bfloat16)
    return pl.pallas_call(
        functools.partial(load_kernel, receivers),
        out_shape=[loaded] * 2,
        in_specs=[HBM, HBM],
        out_specs=[VMEM] * 2,
        scratch_shapes=[pltpu.SemaphoreType.DMA((2 * receivers,))],
        compiler_params=params(LOAD_LIMIT),
        cost_estimate=pl.CostEstimate(flops=0, bytes_accessed=8 * loaded.size, transcendentals=0),
        name="load",
    )(*matrices)


def encode(out, key, value):
    width = key.shape[1]
    high = key.astype(out.dtype)
    out[:, :width], out[:, width : 2 * width] = high, (key - high.astype(jnp.float32)).astype(out.dtype)
    out[:, 2 * width :] = value.astype(out.dtype)


def decode(part):
    width = part.shape[1] // 3
    high, low, value = (part[:, i * width : (i + 1) * width].astype(jnp.float32) for i in range(3))
    return high + low, value


def project_kernel(count, keeps, pair, *refs):
    pieces, (key_matrix, value_matrix), outs = refs[:count], refs[count : count + 2], refs[count + 2 :]
    rows = pieces[0][...] if count == 1 else jnp.concatenate([piece[...] for piece in pieces], axis=0)
    columns = slice(0, key_matrix.shape[1]) if pair is None else slice(2 * pair * HEAD_WIDTH, 2 * (pair + 1) * HEAD_WIDTH)
    sub = outs[0].shape[0]
    keys = jnp.dot(rows, key_matrix[:, columns], preferred_element_type=jnp.float32)
    values = jnp.dot(rows, value_matrix[:, columns], preferred_element_type=jnp.float32)
    width = keys.shape[1]
    for k, out in enumerate(outs):
        at = slice(k * sub, (k + 1) * sub)
        if keeps and k == 0:
            out[:, :width], out[:, width:] = keys[at], values[at]
        else:
            encode(out, keys[at], values[at])


def project(pieces, key_matrix, value_matrix, keeps, pair=None):
    sub, width = pieces[0].shape[0], key_matrix.shape[1] if pair is None else 2 * HEAD_WIDTH
    given = pieces if sub % 16 == 0 else [jnp.concatenate(pieces, axis=0)]
    kept = jax.ShapeDtypeStruct((sub, 2 * width), jnp.float32)
    sent = jax.ShapeDtypeStruct((sub, 3 * width), jnp.bfloat16)
    return list(
        pl.pallas_call(
            functools.partial(project_kernel, len(given), keeps, pair),
            out_shape=[kept if keeps and k == 0 else sent for k in range(len(pieces))],
            in_specs=[VMEM] * (len(given) + 2),
            out_specs=[VMEM] * len(pieces),
            compiler_params=params(),
            cost_estimate=pl.CostEstimate(
                flops=4 * len(pieces) * sub * width * key_matrix.shape[0],
                bytes_accessed=4 * width * key_matrix.shape[0],
                transcendentals=0,
            ),
            name="project",
        )(*given, key_matrix, value_matrix)
    )


def gather_kernel(count, own, *refs):
    parts, outs = refs[:count], refs[count:]
    width = own.shape[1] // 2
    key, value = own[:, :width], own[:, width:]
    for part in parts:
        more = decode(part)
        key, value = key + more[0], value + more[1]
    each = outs[0].shape[1] // 2
    for f, out in enumerate(outs):
        at = slice(f * each, (f + 1) * each)
        if f == 0:
            out[:, :each], out[:, each:] = key[:, at], value[:, at]
        else:
            encode(out, key[:, at], value[:, at])


def gather(own, parts):
    rows, width = own.shape
    pairs = width // (4 * HEAD_WIDTH)
    return pl.pallas_call(
        functools.partial(gather_kernel, len(parts)),
        out_shape=[jax.ShapeDtypeStruct((rows, 4 * HEAD_WIDTH), jnp.float32)]
        + [jax.ShapeDtypeStruct((rows, 6 * HEAD_WIDTH), jnp.bfloat16)] * (pairs - 1),
        in_specs=[VMEM] * (1 + len(parts)),
        out_specs=[VMEM] * pairs,
        compiler_params=params(),
        name="gather",
    )(own, *parts)


def total_kernel(pairs, *refs):
    sums, parts, outs = refs[:pairs], refs[pairs:-2], refs[-2:]
    count = len(parts) // pairs
    shares = []
    for f, share in enumerate(sums):
        width = share.shape[1] // 2
        key, value = (share[:, :width], share[:, width:]) if f == 0 else decode(share)
        for part in parts[f * count : (f + 1) * count]:
            more = decode(part)
            key, value = key + more[0], value + more[1]
        shares.append((key, value))
    for i, out in enumerate(outs):
        for half in range(2):
            columns = [share[half][:, i * HEAD_WIDTH : (i + 1) * HEAD_WIDTH] for share in shares]
            whole = jnp.concatenate(columns, axis=0)
            out[:, half * HEAD_WIDTH : (half + 1) * HEAD_WIDTH] = whole.astype(out.dtype)


def total(sums, parts):
    given = [*sums, *(part for row in parts for part in row)]
    share = jax.ShapeDtypeStruct((sums[0].shape[0] * len(sums), 2 * HEAD_WIDTH), jnp.bfloat16)
    return pl.pallas_call(
        functools.partial(total_kernel, len(sums)),
        out_shape=[share] * 2,
        in_specs=[VMEM] * len(given),
        out_specs=[VMEM] * 2,
        compiler_params=params(),
        name="total",
    )(*given)


def stack_kernel(count, *refs):
    blocks, (keys, values) = refs[:count], refs[count:]
    tokens = blocks[0].shape[0]
    for b, block in enumerate(blocks):
        keys[b * tokens : (b + 1) * tokens, :] = block[:, :HEAD_WIDTH]
        values[b * tokens : (b + 1) * tokens, :] = block[:, HEAD_WIDTH:]


def attend_kernel(count, offsets, head_index, queries, query_pos, key_pos, *refs):
    if count:
        outs, (keys, values) = refs[count:-2], refs[-2:]
        stack_kernel(count, *refs[:count], keys, values)
    else:
        (keys, values), outs = refs[:2], refs[2:]
    sub = outs[0].shape[0]
    per_device = queries.shape[1] // HEAD_WIDTH
    length = keys.shape[0]
    factor = math.log2(math.e) / math.sqrt(HEAD_WIDTH)
    for k, out in zip(offsets, outs):
        first = pl.multiple_of((head_index[0] ^ k) * sub, sub)
        rows = queries[pl.ds(first, sub), :]
        stacked = jnp.concatenate([rows[:, i * HEAD_WIDTH : (i + 1) * HEAD_WIDTH] for i in range(per_device)], axis=0)
        scores = lax.dot_general(stacked, keys[...], (((1,), (1,)), ((), ())), preferred_element_type=jnp.float32)
        allowed = key_pos[...] <= query_pos[pl.ds(first, sub), :]
        scores = jnp.where(allowed[None], scores.reshape(per_device, sub, length), -1e30)
        largest = jnp.max(scores, axis=2, keepdims=True)
        unnormed = jnp.exp2((scores - largest) * factor)
        totals = jnp.sum(unnormed, axis=2, keepdims=True)
        weights = unnormed.astype(jnp.bfloat16).reshape(per_device * sub, length)
        mixed = jnp.dot(weights, values[...], preferred_element_type=jnp.float32)
        mixed = mixed.reshape(per_device, sub, HEAD_WIDTH) / totals
        for i in range(per_device):
            out[:, i * HEAD_WIDTH : (i + 1) * HEAD_WIDTH] = mixed[i].astype(out.dtype)


def attend(offsets, receivers, head_index, queries, query_pos, key_pos, blocks, stacked=()):
    tokens, width = queries.shape
    length = key_pos.shape[1]
    count = 0 if stacked else len(blocks)
    given = stacked or blocks
    piece = jax.ShapeDtypeStruct((tokens // receivers, width), jnp.bfloat16)
    held = [] if stacked else [jax.ShapeDtypeStruct((length, HEAD_WIDTH), jnp.bfloat16)] * 2
    rows = tokens * len(offsets) // receivers
    work = rows * length * width
    return pl.pallas_call(
        functools.partial(attend_kernel, count, offsets),
        out_shape=[piece] * len(offsets) + held,
        in_specs=[SMEM] + [VMEM] * (3 + len(given)),
        out_specs=[VMEM] * (len(offsets) + len(held)),
        compiler_params=params(),
        cost_estimate=pl.CostEstimate(
            flops=16 * work, bytes_accessed=4 * length * HEAD_WIDTH, transcendentals=work // HEAD_WIDTH
        ),
        name="attend",
    )(head_index, queries, query_pos, key_pos, *given)


def join_kernel(count, head_index, *refs):
    pieces, (_, out, sems) = refs[:count], refs[count:]
    width = pieces[0].shape[1]
    copies(
        [
            (piece, out.at[0, 0, :, pl.ds(pl.multiple_of((head_index[0] ^ k) * width, width), width)])
            for k, piece in enumerate(pieces)
        ],
        sems,
    )


def join(head_index, pieces, corner):
    rows, width = pieces[0].shape
    return pl.pallas_call(
        functools.partial(join_kernel, len(pieces)),
        out_shape=jax.ShapeDtypeStruct((1, 1, rows, width * len(pieces)), jnp.bfloat16),
        in_specs=[SMEM] + [VMEM] * len(pieces) + [HBM],
        out_specs=HBM,
        scratch_shapes=[pltpu.SemaphoreType.DMA((len(pieces),))],
        compiler_params=params(),
        name="join",
    )(head_index, *pieces, corner)


def body(activations, key_matrix, value_matrix, queries, block_order):
    heads, inner, outer = (lax.axis_size(name) for name in ("head", "inner", "outer"))
    head, z, x = (lax.axis_index(name) for name in ("head", "inner", "outer"))
    tokens = activations.shape[0]
    sub = tokens // heads
    depth = key_matrix.shape[0]
    head_index = jnp.reshape(head, (1,))

    ring = [0]
    while len(ring) < inner:
        ring = [2 * k for k in ring] + [2 * k + 1 for k in ring]
    pieces = [lax.dynamic_slice(activations, (head * sub, (z ^ k) * depth), (sub, depth)) for k in ring]
    pieces[0], matrices = lax.optimization_barrier((pieces[0], (key_matrix, value_matrix)))
    matrices = load(heads, *matrices)
    arrived = [pieces[0]] + [swap(piece, "inner", k) for piece, k in list(zip(pieces, ring))[1:]]

    bounds = sorted({0, inner // 2, inner * 3 // 4, inner})
    partial = []
    for first, last in zip(bounds, bounds[1:-1]):
        _, rows = lax.optimization_barrier((partial, arrived[first:last]))
        partial = partial + project(rows, *matrices, first == 0)
    _, rows = lax.optimization_barrier((partial, arrived[bounds[-2] :]))
    pairs = range(heads // 2)
    late, done = [None] * len(pairs), ()
    for f in reversed(pairs):
        _, given = lax.optimization_barrier((done, rows))
        done = project(given, *matrices, False, f)
        late[f] = [swap_both(part, "head", 2 * f, "inner", k) for part, k in zip(done, ring[bounds[-2] :])]
    early = [partial[0]] + [swap(part, "inner", k) for part, k in list(zip(partial, ring))[1:]]
    sums = swap_all(gather(early[0], early[1:]), "head", 2)
    mine, others = total(sums, late)
    own = jnp.concatenate([mine, swap(others, "head", 1)], axis=0)

    got = dict(enumerate(swap_all([own] * inner, "inner")))
    blocks, cycle = [], []
    for j in range(outer):
        if j > 0:
            beside = swap(own, "outer", j)
        for k in range(inner):
            if j == 0:
                block = got[k]
            elif k == 0:
                block = beside
            elif k < inner - 1:
                block = swap(beside, "inner", k)
            else:
                block = swap(got[k], "outer", j)
            blocks.append(block)
            cycle.append((z ^ k) * outer + (x ^ j))

    come = sorted(range(len(blocks)), key=lambda i: (i % inner in (1, inner - 1), i))
    blocks, cycle = [blocks[i] for i in come], [cycle[i] for i in come]

    block_size = tokens // 2
    row = jnp.arange(tokens, dtype=jnp.int32)
    order = block_order.reshape(-1, 2)

    def positions(shard):
        return (lax.dynamic_index_in_dim(order, shard, 0, False)[:, None] * block_size + row[None, :block_size]).reshape(
            tokens
        )

    query_pos = positions(z * outer + x)
    shards = jnp.stack(cycle)
    distance = jnp.arange(heads, dtype=jnp.int32).reshape(heads // 2, 2).T.reshape(heads)
    rows_of = ((head ^ distance)[:, None] * sub + row[None, :sub]).reshape(tokens)
    one_hot = shards[:, None] == jnp.arange(order.shape[0], dtype=jnp.int32)[None, :]
    firsts = jnp.sum(jnp.where(one_hot[:, :, None], order[None], 0), axis=1)
    block_of = jnp.where(rows_of[None, :] < block_size, firsts[:, :1], firsts[:, 1:])
    key_pos = (block_of * block_size + rows_of[None, :] % block_size).reshape(1, -1)

    place = head_index, queries, query_pos[:, None], key_pos, blocks
    half = max(heads // 2, 1)
    *far_rows, keys, values = attend(range(half, heads), heads, *place)
    near_rows = attend(range(half), heads, *place, stacked=(keys, values))
    far = [swap(rows, "head", k) for k, rows in zip(range(half, heads), far_rows)]
    near = swap_all(near_rows, "head")
    corner = sum(rows[:8, :HEAD_WIDTH] for rows in far)
    return join(head_index, near + far, corner)


def solution(mesh):
    placed = (
        P(("inner", "outer"), None),
        P("inner", None),
        P("inner", None),
        P(("inner", "outer"), "head"),
        P(),
    )
    return jax.shard_map(
        body,
        mesh=mesh,
        in_specs=placed,
        out_specs=P(("inner", "outer"), "head", None, None),
        check_vma=False,
    )
```
